32 devices in a mesh: dp: 16 (over z, y, core), tensor: 2 (over x).
Axes of the slice: x: 2, y: 2, z: 4, core: 2. Of those that a mesh axis runs over, the one named last changes fastest.
Arguments:
- inputs: bfloat16 [16384, 1024], P(('dp', 'tensor')), may hold values from -6 to 6
- segment_ids: int32 [16384], P('dp'), may hold values from 0 to 1023, as said below
- ln_attn_gain: bfloat16 [1024], P(('dp', 'tensor')), may hold values from 0.25 to 1.75
- ln_attn_bias: bfloat16 [1024], P(('dp', 'tensor')), may hold values from -1.75 to 1.75
- ln_mlp_gain: bfloat16 [1024], P(('dp', 'tensor')), may hold values from 0.25 to 1.75
- ln_mlp_bias: bfloat16 [1024], P(('dp', 'tensor')), may hold values from -1.75 to 1.75
- qkv_weight: bfloat16 [1024, 3, 1024], P('dp', None, 'tensor'), may hold values from -0.1875 to 0.1875
- qkv_bias: bfloat16 [3, 2, 512], P(None, 'tensor', 'dp'), may hold values from -3 to 3
- out_weight: bfloat16 [1024, 1024], P('tensor', 'dp'), may hold values from -2 to 2
- out_bias: bfloat16 [1024], P(('dp', 'tensor')), may hold values from -1.75 to 1.75
- up_weight: bfloat16 [1024, 4096], P('dp', 'tensor'), may hold values from -0.1875 to 0.1875
- up_bias: bfloat16 [2, 2048], P('tensor', 'dp'), may hold values from -3 to 3
- down_weight: bfloat16 [4096, 1024], P('tensor', 'dp'), may hold values from -0.09375 to 0.09375
- down_bias: bfloat16 [1024], P(('dp', 'tensor')), may hold values from -1.75 to 1.75
- cotangent: bfloat16 [16384, 1024], P(('dp', 'tensor')), may hold values from -6 to 6
Outputs:
- output: bfloat16 [16384, 1024], P(('dp', 'tensor'))
- input_grad: float32 [16384, 1024], P(('dp', 'tensor'))
- d_ln_attn_gain: float32 [1024], P(('dp', 'tensor'))
- d_ln_attn_bias: float32 [1024], P(('dp', 'tensor'))
- d_ln_mlp_gain: float32 [1024], P(('dp', 'tensor'))
- d_ln_mlp_bias: float32 [1024], P(('dp', 'tensor'))
- d_qkv_weight: float32 [1024, 3, 1024], P('dp', None, 'tensor')
- d_qkv_bias: float32 [3, 2, 512], P(None, 'tensor', 'dp')
- d_out_weight: float32 [1024, 1024], P('tensor', 'dp')
- d_out_bias: float32 [1024], P(('dp', 'tensor'))
- d_up_weight: float32 [1024, 4096], P('dp', 'tensor')
- d_up_bias: float32 [2, 2048], P('tensor', 'dp')
- d_down_weight: float32 [4096, 1024], P('tensor', 'dp')
- d_down_bias: float32 [1024], P(('dp', 'tensor'))
The draws below stay inside these ranges and needn't reach their ends.
Inputs may be any that keep to these rules, and one draw needn't show every extreme that they name: `segment_ids`: within each packed sequence of 1024 tokens a token's number is the position, within that sequence, of its document's first token, so the numbers never fall and a run of equal numbers is one document; the last token of each sequence is a document of its own.
All inputs are finite; a program needn't handle non-finite values.
Results may differ from the reference program's by a relative error of at most 0.0098.
Values may be sent and summed in bfloat16 or wider, within the bound.
A program may use at most 256 MiB of HBM per device.

```python
import math
import jax
import jax.numpy as jnp
from jax import lax

D = 1024
HEADS = 16
HEAD = 64
FF = 4096
ROT = 16
SEQ = 1024
ROWS = 512
TOKENS = 16384
N_DP = 16
N_TENSOR = 2


def draw_segment_ids(key, part):
    key = jax.random.fold_in(key, 7)
    key_head, key_tail, key_cuts = jax.random.split(key, 3)
    edge = max(ROWS // 2, 2)
    head = jax.random.randint(key_head, (N_DP, 1), 1, edge + 1)
    tail = jax.random.randint(key_tail, (N_DP, 1), 1, edge + 1)
    stop = SEQ - tail
    place = jnp.broadcast_to(jnp.arange(SEQ, dtype=jnp.int32)[None, :], (N_DP, SEQ))
    cuts = jax.random.randint(key_cuts, (N_DP, SEQ), 0, 24) == 0
    inside = (place > head) & (place < stop)
    starts = (place == 0) | (place == head) | (place == stop) | (place == SEQ - 1) | cuts & jnp.logical_not(inside)
    numbers = lax.cummax(jnp.where(starts, place, 0), axis=1)
    return numbers.reshape(N_DP * SEQ).astype(jnp.int32)


def strengthened(values, own_key, source, target, parts, factor):
    def block_of(dim):
        return (jnp.arange(values.shape[dim]) // (values.shape[dim] // parts)).reshape((-1,) + (1,) * (values.ndim - 1 - dim))

    near = jax.random.permutation(own_key, parts)[block_of(target)]
    far = (block_of(target) + parts // 2) % parts
    return jnp.where((block_of(source) == near) | (block_of(source) == far), factor * values, values)


def block_levels(own_key, shape, pieces, least, top_value):
    gain = 1.0
    for dim, shards_of in pieces:
        heights = jax.random.uniform(jax.random.fold_in(jax.random.fold_in(own_key, 6), dim), (shards_of,), jnp.float32, least / len(pieces), top_value / len(pieces))
        gain = gain * jnp.repeat(jnp.exp(heights), shape[dim] // shards_of).reshape((-1,) + (1,) * (len(shape) - 1 - dim))
    return gain


def normal_values(key, shape, spread, limit, cuts=(), held_as=jnp.bfloat16):
    values = jax.random.normal(key, shape, jnp.float32) * spread
    if len(cuts) > 0:
        values = block_levels(key, shape, cuts, -0.22, 0.18) * values
    return jnp.clip(values, min=-limit, max=limit).astype(held_as)


def bell_draw_with(rng, extent, spread, limit, shards, heavy, kind=jnp.bfloat16):
    values = spread * jax.random.normal(rng, extent, jnp.float32)
    if shards:
        values = values * block_levels(rng, extent, shards, -0.22, 0.18)
    return jnp.clip(strengthened(values, jax.random.fold_in(rng, 3), *heavy), -limit, limit).astype(kind)


def setup_inputs(seed: int = 0) -> dict:
    splits = jax.random.split(jax.random.key(seed), 16)
    return {
        "inputs": bell_draw_with(splits[0], (TOKENS, D), 1.0, 6.0, ((0, 32),), (0, 1, 32, 2.75)),
        "segment_ids": draw_segment_ids(jax.random.fold_in(splits[15], 71), 0),
        "ln_attn_gain": jnp.clip(1.0 + 0.15 * jax.random.normal(splits[2], (D,), jnp.float32), 0.25, 1.75).astype(jnp.bfloat16),
        "ln_attn_bias": normal_values(splits[3], (D,), 0.3, 1.75, ((0, 32),)),
        "ln_mlp_gain": jnp.clip(1.0 + 0.15 * jax.random.normal(splits[4], (D,), jnp.float32), 0.25, 1.75).astype(jnp.bfloat16),
        "ln_mlp_bias": normal_values(splits[5], (D,), 0.3, 1.75, ((0, 32),)),
        "qkv_weight": normal_values(splits[6], (D, 3, D), D ** -0.5, 0.1875, ((0, 16), (2, 2))),
        "qkv_bias": normal_values(splits[7], (3, N_TENSOR, D // N_TENSOR), 0.5, 3.0, ((1, 2), (2, 16))),
        "out_weight": normal_values(splits[8], (D, D), (D // 128) ** -0.5, 2.0, ((0, 2), (1, 16))),
        "out_bias": normal_values(splits[9], (D,), 0.3, 1.75, ((0, 32),)),
        "up_weight": normal_values(splits[10], (D, FF), D ** -0.5, 0.1875, ((0, 16), (1, 2))),
        "up_bias": normal_values(splits[11], (N_TENSOR, FF // N_TENSOR), 0.5, 3.0, ((0, 2), (1, 16))),
        "down_weight": normal_values(splits[12], (FF, D), FF ** -0.5, 0.09375, ((0, 2), (1, 16))),
        "down_bias": normal_values(splits[13], (D,), 0.3, 1.75, ((0, 32),)),
        "cotangent": bell_draw_with(splits[14], (TOKENS, D), 1.0, 6.0, ((0, 32),), (0, 1, 32, 2.75)),
    }


EPSILON = 1e-05
NEGATIVE = -1e+30
PRECISE = lax.Precision.HIGHEST

@jax.custom_vjp
def low(v):
    return lax.optimization_barrier(v.astype(jnp.bfloat16)).astype(jnp.float32)

@jax.custom_vjp
def low_back(v):
    return v

def low_keep(v):
    return (low(v), None)

def low_pass(kept, grad):
    return (grad,)

def back_keep(v):
    return (v, None)

def back_low(kept, grad):
    return (low(grad),)
low.defvjp(low_keep, low_pass)
low_back.defvjp(back_keep, back_low)

def rotated(values, cosine, sine, sign):
    half_rot = ROT // 2
    first_half = values[..., :half_rot]
    second_half = values[..., half_rot:ROT]
    new_first = first_half * cosine - sign * second_half * sine
    new_second = second_half * cosine + sign * first_half * sine
    return jnp.concatenate([new_first, new_second, values[..., ROT:]], axis=-1)

def angle_tables(length):
    position = jnp.arange(length).astype(jnp.float32)
    inverse = 10000.0 ** (-(2.0 * jnp.arange(ROT // 2).astype(jnp.float32)) / ROT)
    theta = position[:, None] * inverse[None, :]
    return (jnp.cos(theta)[:, None, :], jnp.sin(theta)[:, None, :])

def gelu_exact(value):
    return jax.nn.gelu(value, approximate=False)

def attention(query, keys, values, segment_row):
    block_rows = min(512, SEQ)
    block_count = SEQ // block_rows
    score_scale = 1.0 / math.sqrt(HEAD)
    places = jnp.arange(SEQ)
    query_blocks = query.reshape(block_count, block_rows, HEADS, HEAD)
    segment_blocks = segment_row.reshape(block_count, block_rows)
    place_blocks = places.reshape(block_count, block_rows)

    def one_block(block_item):
        query_part, segment_part, place_part = block_item
        scores = jnp.einsum('qhe,khe->hqk', query_part, keys, precision=PRECISE) * score_scale
        scores = low_back(scores)
        allowed = (segment_part[:, None] == segment_row[None, :]) & (place_part[:, None] >= places[None, :])
        scores = jnp.where(allowed[None], scores, NEGATIVE)
        row_max = lax.optimization_barrier(jnp.max(scores, axis=-1, keepdims=True))
        exponent = jnp.exp(scores - row_max)
        probability = exponent / lax.optimization_barrier(jnp.sum(exponent, axis=-1, keepdims=True))
        return jnp.einsum('hqk,khe->qhe', low(probability), values, precision=PRECISE)
    context = lax.map(jax.checkpoint(one_block), (query_blocks, segment_blocks, place_blocks))
    return context.reshape(SEQ, HEADS * HEAD)

def forward(params, resid, segment_row):
    gain_attn, shift_attn, gain_mlp, shift_mlp, w_qkv, b_qkv, w_out, b_out, w_up, b_up, w_down, b_down = params
    average = lax.optimization_barrier(jnp.mean(resid, axis=-1, keepdims=True))
    centred = resid - average
    variance = lax.optimization_barrier(jnp.mean(centred * centred, axis=-1, keepdims=True))
    normalized = centred * lax.rsqrt(variance + EPSILON)
    attn_rows = low(normalized * gain_attn + shift_attn)
    mlp_rows = low(normalized * gain_mlp + shift_mlp)
    proj = jnp.einsum('sd,dje->sje', attn_rows, w_qkv, precision=PRECISE) + b_qkv.reshape(3, D)[None]
    proj = low_back(proj)
    cosine, sine = angle_tables(SEQ)
    query = low(rotated(proj[:, 0].reshape(SEQ, HEADS, HEAD), cosine, sine, 1.0))
    keys = low(rotated(proj[:, 1].reshape(SEQ, HEADS, HEAD), cosine, sine, 1.0))
    values = low(proj[:, 2].reshape(SEQ, HEADS, HEAD))
    context = low(low_back(attention(query, keys, values, segment_row)))
    up_in = low_back(jnp.dot(mlp_rows, w_up, precision=PRECISE) + b_up.reshape(FF)[None])
    activated = low(gelu_exact(up_in))
    attn_out = jnp.dot(context, w_out, precision=PRECISE) + b_out
    mlp_out = jnp.dot(activated, w_down, precision=PRECISE) + b_down
    return resid + attn_out + mlp_out

def reference(inputs, segment_ids, ln_attn_gain, ln_attn_bias, ln_mlp_gain, ln_mlp_bias, qkv_weight, qkv_bias, out_weight, out_bias, up_weight, up_bias, down_weight, down_bias, cotangent):
    params = (ln_attn_gain.astype(jnp.float32), ln_attn_bias.astype(jnp.float32), ln_mlp_gain.astype(jnp.float32), ln_mlp_bias.astype(jnp.float32), qkv_weight.astype(jnp.float32), qkv_bias.astype(jnp.float32), out_weight.astype(jnp.float32), out_bias.astype(jnp.float32), up_weight.astype(jnp.float32), up_bias.astype(jnp.float32), down_weight.astype(jnp.float32), down_bias.astype(jnp.float32))
    resid_all = inputs.astype(jnp.float32).reshape(N_DP, SEQ, D)
    segment_all = segment_ids.reshape(N_DP, SEQ)
    grad_all = cotangent.astype(jnp.float32).reshape(N_DP, SEQ, D)

    def one_sequence(carry, item):
        resid, segment_row, grad_row = item
        result, pullback = jax.vjp(lambda weights, rows: forward(weights, rows, segment_row), params, resid)
        d_params, d_resid = pullback(grad_row)
        carry = jax.tree.map(jnp.add, carry, d_params)
        return (carry, (result, d_resid))
    zeros = jax.tree.map(jnp.zeros_like, params)
    grads, (results, d_inputs) = lax.scan(one_sequence, zeros, (resid_all, segment_all, grad_all))
    return (results.reshape(TOKENS, D).astype(jnp.bfloat16), d_inputs.reshape(TOKENS, D), grads[0], grads[1], grads[2], grads[3], grads[4], grads[5], grads[6], grads[7], grads[8], grads[9], grads[10], grads[11])
```

```python
import functools
import math

import jax
import jax.numpy as jnp
import numpy as np
from jax import lax
from jax.experimental import pallas as pl
from jax.experimental.pallas import tpu as pltpu
from jax.sharding import PartitionSpec as P

HEAD = 64
ROT = 16

EPSILON = 1e-05
NEGATIVE = -1e30
MESH = pl.DeviceIdType.MESH
F32 = jnp.float32
BF16 = jnp.bfloat16
NN = (((1,), (0,)), ((), ()))
NT = (((1,), (1,)), ((), ()))
TN = (((0,), (0,)), ((), ()))
VMEM_BYTES = 63 << 20


def dot(a, b, dims=NN):
    return lax.dot_general(a, b, dims, preferred_element_type=F32)


class Sizes:
    def __init__(self, n_dp, n_t, seq, rows, d, width, units):
        self.n_dp, self.n_t, self.seq, self.rows, self.d = n_dp, n_t, seq, rows, d
        self.width, self.units = width, units
        self.nz = n_dp // 4
        self.shard = d // n_dp
        self.nf = units // width
        self.chunks = 4 + 2 * self.nf
        self.block = min(256, rows)
        self.n_blocks = seq // self.block
        self.own_blocks = rows // self.block
        self.pairs = width // 128
        self.sums_width = max(d, 3 * width, units)
        self.p_slots = 2
        self.r_slots = 4


def fused_kernel(sz, *refs):
    (
        x_hbm, g_hbm, w_hbm, small_in, seg_ref, cos_ref, sin_ref,
        out_hbm, igrad_hbm, dw_ref, sums_ref,
        xa, ga, ha, hm, stat, wts, sm, vec_d, vec_q, vec_u, pool, ctx, dproj, dup, acc, bias,
        part, red_c, red_y, red_z, b_send, b_recv, h_send, h_recv, sums_in,
        local_sem, sm_s, sm_r, row_s, row_r, gz_s, gz_r, gy_s, gy_r, gc_s, gc_r,
        rc_s, rc_r, ry_s, ry_r, rz_s, rz_r, xt_s, xt_r, su_s, su_r, credit,
    ) = refs
    nz, r, D, W, S, R, T = sz.nz, sz.shard, sz.d, sz.width, sz.seq, sz.rows, sz.n_t
    nf, NCH = sz.nf, sz.chunks
    dp = lax.axis_index("dp")
    t = lax.axis_index("tensor")
    z, y, c = lax.div(dp, 4), lax.rem(lax.div(dp, 2), 2), lax.rem(dp, 2)

    def dev(z_, y_, c_, t_):
        return ((z_ * 2 + y_) * 2 + c_, t_)

    z_peer = [dev(lax.rem(z + k, nz), y, c, t) for k in range(1, nz)]
    y_peer = dev(z, 1 - y, c, t)
    c_peer = dev(z, y, 1 - c, t)
    t_peer = [dev(z, y, c, lax.rem(t + k, T)) for k in range(1, T)]

    def remote(src, dst, s_sem, r_sem, to):
        return pltpu.make_async_remote_copy(
            src_ref=src, dst_ref=dst, send_sem=s_sem, recv_sem=r_sem, device_id=to, device_id_type=MESH
        )

    own = pl.ds(pl.multiple_of(t * R, R), R)

    cp_w = pltpu.make_async_copy(w_hbm, wts.at[:, z, y, c], local_sem.at[0])
    cp_x = pltpu.make_async_copy(x_hbm, xa.at[own], local_sem.at[1])
    cp_g = pltpu.make_async_copy(g_hbm, ga.at[own], local_sem.at[2])
    cp_w.start()
    cp_x.start()
    cp_g.start()
    sm[z, y, c, t] = small_in[...]
    barrier = pltpu.get_barrier_semaphore()
    everyone = z_peer + [y_peer, c_peer] + t_peer
    for peer in everyone:
        pl.semaphore_signal(barrier, inc=1, device_id=peer, device_id_type=MESH)
    pl.semaphore_wait(barrier, len(everyone))

    sm_t = [remote(sm.at[z, y, c, t], sm.at[z, y, c, t], sm_s.at[k], sm_r.at[k], t_peer[k]) for k in range(T - 1)]
    for cp in sm_t:
        cp.start()
    cp_w.wait()

    def gz(ch, k):
        return remote(wts.at[ch, z, y, c], wts.at[ch, z, y, c], gz_s.at[ch, k], gz_r.at[ch, k], z_peer[k])

    def gy(ch):
        return remote(wts.at[ch, :, y, c], wts.at[ch, :, y, c], gy_s.at[ch], gy_r.at[ch], y_peer)

    def gc(ch):
        return remote(wts.at[ch, :, :, c], wts.at[ch, :, :, c], gc_s.at[ch], gc_r.at[ch], c_peer)

    cp_x.wait()
    cp_g.wait()
    row_x = [remote(xa.at[own], xa.at[own], row_s.at[0, k], row_r.at[0, k], t_peer[k]) for k in range(T - 1)]
    row_g = [remote(ga.at[own], ga.at[own], row_s.at[1, k], row_r.at[1, k], t_peer[k]) for k in range(T - 1)]
    for cp in row_x:
        cp.start()
    sm_z = [remote(sm.at[z, y, c], sm.at[z, y, c], sm_s.at[T - 1 + k], sm_r.at[T - 1 + k], z_peer[k]) for k in range(nz - 1)]
    sm_y = remote(sm.at[:, y, c], sm.at[:, y, c], sm_s.at[T + nz - 2], sm_r.at[T + nz - 2], y_peer)
    sm_c = remote(sm.at[:, :, c], sm.at[:, :, c], sm_s.at[T + nz - 1], sm_r.at[T + nz - 1], c_peer)
    for cp in sm_t:
        cp.wait_recv()
    for cp in sm_z:
        cp.start()

    def start_z(ch, carry):
        for k in range(nz - 1):
            gz(ch, k).start()
        return carry

    lax.fori_loop(0, NCH, start_z, 0)
    for cp in row_g:
        cp.start()

    def gather_event(e):
        def on_y():
            for k in range(nz - 1):
                gz(e, k).wait_recv()
            gy(e).start()

        def on_c():
            gy(e - 1).wait_recv()
            gc(e - 1).start()

        if isinstance(e, int):
            if e < NCH:
                on_y()
            if 1 <= e <= NCH:
                on_c()
        else:
            pl.when(e < NCH)(on_y)
            pl.when((e >= 1) & (e <= NCH))(on_c)

    def weights(ch):
        return wts[ch].reshape(D, W)

    def weight_rows(ch, i, n):
        if n <= nz:
            return wts[ch, pl.ds(i * (nz // n), nz // n)].reshape(D // n, W)
        return wts[ch].reshape(D, W)

    for cp in sm_z:
        cp.wait_recv()
    sm_y.start()
    tile = 128

    def stat_rows(first, count):
        def body(i, carry):
            rows = pl.ds(pl.multiple_of(first + i * tile, tile), tile)
            v = xa[rows, :].astype(F32)
            mean = jnp.mean(v, axis=-1, keepdims=True)
            cen = v - mean
            inv = lax.rsqrt(jnp.mean(cen * cen, axis=-1, keepdims=True) + EPSILON)
            stat[0, rows, :] = jnp.broadcast_to(mean, (tile, 128))
            stat[1, rows, :] = jnp.broadcast_to(inv, (tile, 128))
            return carry

        lax.fori_loop(0, count // tile, body, 0)

    stat_rows(t * R, R)
    sm_y.wait_recv()
    sm_c.start()
    gather_event(0)
    sm_c.wait_recv()

    flat = sm[...].reshape(sz.n_dp * T * 16, 128)
    n_rows = sz.n_dp * T * 16
    pick = (
        jnp.bitwise_and(lax.broadcasted_iota(jnp.int32, (16, n_rows), 1), 15)
        == lax.broadcasted_iota(jnp.int32, (16, n_rows), 0)
    ).astype(F32).astype(BF16)

    def lay_out(width, n, mine_only):
        shift = n.bit_length() - 1
        lane_of = lax.broadcasted_iota(jnp.int32, (128, width), 1)
        spread = (jnp.bitwise_and(lane_of, n - 1) == lax.broadcasted_iota(jnp.int32, (128, width), 0)).astype(F32).astype(BF16)
        wide = dot(flat, spread)
        piece = jnp.right_shift(lax.broadcasted_iota(jnp.int32, (n_rows, width), 1), shift)
        owner = jnp.right_shift(lax.broadcasted_iota(jnp.int32, (n_rows, width), 0), 4)
        if mine_only:
            piece = piece * T + t
        return dot(pick, jnp.where(piece == owner, wide, 0.0).astype(BF16))

    vec_d[...] = lay_out(D, D // (sz.n_dp * T), False)
    vec_q[...] = lay_out(W, W // sz.n_dp, True)
    for f in range(nf):
        vec_u_part = lay_out_units(sz, flat, pick, n_rows, t, f)
        vec_u[f] = vec_u_part

    def norm_rows(first, count):
        def body(i, carry):
            rows = pl.ds(pl.multiple_of(first + i * tile, tile), tile)
            norm = (xa[rows, :].astype(F32) - stat[0, rows, 0:1]) * stat[1, rows, 0:1]
            ha[rows, :] = (norm * vec_d[0:1, :] + vec_d[1:2, :]).astype(BF16)
            hm[rows, :] = (norm * vec_d[2:3, :] + vec_d[3:4, :]).astype(BF16)
            return carry

        lax.fori_loop(0, count // tile, body, 0)

    norm_rows(t * R, R)
    gather_event(1)
    for k in range(1, T):
        row_x[k - 1].wait_recv()
        first = lax.rem(t + T - k, T) * R
        stat_rows(first, R)
        norm_rows(first, R)

    lane = lax.broadcasted_iota(jnp.int32, (1, 128), 1)
    low_half = lane < HEAD
    from_right = jnp.bitwise_and(lane, HEAD - 1) < ROT // 2

    def turned(u, rows, sign):
        other = jnp.where(from_right, pltpu.roll(u, 128 - ROT // 2, 1), pltpu.roll(u, ROT // 2, 1))
        turn = other * sin_ref[rows, :]
        return u * cos_ref[rows, :] + (turn if sign > 0 else -turn)

    big = min(512, R)
    for j in range(3):
        gather_event(j + 2)
        gc(j).wait_recv()

        def project(i, carry, j=j):
            rows = pl.ds(pl.multiple_of(i * big, big), big)
            u = dot(ha[rows, :], weights(j)) + vec_q[6 + j : 7 + j, :]
            for g in range(sz.pairs):
                part_u = u[:, g * 128 : (g + 1) * 128]
                if j < 2:
                    part_u = turned(part_u, rows, 1)
                if j == 0:
                    part_u = part_u * (1.0 / math.sqrt(HEAD))
                pool[j, rows, g * 128 : (g + 1) * 128] = part_u.astype(BF16)
            return carry

        lax.fori_loop(0, S // big, project, 0)
    gc(3).wait_recv()

    def d_context(first):
        def body(i, carry):
            rows = pl.ds(pl.multiple_of(first + i * big, big), big)
            pool[3, rows, :] = dot(ga[rows, :], weights(3)).astype(BF16)
            return carry

        lax.fori_loop(0, R // big, body, 0)

    d_context(t * R)
    acc[...] = jnp.zeros_like(acc)

    B = sz.block
    n_steps = sz.n_blocks * sz.pairs
    first_event = 5
    stride = 3

    def attend(qb, step0):
        L = (qb + 1) * B
        rows = pl.ds(qb * B, B)
        for s in range(B // 128):
            here = pl.ds(s * 128, 128)
            start = jnp.broadcast_to(seg_ref[0:1, qb * B + s * 128 : qb * B + (s + 1) * 128].astype(F32), (128, 128)).T
            start = start[:, 0:1].astype(jnp.int32)
            key_at = lax.broadcasted_iota(jnp.int32, (128, L), 1)
            row_at = lax.broadcasted_iota(jnp.int32, (128, L), 0) + (qb * B + s * 128)
            bias[here, :L] = jnp.where((key_at >= start) & (key_at <= row_at), 0.0, NEGATIVE)

        def pair(p, carry):
            cols = pl.ds(pl.multiple_of(p * 128, 128), 128)
            keys, values = pool[1, :L, cols], pool[2, :L, cols]
            query, d_ctx = pool[0, rows, cols], pool[3, rows, cols]
            made = []
            for h in range(2):
                mine = low_half if h == 0 else jnp.logical_not(low_half)
                q_h = jnp.where(mine, query, jnp.zeros_like(query))
                d_h = jnp.where(mine, d_ctx, jnp.zeros_like(d_ctx))
                scores = dot(q_h, keys, NT) + bias[:, :L]
                top = jnp.max(scores, axis=1, keepdims=True)
                e = jnp.exp(scores - top)
                prob = e * (1.0 / jnp.sum(e, axis=1, keepdims=True))
                d_prob = dot(d_h, values, NT)
                delta = jnp.sum(prob * d_prob, axis=1, keepdims=True)
                d_s = (prob * (d_prob - delta)).astype(BF16)
                p_b = prob.astype(BF16)
                made.append((dot(p_b, values), dot(d_s, keys), dot(d_s, q_h, TN), dot(p_b, d_h, TN)))
            ctx[rows, cols] = jnp.where(low_half, made[0][0], made[1][0]).astype(BF16)
            d_q = jnp.where(low_half, made[0][1], made[1][1]) * (1.0 / math.sqrt(HEAD))
            dproj[0, rows, cols] = turned(d_q, rows, -1).astype(BF16)
            acc[:L, cols] += made[0][2] + made[1][2]
            cols_v = pl.ds(pl.multiple_of(W + p * 128, 128), 128)
            acc[:L, cols_v] += made[0][3] + made[1][3]
            at = step0 + p
            pl.when(lax.rem(at, stride) == stride - 1)(lambda: gather_event(first_event + lax.div(at, stride)))
            return carry

        lax.fori_loop(0, sz.pairs, pair, 0)

    def block_step(j, carry):
        def rest():
            for k in range(1, T):
                row_g[k - 1].wait_recv()
                d_context(lax.rem(t + T - k, T) * R)

        pl.when(j == sz.own_blocks)(rest)
        which = lax.rem(j + t * sz.own_blocks, sz.n_blocks)
        for qb in range(sz.n_blocks):
            pl.when(which == qb)(functools.partial(attend, qb, j * sz.pairs))
        return carry

    lax.fori_loop(0, sz.n_blocks, block_step, 0)
    next_event = first_event + n_steps // stride

    def finish_proj(i, carry):
        rows = pl.ds(pl.multiple_of(i * tile, tile), tile)
        for g in range(sz.pairs):
            cols = pl.ds(g * 128, 128)
            dproj[1, rows, cols] = turned(acc[rows, cols], rows, -1).astype(BF16)
            dproj[2, rows, cols] = acc[rows, pl.ds(W + g * 128, 128)].astype(BF16)
        return carry

    lax.fori_loop(0, S // tile, finish_proj, 0)

    def rc(i):
        return remote(
            part.at[lax.rem(i, sz.p_slots), :, :, 1 - c], red_c.at[lax.rem(i, sz.r_slots)], rc_s.at[i], rc_r.at[i], c_peer
        )

    def ry(i):
        return remote(red_c.at[lax.rem(i, sz.r_slots), :, 1 - y], red_y.at[i], ry_s.at[i], ry_r.at[i], y_peer)

    def rz(i, k):
        return remote(red_y.at[i, lax.rem(z + k + 1, nz)], red_z.at[i, k], rz_s.at[i, k], rz_r.at[i, k], z_peer[k])

    def emit(i, left, right):
        slot = lax.rem(i, sz.p_slots)

        def body(n, carry):
            cols = pl.ds(pl.multiple_of(n * (D // 2), D // 2), D // 2)
            made = dot(left[:, cols], right[...], TN)
            part[slot, pl.ds(n * (nz // 2), nz // 2)] = made.astype(BF16).reshape(nz // 2, 2, 2, r, W)
            return carry

        lax.fori_loop(0, 2, body, 0)
        pl.when(i >= sz.r_slots)(lambda: pl.semaphore_wait(credit, 1))
        rc(i).start()

    def event_c(i):
        rc(i).wait()
        slot, rslot = lax.rem(i, sz.p_slots), lax.rem(i, sz.r_slots)
        red_c[rslot] = (part[slot, :, :, c].astype(F32) + red_c[rslot].astype(F32)).astype(BF16)
        ry(i).start()

    def event_y(i):
        ry(i).wait()
        rslot = lax.rem(i, sz.r_slots)
        red_y[i] = (red_c[rslot, :, y].astype(F32) + red_y[i].astype(F32)).astype(BF16)
        pl.when(i < NCH - sz.r_slots)(lambda: pl.semaphore_signal(credit, inc=1, device_id=c_peer, device_id_type=MESH))
        for k in range(nz - 1):
            rz(i, k).start()

    def event_z(i):
        for k in range(nz - 1):
            rz(i, k).wait()
        total = red_y[i, z].astype(F32)
        for k in range(nz - 1):
            total = total + red_z[i, k].astype(F32)
        dw_ref[i] = total

    sums_ref[...] = jnp.zeros_like(sums_ref)

    def row_sum(v):
        return jnp.sum(v.astype(F32), axis=0, keepdims=True)

    for j in range(3):
        emit(j, ha, dproj.at[j])
        sums_ref[5:6, j * W : (j + 1) * W] = row_sum(dproj[j])
        if j:
            event_c(j - 1)
    emit(3, ga, ctx)
    event_c(2)
    for e in range(next_event, NCH + 1):
        gather_event(e)
    event_c(3)

    for ch in range(4, NCH):
        gc(ch).wait_recv()

    def mlp(first, f):
        def body(i, carry):
            rows = pl.ds(pl.multiple_of(first + i * big, big), big)
            u = dot(hm[rows, :], weights(4 + 2 * f)) + vec_u[f, 9:10, :]
            cdf = 0.5 + 0.5 * lax.erf(u * math.sqrt(0.5))
            pool[f, rows, :] = (u * cdf).astype(BF16)
            slope = cdf + u * (jnp.exp(u * u * -0.5) * (1.0 / math.sqrt(2.0 * math.pi)))
            back = slope * dot(ga[rows, :], weights(5 + 2 * f))
            dup[f, rows, :] = back.astype(BF16)
            return carry

        lax.fori_loop(0, R // big, body, 0)

    half = D // 2

    def branch(first, i, n):
        rows = pl.ds(pl.multiple_of(first + i * big, big), big)
        total = dot(ctx[rows, :], weight_rows(3, n, 2), NT)
        for f in range(nf):
            total = total + dot(pool[f, rows, :], weight_rows(5 + 2 * f, n, 2), NT)
        return total

    def d_hidden(first, i, n):
        rows = pl.ds(pl.multiple_of(first + i * big, big), big)
        cols = pl.ds(pl.multiple_of(n * half, half), half)
        d_attn = dot(dproj[0, rows, :], weight_rows(0, n, 2), NT)
        for j in range(1, 3):
            d_attn = d_attn + dot(dproj[j, rows, :], weight_rows(j, n, 2), NT)
        d_mlp = dot(dup[0, rows, :], weight_rows(4, n, 2), NT)
        for f in range(1, nf):
            d_mlp = d_mlp + dot(dup[f, rows, :], weight_rows(4 + 2 * f, n, 2), NT)
        norm = (xa[rows, cols].astype(F32) - stat[0, rows, 0:1]) * stat[1, rows, 0:1]
        sums_ref[0:1, cols] += row_sum(d_attn * norm)
        sums_ref[1:2, cols] += row_sum(d_attn)
        sums_ref[2:3, cols] += row_sum(d_mlp * norm)
        sums_ref[3:4, cols] += row_sum(d_mlp)
        return d_attn * vec_d[0:1, cols] + d_mlp * vec_d[2:3, cols]

    def xt(which, k):
        src, dst = ((b_send, b_recv), (h_send, h_recv))[which]
        return remote(src.at[k], dst.at[k], xt_s.at[which, k], xt_r.at[which, k], t_peer[k])

    for k in range(T - 1):
        first = lax.rem(t + k + 1, T) * R

        def forward_units(f, carry, first=first):
            mlp(first, f)
            return carry

        lax.fori_loop(0, nf, forward_units, 0)
        if k == 0:
            event_y(0)

        def both(q, carry, first=first, k=k):
            i, n = lax.div(q, 2), lax.rem(q, 2)
            cols = pl.ds(pl.multiple_of(n * half, half), half)
            rows = pl.ds(pl.multiple_of(i * big, big), big)
            b_send[k, rows, cols] = branch(first, i, n).astype(BF16)
            return carry

        lax.fori_loop(0, 2 * (R // big), both, 0)
        xt(0, k).start()
        if k == 0:
            event_y(1)
            event_z(0)

        def both_back(q, carry, first=first, k=k):
            i, n = lax.div(q, 2), lax.rem(q, 2)
            cols = pl.ds(pl.multiple_of(n * half, half), half)
            rows = pl.ds(pl.multiple_of(i * big, big), big)
            h_send[k, rows, cols] = d_hidden(first, i, n).astype(BF16)
            return carry

        lax.fori_loop(0, 2 * (R // big), both_back, 0)
        xt(1, k).start()

    def own_units(f, carry):
        mlp(t * R, f)
        first = 4 + 2 * f
        sums_ref[6:7, pl.ds(pl.multiple_of(f * W, W), W)] = row_sum(dup[f])
        emit(first, hm, dup.at[f])
        pl.when(f > 0)(lambda: event_c(first - 1))
        event_y(first - 2)
        event_z(first - 3)
        emit(first + 1, ga, pool.at[f])
        event_c(first)
        event_y(first - 1)
        event_z(first - 2)
        return carry

    lax.fori_loop(0, nf, own_units, 0)
    last = NCH - 1
    event_c(last)

    def own_both(q, carry):
        i, n = lax.div(q, 2), lax.rem(q, 2)
        cols = pl.ds(pl.multiple_of(n * half, half), half)
        acc[pl.ds(pl.multiple_of(i * big, big), big), cols] = branch(t * R, i, n)
        return carry

    lax.fori_loop(0, 2 * (R // big), own_both, 0)
    event_y(last - 1)
    event_z(last - 2)

    def own_back(q, carry):
        i, n = lax.div(q, 2), lax.rem(q, 2)
        cols = pl.ds(pl.multiple_of(n * half, half), half)
        acc[pl.ds(pl.multiple_of(R + i * big, big), big), cols] = d_hidden(t * R, i, n)
        return carry

    lax.fori_loop(0, 2 * (R // big), own_back, 0)
    sums_ref[4:5, :D] = row_sum(ga[own, :])
    event_y(last)

    su_c = remote(sums_ref, sums_in.at[0], su_s.at[0], su_r.at[0], c_peer)
    su_c.start()
    event_z(last - 1)
    su_c.wait()
    sums_ref[...] += sums_in[0]
    su_y = remote(sums_ref, sums_in.at[1], su_s.at[1], su_r.at[1], y_peer)
    su_y.start()

    for k in range(T - 1):
        xt(0, k).wait()

    def finish_out(i, carry):
        rows = pl.ds(pl.multiple_of(i * tile, tile), tile)
        here = pl.ds(pl.multiple_of(t * R + i * tile, tile), tile)
        total = xa[here, :].astype(F32) + acc[rows, :] + (vec_d[4:5, :] + vec_d[5:6, :])
        for k in range(T - 1):
            total = total + b_recv[k, rows, :].astype(F32)
        b_send[0, rows, :] = total.astype(BF16)
        return carry

    lax.fori_loop(0, R // tile, finish_out, 0)
    cp_out = pltpu.make_async_copy(b_send.at[0], out_hbm, local_sem.at[3])
    cp_out.start()
    su_y.wait()
    sums_ref[...] += sums_in[1]
    su_z = [remote(sums_ref, sums_in.at[2 + k], su_s.at[2 + k], su_r.at[2 + k], z_peer[k]) for k in range(nz - 1)]
    for cp in su_z:
        cp.start()

    for k in range(T - 1):
        xt(1, k).wait()

    def finish_grad(i, carry):
        rows = pl.ds(pl.multiple_of(R + i * tile, tile), tile)
        there = pl.ds(pl.multiple_of(i * tile, tile), tile)
        here = pl.ds(pl.multiple_of(t * R + i * tile, tile), tile)
        inv = stat[1, here, 0:1]
        norm = (xa[here, :].astype(F32) - stat[0, here, 0:1]) * inv
        d_hat = acc[rows, :]
        for k in range(T - 1):
            d_hat = d_hat + h_recv[k, there, :].astype(F32)
        inner = jnp.mean(d_hat * norm, axis=-1, keepdims=True)
        acc[rows, :] = ga[here, :].astype(F32) + inv * (d_hat - jnp.mean(d_hat, axis=-1, keepdims=True) - norm * inner)
        return carry

    lax.fori_loop(0, R // tile, finish_grad, 0)
    cp_grad = pltpu.make_async_copy(acc.at[pl.ds(R, R)], igrad_hbm, local_sem.at[4])
    cp_grad.start()
    for cp in su_z:
        cp.wait()
    for k in range(nz - 1):
        sums_ref[...] += sums_in[2 + k]
    su_t = [
        remote(sums_ref, sums_in.at[1 + nz + k], su_s.at[1 + nz + k], su_r.at[1 + nz + k], t_peer[k]) for k in range(T - 1)
    ]
    for cp in su_t:
        cp.start()
    event_z(last)
    for cp in su_t:
        cp.wait()
    for k in range(T - 1):
        sums_ref[0:5, :] += sums_in[1 + nz + k, 0:5, :]

    for cp in sm_t + sm_z + [sm_y, sm_c] + row_x + row_g:
        cp.wait_send()

    def sent(ch, carry):
        for k in range(nz - 1):
            gz(ch, k).wait_send()
        gy(ch).wait_send()
        gc(ch).wait_send()
        return carry

    lax.fori_loop(0, NCH, sent, 0)
    cp_out.wait()
    cp_grad.wait()


def lay_out_units(sz, flat, pick, n_rows, t, f):
    n = sz.units // sz.n_dp
    shift = n.bit_length() - 1
    W = sz.width
    lane_of = lax.broadcasted_iota(jnp.int32, (128, W), 1) + f * W
    spread = (jnp.bitwise_and(lane_of, n - 1) == lax.broadcasted_iota(jnp.int32, (128, W), 0)).astype(F32).astype(BF16)
    wide = dot(flat, spread)
    piece = jnp.right_shift(lax.broadcasted_iota(jnp.int32, (n_rows, W), 1) + f * W, shift) * sz.n_t + t
    owner = jnp.right_shift(lax.broadcasted_iota(jnp.int32, (n_rows, W), 0), 4)
    return dot(pick, jnp.where(piece == owner, wide, 0.0).astype(BF16))


def fused(sz, args):
    (
        inputs, segment_ids, ln_attn_gain, ln_attn_bias, ln_mlp_gain, ln_mlp_bias, qkv_weight, qkv_bias,
        out_weight, out_bias, up_weight, up_bias, down_weight, down_bias, cotangent,
    ) = args
    nz, r, D, W, S, R, T, nf, NCH = sz.nz, sz.shard, sz.d, sz.width, sz.seq, sz.rows, sz.n_t, sz.nf, sz.chunks

    def row(v):
        v = v.reshape(1, -1)
        return jnp.pad(v, ((0, 0), (0, 128 - v.shape[1])))

    small = jnp.concatenate(
        [row(v) for v in (ln_attn_gain, ln_attn_bias, ln_mlp_gain, ln_mlp_bias, out_bias, down_bias)]
        + [row(qkv_bias[j]) for j in range(3)]
        + [row(up_bias), jnp.zeros((6, 128), BF16)],
        axis=0,
    )
    up = up_weight.reshape(r, nf, W).transpose(1, 0, 2)
    down = down_weight.reshape(nf, W, r).transpose(0, 2, 1)
    packed = jnp.concatenate(
        [
            qkv_weight.transpose(1, 0, 2),
            out_weight.T[None],
            jnp.stack([up, down], axis=1).reshape(2 * nf, r, W),
        ],
        axis=0,
    )
    half_rot = ROT // 2
    place = np.arange(S, dtype=np.float32)
    inverse = (10000.0 ** (-(2.0 * np.arange(half_rot, dtype=np.float32)) / ROT)).astype(np.float32)
    theta = place[:, None] * inverse[None, :]
    cos, sin = np.cos(theta), np.sin(theta)
    cos_head = np.concatenate([cos, cos, np.ones((S, HEAD - ROT), np.float32)], axis=1)
    sin_head = np.concatenate([-sin, sin, np.zeros((S, HEAD - ROT), np.float32)], axis=1)
    cos_table = jnp.asarray(np.tile(cos_head, (1, 128 // HEAD)), F32)
    sin_table = jnp.asarray(np.tile(sin_head, (1, 128 // HEAD)), F32)

    hbm = pl.BlockSpec(memory_space=pl.ANY)
    vmem = pl.BlockSpec(memory_space=pltpu.VMEM)
    sw = sz.sums_width
    dma = pltpu.SemaphoreType.DMA
    n_small = T - 1 + nz - 1 + 2
    scratch = [
        pltpu.VMEM((S, D), BF16),
        pltpu.VMEM((S, D), BF16),
        pltpu.VMEM((S, D), BF16),
        pltpu.VMEM((S, D), BF16),
        pltpu.VMEM((2, S, 128), F32),
        pltpu.VMEM((NCH, nz, 2, 2, r, W), BF16),
        pltpu.VMEM((nz, 2, 2, T, 16, 128), BF16),
        pltpu.VMEM((16, D), F32),
        pltpu.VMEM((16, W), F32),
        pltpu.VMEM((nf, 16, W), F32),
        pltpu.VMEM((max(4, nf), S, W), BF16),
        pltpu.VMEM((S, W), BF16),
        pltpu.VMEM((3, S, W), BF16),
        pltpu.VMEM((nf, S, W), BF16),
        pltpu.VMEM((S, D), F32),
        pltpu.VMEM((sz.block, S), F32),
        pltpu.VMEM((sz.p_slots, nz, 2, 2, r, W), BF16),
        pltpu.VMEM((sz.r_slots, nz, 2, r, W), BF16),
        pltpu.VMEM((NCH, nz, r, W), BF16),
        pltpu.VMEM((NCH, nz - 1, r, W), BF16),
        pltpu.VMEM((T - 1, R, D), BF16),
        pltpu.VMEM((T - 1, R, D), BF16),
        pltpu.VMEM((T - 1, R, D), BF16),
        pltpu.VMEM((T - 1, R, D), BF16),
        pltpu.VMEM((nz + T, 8, sw), F32),
        dma((5,)),
        dma((n_small,)), dma((n_small,)),
        dma((2, T - 1)), dma((2, T - 1)),
        dma((NCH, nz - 1)), dma((NCH, nz - 1)),
        dma((NCH,)), dma((NCH,)),
        dma((NCH,)), dma((NCH,)),
        dma((NCH,)), dma((NCH,)),
        dma((NCH,)), dma((NCH,)),
        dma((NCH, nz - 1)), dma((NCH, nz - 1)),
        dma((2, T - 1)), dma((2, T - 1)),
        dma((nz + T,)), dma((nz + T,)),
        pltpu.SemaphoreType.REGULAR,
    ]
    output, input_grad, dw, sums = pl.pallas_call(
        functools.partial(fused_kernel, sz),
        out_shape=(
            jax.ShapeDtypeStruct((R, D), BF16),
            jax.ShapeDtypeStruct((R, D), F32),
            jax.ShapeDtypeStruct((NCH, r, W), F32),
            jax.ShapeDtypeStruct((8, sw), F32),
        ),
        in_specs=[hbm, hbm, hbm, vmem, vmem, vmem, vmem],
        out_specs=(hbm, hbm, vmem, vmem),
        scratch_shapes=scratch,
        compiler_params=pltpu.CompilerParams(collective_id=0, has_side_effects=True, vmem_limit_bytes=VMEM_BYTES),
    )(inputs, cotangent, packed, small, segment_ids.reshape(1, S), cos_table, sin_table)

    dp, t = lax.axis_index("dp"), lax.axis_index("tensor")
    n = D // (sz.n_dp * T)
    here = lax.dynamic_slice(sums, (0, (dp * T + t) * n), (5, n))
    nq, nu = W // sz.n_dp, sz.units // sz.n_dp
    d_qkv_bias = lax.dynamic_slice(sums[5, : 3 * W].reshape(3, 1, W), (0, 0, dp * nq), (3, 1, nq))
    d_up_bias = lax.dynamic_slice(sums, (6, dp * nu), (1, nu))
    return (
        output, input_grad, here[0], here[1], here[2], here[3],
        dw[:3].transpose(1, 0, 2), d_qkv_bias, dw[3].T, here[4],
        dw[4::2].transpose(1, 0, 2).reshape(r, sz.units), d_up_bias,
        dw[5::2].transpose(0, 2, 1).reshape(sz.units, r), here[4],
    )


def rotated(values, cosine, sine, sign):
    half_rot = ROT // 2
    first_half = values[..., :half_rot]
    second_half = values[..., half_rot:ROT]
    new_first = first_half * cosine - sign * second_half * sine
    new_second = second_half * cosine + sign * first_half * sine
    return jnp.concatenate([new_first, new_second, values[..., ROT:]], axis=-1)


def angle_tables(length):
    position = jnp.arange(length).astype(jnp.float32)
    inverse = 10000.0 ** (-(2.0 * jnp.arange(ROT // 2).astype(jnp.float32)) / ROT)
    theta = position[:, None] * inverse[None, :]
    return (jnp.cos(theta)[:, None, :], jnp.sin(theta)[:, None, :])


def gelu_exact(value):
    return jax.nn.gelu(value, approximate=False)


def layer_norm(rows):
    centred = rows - jnp.mean(rows, axis=-1, keepdims=True)
    inv_std = lax.rsqrt(jnp.mean(centred * centred, axis=-1, keepdims=True) + EPSILON)
    return (centred * inv_std, inv_std)


def plain(
    inputs,
    segment_ids,
    ln_attn_gain,
    ln_attn_bias,
    ln_mlp_gain,
    ln_mlp_bias,
    qkv_weight,
    qkv_bias,
    out_weight,
    out_bias,
    up_weight,
    up_bias,
    down_weight,
    down_bias,
    cotangent,
):
    seq_len = segment_ids.shape[0]
    norm_terms = (
        lax.all_gather(ln_attn_gain, ("dp", "tensor"), axis=0, tiled=True),
        lax.all_gather(ln_attn_bias, ("dp", "tensor"), axis=0, tiled=True),
        lax.all_gather(ln_mlp_gain, ("dp", "tensor"), axis=0, tiled=True),
        lax.all_gather(ln_mlp_bias, ("dp", "tensor"), axis=0, tiled=True),
        lax.all_gather(out_bias, ("dp", "tensor"), axis=0, tiled=True),
        lax.all_gather(down_bias, ("dp", "tensor"), axis=0, tiled=True),
    )
    gain_attn = norm_terms[0].astype(jnp.float32)
    shift_attn = norm_terms[1].astype(jnp.float32)
    gain_mlp = norm_terms[2].astype(jnp.float32)
    shift_mlp = norm_terms[3].astype(jnp.float32)
    bias_sum = norm_terms[4].astype(jnp.float32) + norm_terms[5].astype(jnp.float32)
    w_qkv, b_qkv, w_out, w_up, b_up, w_down = (
        lax.all_gather(qkv_weight, "dp", axis=0, tiled=True),
        lax.all_gather(qkv_bias, "dp", axis=2, tiled=True),
        lax.all_gather(out_weight, "dp", axis=1, tiled=True),
        lax.all_gather(up_weight, "dp", axis=0, tiled=True),
        lax.all_gather(up_bias, "dp", axis=1, tiled=True),
        lax.all_gather(down_weight, "dp", axis=1, tiled=True),
    )
    local_width = w_qkv.shape[2]
    heads_here = local_width // HEAD
    score_scale = 1.0 / math.sqrt(HEAD)
    resid = inputs.astype(jnp.float32)
    normalized, inv_std = layer_norm(resid)
    whole_inputs = lax.all_gather(inputs, "tensor", axis=0, tiled=True)
    normal_all, unused_std = layer_norm(whole_inputs.astype(jnp.float32))
    attn_rows = (normal_all * gain_attn + shift_attn).astype(jnp.bfloat16)
    mlp_rows = (normal_all * gain_mlp + shift_mlp).astype(jnp.bfloat16)
    proj = jnp.einsum("sd,dje->sje", attn_rows, w_qkv, preferred_element_type=jnp.float32)
    proj = proj + b_qkv.astype(jnp.float32).reshape(1, 3, local_width)
    cosine, sine = angle_tables(seq_len)
    query = rotated(proj[:, 0].reshape(seq_len, heads_here, HEAD), cosine, sine, 1.0).astype(
        jnp.bfloat16
    )
    keys = rotated(proj[:, 1].reshape(seq_len, heads_here, HEAD), cosine, sine, 1.0).astype(
        jnp.bfloat16
    )
    values = proj[:, 2].reshape(seq_len, heads_here, HEAD).astype(jnp.bfloat16)
    block_rows = min(512, seq_len)
    block_count = seq_len // block_rows
    places = jnp.arange(seq_len)
    query_blocks = query.reshape(block_count, block_rows, heads_here, HEAD)
    segment_blocks = segment_ids.reshape(block_count, block_rows)
    place_blocks = places.reshape(block_count, block_rows)

    def masked_scores(query_part, segment_part, place_part):
        scores = (
            jnp.einsum("qhe,khe->hqk", query_part, keys, preferred_element_type=jnp.float32)
            * score_scale
        )
        allowed = (segment_part[:, None] == segment_ids[None, :]) & (
            place_part[:, None] >= places[None, :]
        )
        return jnp.where(allowed[None], scores, NEGATIVE)

    def forward_block(block_item):
        query_part, segment_part, place_part = block_item
        scores = masked_scores(query_part, segment_part, place_part)
        row_max = jnp.max(scores, axis=-1, keepdims=True)
        exponent = jnp.exp(scores - row_max)
        row_total = jnp.sum(exponent, axis=-1, keepdims=True)
        probability = (exponent / row_total).astype(jnp.bfloat16)
        context_part = jnp.einsum(
            "hqk,khe->qhe", probability, values, preferred_element_type=jnp.float32
        )
        return (context_part, (row_max + jnp.log(row_total))[..., 0])

    context_blocks, log_totals = lax.map(
        forward_block, (query_blocks, segment_blocks, place_blocks)
    )
    context = context_blocks.reshape(seq_len, local_width).astype(jnp.bfloat16)
    up_in = jnp.dot(mlp_rows, w_up, preferred_element_type=jnp.float32) + b_up.astype(jnp.float32)
    activated = gelu_exact(up_in).astype(jnp.bfloat16)
    context_part = context
    branch_sum = lax.psum_scatter(
        jnp.dot(context_part, w_out, preferred_element_type=jnp.float32)
        + jnp.dot(activated, w_down, preferred_element_type=jnp.float32),
        "tensor",
        scatter_dimension=0,
        tiled=True,
    )
    output = (resid + branch_sum + bias_sum).astype(jnp.bfloat16)
    grad_all = lax.all_gather(cotangent, "tensor", axis=0, tiled=True)
    d_active = jnp.einsum("sd,fd->sf", grad_all, w_down, preferred_element_type=jnp.float32)
    gelu_value, gelu_back = jax.vjp(gelu_exact, up_in)
    d_up = gelu_back(d_active)[0].astype(jnp.bfloat16)
    d_w_down = jnp.einsum("sf,sd->fd", activated, grad_all, preferred_element_type=jnp.float32)
    d_w_up = jnp.einsum("sd,sf->df", mlp_rows, d_up, preferred_element_type=jnp.float32)
    d_b_up = jnp.sum(d_up, axis=0, dtype=jnp.float32).reshape(1, -1)
    unit_sums = (d_w_up, d_b_up, d_w_down)
    d_context = jnp.einsum("sd,cd->sc", grad_all, w_out, preferred_element_type=jnp.float32).astype(
        jnp.bfloat16
    )
    d_w_out = jnp.einsum("sc,sd->cd", context, grad_all, preferred_element_type=jnp.float32)
    d_context_blocks = d_context.reshape(block_count, block_rows, heads_here, HEAD)

    def backward_block(carry, block_item):
        d_keys, d_values = carry
        query_part, d_context_part, segment_part, place_part, log_part = block_item
        scores = masked_scores(query_part, segment_part, place_part)
        probability = jnp.exp(scores - log_part[..., None])
        d_prob = jnp.einsum(
            "qhe,khe->hqk", d_context_part, values, preferred_element_type=jnp.float32
        )
        row_delta = jnp.sum(probability * d_prob, axis=-1, keepdims=True)
        d_scores = (probability * (d_prob - row_delta)).astype(jnp.bfloat16)
        d_query_part = (
            jnp.einsum("hqk,khe->qhe", d_scores, keys, preferred_element_type=jnp.float32)
            * score_scale
        )
        d_keys = (
            d_keys
            + jnp.einsum("hqk,qhe->khe", d_scores, query_part, preferred_element_type=jnp.float32)
            * score_scale
        )
        d_values = d_values + jnp.einsum(
            "hqk,qhe->khe",
            probability.astype(jnp.bfloat16),
            d_context_part,
            preferred_element_type=jnp.float32,
        )
        return ((d_keys, d_values), d_query_part)

    zero_rows = jnp.zeros((seq_len, heads_here, HEAD), jnp.float32)
    (d_keys, d_values), d_query_blocks = lax.scan(
        backward_block,
        (zero_rows, zero_rows),
        (query_blocks, d_context_blocks, segment_blocks, place_blocks, log_totals),
    )
    d_query = d_query_blocks.reshape(seq_len, heads_here, HEAD)
    d_proj = jnp.stack(
        [
            rotated(d_query, cosine, sine, -1.0).reshape(seq_len, local_width),
            rotated(d_keys, cosine, sine, -1.0).reshape(seq_len, local_width),
            d_values.reshape(seq_len, local_width),
        ],
        axis=1,
    ).astype(jnp.bfloat16)
    d_w_qkv = jnp.einsum("sd,sje->dje", attn_rows, d_proj, preferred_element_type=jnp.float32)
    d_b_qkv = jnp.sum(d_proj, axis=0, dtype=jnp.float32).reshape(3, 1, local_width)
    grad_rows = cotangent.astype(jnp.float32)
    attn_term = jnp.einsum("sje,dje->sd", d_proj, w_qkv, preferred_element_type=jnp.float32)
    mlp_term = jnp.einsum("sf,df->sd", d_up, w_up, preferred_element_type=jnp.float32)
    stacked = lax.psum_scatter(
        jnp.stack([attn_term, mlp_term], axis=1), "tensor", scatter_dimension=0, tiled=True
    )
    d_attn_norm = stacked[:, 0]
    d_mlp_norm = stacked[:, 1]
    d_hat = d_attn_norm * gain_attn + d_mlp_norm * gain_mlp
    norm_sums = (
        jnp.sum(d_attn_norm * normalized, axis=0),
        jnp.sum(d_attn_norm, axis=0),
        jnp.sum(d_mlp_norm * normalized, axis=0),
        jnp.sum(d_mlp_norm, axis=0),
    )
    input_grad = grad_rows + inv_std * (
        d_hat
        - jnp.mean(d_hat, axis=-1, keepdims=True)
        - normalized * jnp.mean(d_hat * normalized, axis=-1, keepdims=True)
    )
    small_sums = (
        lax.psum_scatter(norm_sums[0], ("dp", "tensor"), scatter_dimension=0, tiled=True),
        lax.psum_scatter(norm_sums[1], ("dp", "tensor"), scatter_dimension=0, tiled=True),
        lax.psum_scatter(norm_sums[2], ("dp", "tensor"), scatter_dimension=0, tiled=True),
        lax.psum_scatter(norm_sums[3], ("dp", "tensor"), scatter_dimension=0, tiled=True),
        lax.psum_scatter(
            jnp.sum(grad_rows, axis=0), ("dp", "tensor"), scatter_dimension=0, tiled=True
        ),
    )
    summed = (
        lax.psum_scatter(d_w_qkv, "dp", scatter_dimension=0, tiled=True),
        lax.psum_scatter(d_b_qkv, "dp", scatter_dimension=2, tiled=True),
        lax.psum_scatter(d_w_out, "dp", scatter_dimension=1, tiled=True),
        lax.psum_scatter(unit_sums[0], "dp", scatter_dimension=0, tiled=True),
        lax.psum_scatter(unit_sums[1], "dp", scatter_dimension=1, tiled=True),
        lax.psum_scatter(unit_sums[2], "dp", scatter_dimension=1, tiled=True),
    )
    return (
        output,
        input_grad,
        small_sums[0],
        small_sums[1],
        small_sums[2],
        small_sums[3],
        summed[0],
        summed[1],
        summed[2],
        small_sums[4],
        summed[3],
        summed[4],
        summed[5],
        small_sums[4],
    )


def fits(n_dp, n_t, seq, rows, d, width, units):
    if n_dp % 8 or n_t < 2 or width % 128 or units % width or rows % 128 or seq != rows * n_t:
        return False
    small = (d // (n_dp * n_t), width // n_dp, units // n_dp)
    if any(n < 1 or n > 128 or n & (n - 1) for n in small) or (d // n_dp) % 16:
        return False
    rows_of = 2 * (4 * seq * d + seq * (max(4, units // width) * width + 4 * width + units)) + 4 * seq * d
    chunks = 4 + 2 * (units // width)
    weights_of = 2 * chunks * d * width
    reduction = 2 * d * width * (2 + 2) + weights_of * 7 // 16 + 4 * chunks * (d // n_dp) * width
    exchange = 8 * (n_t - 1) * rows * d
    return rows_of + weights_of + reduction + exchange <= 54 << 20


def local(n_dp, n_t, *args):
    rows, d = args[0].shape
    seq, width, units = args[1].shape[0], args[6].shape[2], args[10].shape[1]
    if fits(n_dp, n_t, seq, rows, d, width, units):
        return fused(Sizes(n_dp, n_t, seq, rows, d, width, units), args)
    return plain(*args)


def solution(mesh):
    return jax.shard_map(
        functools.partial(local, mesh.shape["dp"], mesh.shape["tensor"]),
        mesh=mesh,
        in_specs=(
            P(("dp", "tensor"), None),
            P("dp"),
            P(("dp", "tensor")),
            P(("dp", "tensor")),
            P(("dp", "tensor")),
            P(("dp", "tensor")),
            P("dp", None, "tensor"),
            P(None, "tensor", "dp"),
            P("tensor", "dp"),
            P(("dp", "tensor")),
            P("dp", "tensor"),
            P("tensor", "dp"),
            P("tensor", "dp"),
            P(("dp", "tensor")),
            P(("dp", "tensor"), None),
        ),
        out_specs=(
            P(("dp", "tensor"), None),
            P(("dp", "tensor"), None),
            P(("dp", "tensor")),
            P(("dp", "tensor")),
            P(("dp", "tensor")),
            P(("dp", "tensor")),
            P("dp", None, "tensor"),
            P(None, "tensor", "dp"),
            P("tensor", "dp"),
            P(("dp", "tensor")),
            P("dp", "tensor"),
            P("tensor", "dp"),
            P("tensor", "dp"),
            P(("dp", "tensor")),
        ),
        check_vma=False,
    )
```

```python
import functools
import math

import jax
import jax.numpy as jnp
import numpy as np
from jax import lax
from jax.experimental import pallas as pl
from jax.experimental.pallas import tpu as pltpu
from jax.sharding import PartitionSpec as P

HEAD = 64
ROT = 16

EPSILON = 1e-05
NEGATIVE = -1e30
MESH = pl.DeviceIdType.MESH
F32 = jnp.float32
BF16 = jnp.bfloat16
NN = (((1,), (0,)), ((), ()))
NT = (((1,), (1,)), ((), ()))
TN = (((0,), (0,)), ((), ()))
VMEM_BYTES = 63 << 20


def dot(a, b, dims=NN):
    return lax.dot_general(a, b, dims, preferred_element_type=F32)


class Sizes:
    def __init__(self, n_dp, n_t, seq, rows, d, width, units):
        self.n_dp, self.n_t, self.seq, self.rows, self.d = n_dp, n_t, seq, rows, d
        self.width, self.units = width, units
        self.nz = n_dp // 4
        self.shard = d // n_dp
        self.nf = units // width
        self.chunks = 4 + 2 * self.nf
        self.block = min(256, rows)
        self.n_blocks = seq // self.block
        self.own_blocks = rows // self.block
        self.pairs = width // 128
        self.sums_width = max(d, 3 * width, units)
        self.p_slots = 2
        self.r_slots = 7
        self.ahead_y, self.ahead_z = 4, 3
        self.gather_z_last = ()
        self.reduce_y_last = ()


def fused_kernel(sz, *refs):
    (
        x_hbm, g_hbm, qkv_hbm, outw_hbm, up_hbm, down_hbm, small_in, seg_ref, cos_ref, sin_ref,
        out_hbm, igrad_hbm, dqkv_ref, doutw_ref, dupw_ref, ddown_ref, small_out, sums_ref,
        xa, ga, ha, hm, stat, wts, sm, vec_d, vec_q, vec_u, pool, dqk, dvc, dup, acc, bias,
        part, red_c, red_y, red_z1, red_z2, b_send, b_recv, h_send, h_recv, sums_in,
        local_sem, w_sem, sm_s, sm_r, row_s, row_r, gz_s, gz_r, gy_s, gy_r, gc_s, gc_r,
        rc_s, rc_r, ry_s, ry_r, rz_s, rz_r, xt_s, xt_r, su_s, su_r, credit,
    ) = refs
    nz, r, D, W, S, R, T = sz.nz, sz.shard, sz.d, sz.width, sz.seq, sz.rows, sz.n_t
    nf, NCH = sz.nf, sz.chunks
    dp = lax.axis_index("dp")
    t = lax.axis_index("tensor")
    z, y, c = lax.div(dp, 4), lax.rem(lax.div(dp, 2), 2), lax.rem(dp, 2)

    def dev(z_, y_, c_, t_):
        return ((z_ * 2 + y_) * 2 + c_, t_)

    hi, lo = lax.div(z, 2), lax.rem(z, 2)
    far, near = dev((1 - hi) * 2 + lo, y, c, t), dev(hi * 2 + 1 - lo, y, c, t)
    z_peer = [dev(lax.rem(z + k, nz), y, c, t) for k in range(1, nz)]
    y_peer = dev(z, 1 - y, c, t)
    c_peer = dev(z, y, 1 - c, t)
    t_peer = [dev(z, y, c, lax.rem(t + k, T)) for k in range(1, T)]

    def remote(src, dst, s_sem, r_sem, to):
        return pltpu.make_async_remote_copy(
            src_ref=src, dst_ref=dst, send_sem=s_sem, recv_sem=r_sem, device_id=to, device_id_type=MESH
        )

    own = pl.ds(pl.multiple_of(t * R, R), R)

    Q = W // 2

    def shard_copies():
        copies = []

        def copy(src, ch, first, width):
            dst = wts.at[ch, hi, lo, y, c, :, pl.ds(first, width)]
            copies.append(pltpu.make_async_copy(src, dst, w_sem.at[len(copies)]))

        for g in range(2):
            mine_cols = pl.ds(g * Q, Q)
            copy(qkv_hbm.at[0, :, mine_cols], 2 * g, 0, Q)
            copy(qkv_hbm.at[1, :, mine_cols], 2 * g, Q, Q)
            copy(qkv_hbm.at[2, :, mine_cols], 2 * g + 1, 0, Q)
            copy(outw_hbm.at[:, mine_cols], 2 * g + 1, Q, Q)
        for f in range(nf):
            copy(up_hbm.at[:, pl.ds(f * W, W)], 4 + 2 * f, 0, W)
            copy(down_hbm.at[:, pl.ds(f * W, W)], 5 + 2 * f, 0, W)
        return copies

    cp_w = shard_copies()
    cp_x = pltpu.make_async_copy(x_hbm, xa.at[own], local_sem.at[1])
    cp_g = pltpu.make_async_copy(g_hbm, ga.at[own], local_sem.at[2])
    for cp in cp_w:
        cp.start()
    cp_x.start()
    cp_g.start()
    sm[z, y, c, t] = small_in[...]
    barrier = pltpu.get_barrier_semaphore()
    everyone = z_peer + [y_peer, c_peer] + t_peer
    for peer in everyone:
        pl.semaphore_signal(barrier, inc=1, device_id=peer, device_id_type=MESH)
    for cp in cp_w:
        cp.wait()
    cp_x.wait()
    cp_g.wait()
    pl.semaphore_wait(barrier, len(everyone))

    sm_t = [remote(sm.at[z, y, c, t], sm.at[z, y, c, t], sm_s.at[k], sm_r.at[k], t_peer[k]) for k in range(T - 1)]
    for cp in sm_t:
        cp.start()

    def one_of(ch, names):
        if isinstance(ch, int):
            return ch in names
        return functools.reduce(jnp.logical_or, [ch == n for n in names])

    def by_kind(ch, z_first, y_first):
        if not sz.gather_z_last:
            return z_first()
        kind = one_of(ch, sz.gather_z_last)
        if isinstance(ch, int):
            (y_first if kind else z_first)()
        else:
            pl.when(kind)(y_first)
            pl.when(jnp.logical_not(kind))(z_first)

    def g_far(ch, which=0):
        at = wts.at[ch, hi, lo, (1 - y) if which else y, c]
        return remote(at, at, gz_s.at[ch, which], gz_r.at[ch, which], far)

    def g_near(ch, which=0):
        at = wts.at[ch, hi, lo, (1 - y) if which else y, c]
        return remote(at, at, gz_s.at[ch, 2 + which], gz_r.at[ch, 2 + which], near)

    def g_pass(ch):
        at = wts.at[ch, 1 - hi, lo, y, c]
        return remote(at, at, gz_s.at[ch, 4], gz_r.at[ch, 4], near)

    def g_pass_both(ch):
        at = wts.at[ch, 1 - hi, lo, :, c]
        return remote(at, at, gz_s.at[ch, 4], gz_r.at[ch, 4], near)

    def gy(ch, which):
        at = (wts.at[ch, hi, lo, y, c], wts.at[ch, 1 - hi, lo, y, c], wts.at[ch, :, 1 - lo, y, c])[which]
        return remote(at, at, gy_s.at[ch, which], gy_r.at[ch, which], y_peer)

    def gc(ch):
        return remote(wts.at[ch, :, :, :, c], wts.at[ch, :, :, :, c], gc_s.at[ch], gc_r.at[ch], c_peer)

    def start_z(ch):
        g_far(ch).start()
        g_near(ch).start()

    start_z(0)
    for ch in range(sz.ahead_y):
        gy(ch, 0).start()
    row_x = [remote(xa.at[own], xa.at[own], row_s.at[0, k], row_r.at[0, k], t_peer[k]) for k in range(T - 1)]
    row_g = [remote(ga.at[own], ga.at[own], row_s.at[1, k], row_r.at[1, k], t_peer[k]) for k in range(T - 1)]
    for cp in row_x:
        cp.start()
    sm_z = [remote(sm.at[z, y, c], sm.at[z, y, c], sm_s.at[T - 1 + k], sm_r.at[T - 1 + k], z_peer[k]) for k in range(nz - 1)]
    sm_y = remote(sm.at[:, y, c], sm.at[:, y, c], sm_s.at[T + nz - 2], sm_r.at[T + nz - 2], y_peer)
    sm_c = remote(sm.at[:, :, c], sm.at[:, :, c], sm_s.at[T + nz - 1], sm_r.at[T + nz - 1], c_peer)
    tile = 128

    def stat_rows(first, count):
        def body(i, carry):
            rows = pl.ds(pl.multiple_of(first + i * tile, tile), tile)
            v = xa[rows, :].astype(F32)
            mean = jnp.mean(v, axis=-1, keepdims=True)
            cen = v - mean
            inv = lax.rsqrt(jnp.mean(cen * cen, axis=-1, keepdims=True) + EPSILON)
            stat[0, rows, :] = jnp.broadcast_to(mean, (tile, 128))
            stat[1, rows, :] = jnp.broadcast_to(inv, (tile, 128))
            return carry

        lax.fori_loop(0, count // tile, body, 0)

    stat_rows(t * R, R)
    for cp in sm_t:
        cp.wait_recv()
    for cp in sm_z:
        cp.start()

    def when(condition, act):
        if isinstance(condition, bool):
            if condition:
                act()
        else:
            pl.when(condition)(act)

    def on_z(e):
        def z_first():
            g_far(e).wait_recv()
            g_pass(e).start()
            gy(e, 1).start()

        def y_first():
            gy(e, 0).wait_recv()
            g_far(e, 1).start()
            g_near(e, 1).start()

        by_kind(e, z_first, y_first)

    def on_y(e):
        def z_first():
            g_near(e).wait_recv()
            g_pass(e).wait_recv()
            gy(e, 2).start()

        def y_first():
            g_far(e).wait_recv()
            g_far(e, 1).wait_recv()
            g_pass_both(e).start()

        by_kind(e, z_first, y_first)
        when(e + sz.ahead_z < NCH, lambda: start_z(e + sz.ahead_z))
        when(e + sz.ahead_y < NCH, lambda: gy(e + sz.ahead_y, 0).start())

    def on_c(e):
        def z_first():
            for which in range(3):
                gy(e, which).wait_recv()

        def y_first():
            g_near(e).wait_recv()
            g_near(e, 1).wait_recv()
            g_pass_both(e).wait_recv()

        by_kind(e, z_first, y_first)
        gc(e).start()

    def weights(ch):
        return wts[ch].reshape(D, W)

    def weight_half(ch, side):
        return wts[ch, :, :, :, :, :, side * Q : (side + 1) * Q].reshape(D, Q)

    def weight_rows_half(ch, i, side):
        return wts[ch, i, :, :, :, :, side * Q : (side + 1) * Q].reshape(D // 2, Q)

    def weight_rows(ch, i):
        return wts[ch, i].reshape(D // 2, W)

    on_z(0)
    for ch in range(1, sz.ahead_z):
        start_z(ch)
    for cp in sm_z:
        cp.wait_recv()
    sm_y.start()
    on_y(0)
    on_z(1)
    sm_y.wait_recv()
    sm_c.start()
    on_y(1)
    on_z(2)
    sm_c.wait_recv()

    flat = sm[...].reshape(sz.n_dp * T * 16, 128)
    n_rows = sz.n_dp * T * 16
    pick = (
        jnp.bitwise_and(lax.broadcasted_iota(jnp.int32, (16, n_rows), 1), 15)
        == lax.broadcasted_iota(jnp.int32, (16, n_rows), 0)
    ).astype(F32).astype(BF16)

    def lay_out(width, n, mine_only):
        shift = n.bit_length() - 1
        lane_of = lax.broadcasted_iota(jnp.int32, (128, width), 1)
        spread = (jnp.bitwise_and(lane_of, n - 1) == lax.broadcasted_iota(jnp.int32, (128, width), 0)).astype(F32).astype(BF16)
        wide = dot(flat, spread)
        piece = jnp.right_shift(lax.broadcasted_iota(jnp.int32, (n_rows, width), 1), shift)
        owner = jnp.right_shift(lax.broadcasted_iota(jnp.int32, (n_rows, width), 0), 4)
        if mine_only:
            piece = piece * T + t
        return dot(pick, jnp.where(piece == owner, wide, 0.0).astype(BF16))

    vec_d[...] = lay_out(D, D // (sz.n_dp * T), False)
    vec_q[...] = lay_out(W, W // sz.n_dp, True)
    def norm_rows(first, count):
        def body(i, carry):
            rows = pl.ds(pl.multiple_of(first + i * tile, tile), tile)
            norm = (xa[rows, :].astype(F32) - stat[0, rows, 0:1]) * stat[1, rows, 0:1]
            ha[rows, :] = (norm * vec_d[0:1, :] + vec_d[1:2, :]).astype(BF16)
            hm[rows, :] = (norm * vec_d[2:3, :] + vec_d[3:4, :]).astype(BF16)
            return carry

        lax.fori_loop(0, count // tile, body, 0)

    lane = lax.broadcasted_iota(jnp.int32, (1, 128), 1)
    low_half = lane < HEAD
    from_right = jnp.bitwise_and(lane, HEAD - 1) < ROT // 2
    big = min(512, R)
    scale = 1.0 / math.sqrt(HEAD)

    def turned(u, rows, sign):
        other = jnp.where(from_right, pltpu.roll(u, 128 - ROT // 2, 1), pltpu.roll(u, ROT // 2, 1))
        turn = other * sin_ref[rows, :]
        return u * cos_ref[rows, :] + (turn if sign > 0 else -turn)

    def project_qk(g, first):
        def body(i, carry):
            rows = pl.ds(pl.multiple_of(first + i * big, big), big)
            u = dot(ha[rows, :], weights(2 * g))
            for k in range(W // 128):
                side, at = divmod(k * 128, Q)
                part_u = u[:, k * 128 : (k + 1) * 128] + vec_q[6 + side : 7 + side, g * Q + at : g * Q + at + 128]
                part_u = turned(part_u, rows, 1)
                pool[2 * g, rows, k * 128 : (k + 1) * 128] = (part_u * scale if side == 0 else part_u).astype(BF16)
            return carry

        lax.fori_loop(0, R // big, body, 0)

    def project_v(g, first):
        def body(i, carry):
            rows = pl.ds(pl.multiple_of(first + i * big, big), big)
            u = dot(ha[rows, :], weight_half(2 * g + 1, 0)) + vec_q[8:9, g * Q : (g + 1) * Q]
            pool[2 * g + 1, rows, :Q] = u.astype(BF16)
            return carry

        lax.fori_loop(0, R // big, body, 0)

    def d_context(g, first):
        def body(i, carry):
            rows = pl.ds(pl.multiple_of(first + i * big, big), big)
            pool[2 * g + 1, rows, Q:] = dot(ga[rows, :], weight_half(2 * g + 1, 1)).astype(BF16)
            return carry

        lax.fori_loop(0, R // big, body, 0)

    norm_rows(t * R, R)
    for f in range(nf):
        vec_u[f] = lay_out_units(sz, flat, pick, n_rows, t, f)
    on_c(0)
    on_y(2)
    on_z(3)
    gc(0).wait_recv()
    project_qk(0, t * R)
    for k in range(1, T):
        row_x[k - 1].wait_recv()
        row_g[k - 1].start()
        first = lax.rem(t + T - k, T) * R
        stat_rows(first, R)
        norm_rows(first, R)
        project_qk(0, first)
    on_c(1)
    on_y(3)
    on_z(4)
    gc(1).wait_recv()
    for k in range(T):
        project_v(0, k * R)
    d_context(0, t * R)

    acc[...] = jnp.zeros_like(acc)

    def rc(i):
        return remote(
            part.at[lax.rem(i, sz.p_slots), :, :, :, 1 - c], red_c.at[lax.rem(i, sz.r_slots)], rc_s.at[i], rc_r.at[i], c_peer
        )

    def r1(i):
        at = red_c.at[lax.rem(i, sz.r_slots)]
        src, to = (at.at[:, 1 - lo], near) if i in sz.reduce_y_last else (at.at[:, :, 1 - y], y_peer)
        return remote(src, red_y.at[i], ry_s.at[i], ry_r.at[i], to)

    def r2(i):
        src, to = (red_y.at[i, 1 - hi], far) if i in sz.reduce_y_last else (red_y.at[i, :, 1 - lo], near)
        return remote(src, red_z1.at[i], rz_s.at[i, 0], rz_r.at[i, 0], to)

    def r3(i):
        src, to = (red_y.at[i, hi, 1 - y], y_peer) if i in sz.reduce_y_last else (red_y.at[i, 1 - hi, lo], far)
        return remote(src, red_z2.at[i], rz_s.at[i, 1], rz_r.at[i, 1], to)

    def emit(i, left, right):
        slot = lax.rem(i, sz.p_slots)

        def body(n, carry):
            cols = pl.ds(pl.multiple_of(n * (D // 2), D // 2), D // 2)
            made = dot(left[:, cols], right[...], TN)
            part[slot, n] = made.astype(BF16).reshape(2, 2, 2, r, W)
            return carry

        lax.fori_loop(0, 2, body, 0)
        send(i)

    def emit_heads(i, g):
        slot = lax.rem(i, sz.p_slots)

        def body(n, carry):
            cols = pl.ds(pl.multiple_of(n * (D // 2), D // 2), D // 2)
            for side, left in enumerate((ha, ga)):
                right = dvc[g, :, side * Q : (side + 1) * Q]
                made = dot(left[:, cols], right, TN).astype(BF16).reshape(2, 2, 2, r, Q)
                part[slot, n, :, :, :, :, side * Q : (side + 1) * Q] = made
            return carry

        lax.fori_loop(0, 2, body, 0)
        send(i)

    def send(i):
        if i >= sz.r_slots:
            pl.semaphore_wait(credit, 1)
        rc(i).start()

    def event_c(i):
        rc(i).wait()
        slot, rslot = lax.rem(i, sz.p_slots), lax.rem(i, sz.r_slots)
        red_c[rslot] = (part[slot, :, :, :, c].astype(F32) + red_c[rslot].astype(F32)).astype(BF16)
        r1(i).start()

    def event_y(i):
        r1(i).wait()
        rslot = lax.rem(i, sz.r_slots)
        kept = red_c[rslot, :, lo] if i in sz.reduce_y_last else red_c[rslot, :, :, y]
        red_y[i] = (kept.astype(F32) + red_y[i].astype(F32)).astype(BF16)
        if i < NCH - sz.r_slots:
            pl.semaphore_signal(credit, inc=1, device_id=c_peer, device_id_type=MESH)
        r2(i).start()

    def event_n(i):
        r2(i).wait()
        if i in sz.reduce_y_last:
            red_y[i, hi] = (red_y[i, hi].astype(F32) + red_z1[i].astype(F32)).astype(BF16)
        else:
            red_y[i, :, lo] = (red_y[i, :, lo].astype(F32) + red_z1[i].astype(F32)).astype(BF16)
        r3(i).start()

    def event_z(i):
        r3(i).wait()
        kept = red_y[i, hi, y] if i in sz.reduce_y_last else red_y[i, hi, lo]
        total = kept.astype(F32) + red_z2[i].astype(F32)
        g = i // 2
        if i < 4 and i % 2 == 0:
            dqkv_ref[0, :, g * Q : (g + 1) * Q] = total[:, :Q]
            dqkv_ref[1, :, g * Q : (g + 1) * Q] = total[:, Q:]
        elif i < 4:
            dqkv_ref[2, :, g * Q : (g + 1) * Q] = total[:, :Q]
            doutw_ref[:, g * Q : (g + 1) * Q] = total[:, Q:]
        else:
            (dupw_ref, ddown_ref)[i % 2][:, (g - 2) * W : (g - 1) * W] = total

    sums_ref[...] = jnp.zeros_like(sums_ref)

    def row_sum(v):
        return jnp.sum(v.astype(F32), axis=0, keepdims=True)

    def mlp(first, count, f, act):
        def body(i, carry):
            rows = pl.ds(pl.multiple_of(first + i * big, big), big)
            u = dot(hm[rows, :], weights(4 + 2 * f)) + vec_u[f, 9:10, :]
            cdf = 0.5 + 0.5 * lax.erf(u * math.sqrt(0.5))
            act[rows, :] = (u * cdf).astype(BF16)
            slope = cdf + u * (jnp.exp(u * u * -0.5) * (1.0 / math.sqrt(2.0 * math.pi)))
            back = slope * dot(ga[rows, :], weights(5 + 2 * f))
            dup[f, rows, :] = back.astype(BF16)
            return carry

        lax.fori_loop(0, count // big, body, 0)

    def emit_units(i):
        f = (i - 4) // 2
        if i % 2:
            emit(i, ga, pool.at[f])
        else:
            emit(i, hm, dup.at[f])

    B = sz.block
    n_pairs = Q // 128
    steps = 2 * sz.n_blocks
    own_steps = 2 * sz.own_blocks

    def attend(qb, g, step):
        L = (qb + 1) * B
        rows = pl.ds(qb * B, B)
        for s in range(B // 128):
            here = pl.ds(s * 128, 128)
            start = jnp.broadcast_to(seg_ref[0:1, qb * B + s * 128 : qb * B + (s + 1) * 128].astype(F32), (128, 128)).T
            start = start[:, 0:1].astype(jnp.int32)
            key_at = lax.broadcasted_iota(jnp.int32, (128, L), 1)
            row_at = lax.broadcasted_iota(jnp.int32, (128, L), 0) + (qb * B + s * 128)
            bias[here, :L] = jnp.where((key_at >= start) & (key_at <= row_at), 0.0, NEGATIVE)

        def pair(p, carry):
            cols = pl.ds(pl.multiple_of(p * 128, 128), 128)
            cols_2 = pl.ds(pl.multiple_of(Q + p * 128, 128), 128)
            query, keys = pool[2 * g, rows, cols], pool[2 * g, :L, cols_2]
            values, d_ctx = pool[2 * g + 1, :L, cols], pool[2 * g + 1, rows, cols_2]
            made = []
            for h in range(2):
                mine = low_half if h == 0 else jnp.logical_not(low_half)
                q_h = jnp.where(mine, query, jnp.zeros_like(query))
                d_h = jnp.where(mine, d_ctx, jnp.zeros_like(d_ctx))
                scores = dot(q_h, keys, NT) + bias[:, :L]
                top = jnp.max(scores, axis=1, keepdims=True)
                e = jnp.exp(scores - top)
                prob = e * (1.0 / jnp.sum(e, axis=1, keepdims=True))
                d_prob = dot(d_h, values, NT)
                delta = jnp.sum(prob * d_prob, axis=1, keepdims=True)
                d_s = (prob * (d_prob - delta)).astype(BF16)
                p_b = prob.astype(BF16)
                made.append((dot(p_b, values), dot(d_s, keys), dot(d_s, q_h, TN), dot(p_b, d_h, TN)))
            dvc[g, rows, cols_2] = jnp.where(low_half, made[0][0], made[1][0]).astype(BF16)
            d_q = jnp.where(low_half, made[0][1], made[1][1]) * scale
            dqk[g, rows, cols] = turned(d_q, rows, -1).astype(BF16)
            cols_k = pl.ds(pl.multiple_of(g * Q + p * 128, 128), 128)
            cols_v = pl.ds(pl.multiple_of(W + g * Q + p * 128, 128), 128)
            acc[:L, cols_k] += made[0][2] + made[1][2]
            acc[:L, cols_v] += made[0][3] + made[1][3]
            at = step * n_pairs + p

            def poll():
                turn = lax.div(at, 2)
                e = 4 + turn + jnp.where(turn >= 2, 1, 0)
                on_z(e + 1)
                on_y(e)
                on_c(e - 2)

            pl.when((lax.rem(at, 2) == 0) & (at <= 10))(poll)
            pl.when(at == 12)(lambda: on_c(10))
            return carry

        lax.fori_loop(0, n_pairs, pair, 0)

    def finish_group(g):
        def body(i, carry):
            rows = pl.ds(pl.multiple_of(i * tile, tile), tile)
            for k in range(n_pairs):
                cols = pl.ds(g * Q + k * 128, 128)
                dqk[g, rows, pl.ds(Q + k * 128, 128)] = turned(acc[rows, cols], rows, -1).astype(BF16)
            dvc[g, rows, :Q] = acc[rows, pl.ds(W + g * Q, Q)].astype(BF16)
            return carry

        lax.fori_loop(0, S // tile, body, 0)
        emit(2 * g, ha, dqk.at[g])
        if g == 0:
            on_y(11)
            on_c(9)
        emit_heads(2 * g + 1, g)
        event_c(2 * g)
        sums_ref[5:6, g * Q : (g + 1) * Q] = row_sum(dqk[g, :, :Q])
        sums_ref[5:6, W + g * Q : W + (g + 1) * Q] = row_sum(dqk[g, :, Q:])
        sums_ref[5:6, 2 * W + g * Q : 2 * W + (g + 1) * Q] = row_sum(dvc[g, :, :Q])

    other_blocks = sz.n_blocks - sz.own_blocks

    def block_step(step, carry):
        def second_group():
            gc(2).wait_recv()
            gc(3).wait_recv()
            for k in range(T):
                project_qk(1, k * R)
            on_z(7)
            on_y(6)
            on_c(4)
            for k in range(T):
                project_v(1, k * R)
            d_context(1, t * R)

        def other_rows():
            for k in range(1, T):
                row_g[k - 1].wait_recv()
                for g in range(2):
                    d_context(g, lax.rem(t + T - k, T) * R)

        pl.when(step == sz.own_blocks)(second_group)
        pl.when(step == own_steps)(other_rows)
        pl.when(step == own_steps + other_blocks)(lambda: finish_group(0))
        later = step >= own_steps
        count = jnp.where(later, other_blocks, sz.own_blocks)
        at = jnp.where(later, step - own_steps, step)
        g = lax.div(at, count)
        j = lax.rem(at, count) + jnp.where(later, sz.own_blocks, 0)
        which = lax.rem(j + t * sz.own_blocks, sz.n_blocks)
        for qb in range(sz.n_blocks):
            pl.when(which == qb)(functools.partial(attend, qb, g, step))
        return carry

    lax.fori_loop(0, steps, block_step, 0)
    event_c(1)
    on_c(11)
    finish_group(1)

    half = D // 2

    def branch(first, i, n):
        rows = pl.ds(pl.multiple_of(first + i * big, big), big)
        total = dot(pool[0, rows, :], weight_rows(5, n), NT)
        for f in range(1, nf):
            total = total + dot(pool[f, rows, :], weight_rows(5 + 2 * f, n), NT)
        for g in range(2):
            total = total + dot(dvc[g, rows, Q:], weight_rows_half(2 * g + 1, n, 1), NT)
        return total

    def d_hidden(first, i, n):
        rows = pl.ds(pl.multiple_of(first + i * big, big), big)
        cols = pl.ds(pl.multiple_of(n * half, half), half)
        d_attn = dot(dqk[0, rows, :], weight_rows(0, n), NT) + dot(dqk[1, rows, :], weight_rows(2, n), NT)
        for g in range(2):
            d_attn = d_attn + dot(dvc[g, rows, :Q], weight_rows_half(2 * g + 1, n, 0), NT)
        d_mlp = dot(dup[0, rows, :], weight_rows(4, n), NT)
        for f in range(1, nf):
            d_mlp = d_mlp + dot(dup[f, rows, :], weight_rows(4 + 2 * f, n), NT)
        norm = (xa[rows, cols].astype(F32) - stat[0, rows, 0:1]) * stat[1, rows, 0:1]
        sums_ref[0:1, cols] += row_sum(d_attn * norm)
        sums_ref[1:2, cols] += row_sum(d_attn)
        sums_ref[2:3, cols] += row_sum(d_mlp * norm)
        sums_ref[3:4, cols] += row_sum(d_mlp)
        return d_attn * vec_d[0:1, cols] + d_mlp * vec_d[2:3, cols]

    def xt(which, k):
        src, dst = ((b_send, b_recv), (h_send, h_recv))[which]
        return remote(src.at[k], dst.at[k], xt_s.at[which, k], xt_r.at[which, k], t_peer[k])

    def events(i_y, i_n, i_z):
        if i_y is not None:
            event_y(i_y)
        if i_n is not None:
            event_n(i_n)
        if i_z is not None:
            event_z(i_z)

    for k in range(T - 1):
        first = lax.rem(t + k + 1, T) * R

        def other_units(f, carry, first=first, k=k):
            if k == 0:
                gc(4 + 2 * f).wait_recv()
                gc(5 + 2 * f).wait_recv()
            mlp(first, R, f, pool.at[f])
            return carry

        lax.fori_loop(0, nf, other_units, 0)
    event_c(3)
    event_y(0)
    for k in range(T - 1):
        first = lax.rem(t + k + 1, T) * R

        def both(q, carry, first=first, k=k):
            i, n = lax.div(q, 2), lax.rem(q, 2)
            cols = pl.ds(pl.multiple_of(n * half, half), half)
            rows = pl.ds(pl.multiple_of(i * big, big), big)
            b_send[k, rows, cols] = branch(first, i, n).astype(BF16)
            return carry

        lax.fori_loop(0, 2 * (R // big), both, 0)
        xt(0, k).start()
    event_y(1)
    mlp(t * R, R, 0, pool.at[0])
    emit_units(4)
    event_n(0)
    emit_units(5)
    event_c(4)
    event_y(2)
    for k in range(T - 1):
        first = lax.rem(t + k + 1, T) * R

        def both_back(q, carry, first=first, k=k):
            i, n = lax.div(q, 2), lax.rem(q, 2)
            cols = pl.ds(pl.multiple_of(n * half, half), half)
            rows = pl.ds(pl.multiple_of(i * big, big), big)
            h_send[k, rows, cols] = d_hidden(first, i, n).astype(BF16)
            return carry

        lax.fori_loop(0, 2 * (R // big), both_back, 0)
        xt(1, k).start()
    event_c(5)
    events(3, 1, 0)
    mlp(t * R, R, 1, pool.at[1])
    emit_units(6)
    event_n(2)
    emit_units(7)
    event_c(6)
    events(4, None, 1)
    mlp(t * R, R, 2, pool.at[2])
    event_c(7)
    mlp(t * R, R, 3, pool.at[3])
    events(5, 3, 2)

    def own_back(q, carry):
        i, n = lax.div(q, 2), lax.rem(q, 2)
        cols = pl.ds(pl.multiple_of(n * half, half), half)
        acc[pl.ds(pl.multiple_of(R + i * big, big), big), cols] = d_hidden(t * R, i, n)
        return carry

    lax.fori_loop(0, 2 * (R // big), own_back, 0)
    sums_ref[4:5, :D] = row_sum(ga[own, :])
    for f in range(nf):
        sums_ref[6:7, f * W : (f + 1) * W] = row_sum(dup[f])

    su_c = remote(sums_ref, sums_in.at[0], su_s.at[0], su_r.at[0], c_peer)
    su_y = remote(sums_ref, sums_in.at[1], su_s.at[1], su_r.at[1], y_peer)
    su_n = remote(sums_ref, sums_in.at[2], su_s.at[2], su_r.at[2], near)
    su_f = remote(sums_ref, sums_in.at[3], su_s.at[3], su_r.at[3], far)
    su_t = [remote(sums_ref, sums_in.at[4 + k], su_s.at[4 + k], su_r.at[4 + k], t_peer[k]) for k in range(T - 1)]
    stages = (su_c, su_y, su_n, su_f)

    def sums_step(n):
        if n < 4:
            stages[n].wait()
            sums_ref[...] += sums_in[n]
        if n < 3:
            stages[n + 1].start()
        elif n == 3:
            for cp in su_t:
                cp.start()
        else:
            for cp in su_t:
                cp.wait()
            for k in range(T - 1):
                sums_ref[0:5, :] += sums_in[4 + k, 0:5, :]

    def mine(row, first, width, n, at):
        part_row = jnp.broadcast_to(sums_ref[row : row + 1, first : first + width], (8, width))
        return pltpu.roll(part_row, lax.rem(width - at, width), 1)[0:1, 0:128]

    def finish_out(i, carry):
        rows = pl.ds(pl.multiple_of(i * tile, tile), tile)
        here = pl.ds(pl.multiple_of(t * R + i * tile, tile), tile)
        total = xa[here, :].astype(F32) + acc[rows, :] + (vec_d[4:5, :] + vec_d[5:6, :])
        for k in range(T - 1):
            total = total + b_recv[k, rows, :].astype(F32)
        b_send[0, rows, :] = total.astype(BF16)
        return carry

    def finish_grad(i, carry):
        rows = pl.ds(pl.multiple_of(R + i * tile, tile), tile)
        there = pl.ds(pl.multiple_of(i * tile, tile), tile)
        here = pl.ds(pl.multiple_of(t * R + i * tile, tile), tile)
        inv = stat[1, here, 0:1]
        norm = (xa[here, :].astype(F32) - stat[0, here, 0:1]) * inv
        d_hat = acc[rows, :]
        for k in range(T - 1):
            d_hat = d_hat + h_recv[k, there, :].astype(F32)
        inner = jnp.mean(d_hat * norm, axis=-1, keepdims=True)
        acc[rows, :] = ga[here, :].astype(F32) + inv * (d_hat - jnp.mean(d_hat, axis=-1, keepdims=True) - norm * inner)
        return carry

    su_c.start()
    event_n(4)
    emit_units(8)
    sums_step(0)
    emit_units(9)
    event_c(8)
    event_y(6)
    emit_units(10)
    event_c(9)
    events(None, 5, 3)
    emit_units(11)
    event_c(10)
    events(7, None, 4)
    event_c(11)

    def own_both(q, carry):
        i, n = lax.div(q, 2), lax.rem(q, 2)
        cols = pl.ds(pl.multiple_of(n * half, half), half)
        acc[pl.ds(pl.multiple_of(i * big, big), big), cols] = branch(t * R, i, n)
        return carry

    lax.fori_loop(0, 2 * (R // big), own_both, 0)
    events(8, 6, 5)
    sums_step(1)
    event_n(7)

    for k in range(T - 1):
        xt(0, k).wait()
    lax.fori_loop(0, R // tile, finish_out, 0)
    cp_out = pltpu.make_async_copy(b_send.at[0], out_hbm, local_sem.at[3])
    cp_out.start()
    event_y(9)
    sums_step(2)
    events(10, 8, 6)
    event_z(7)
    sums_step(3)
    events(11, 9, 8)
    for k in range(T - 1):
        xt(1, k).wait()
    lax.fori_loop(0, R // tile, finish_grad, 0)
    cp_grad = pltpu.make_async_copy(acc.at[pl.ds(R, R)], igrad_hbm, local_sem.at[4])
    cp_grad.start()
    event_n(10)
    sums_step(4)
    event_z(9)
    event_n(11)
    n_d, n_q, n_u = D // (sz.n_dp * T), W // sz.n_dp, sz.units // sz.n_dp
    small_out[...] = jnp.zeros_like(small_out)
    for k in range(5):
        small_out[k : k + 1, :] = mine(k, 0, D, n_d, (dp * T + t) * n_d)
    for j in range(3):
        small_out[5 + j : 6 + j, :] = mine(5, j * W, W, n_q, dp * n_q)
    small_out[8:9, :] = mine(6, 0, sz.units, n_u, dp * n_u)
    event_z(10)
    event_z(11)

    for cp in sm_t + sm_z + [sm_y, sm_c] + row_x + row_g:
        cp.wait_send()

    def sent(ch, carry):
        for copy in (g_far(ch), gy(ch, 0), g_near(ch), gc(ch)):
            copy.wait_send()

        def z_first():
            for copy in (g_pass(ch), gy(ch, 1), gy(ch, 2)):
                copy.wait_send()

        def y_first():
            for copy in (g_far(ch, 1), g_near(ch, 1), g_pass_both(ch)):
                copy.wait_send()

        by_kind(ch, z_first, y_first)
        return carry

    lax.fori_loop(0, NCH, sent, 0)
    cp_out.wait()
    cp_grad.wait()


def lay_out_units(sz, flat, pick, n_rows, t, f):
    n = sz.units // sz.n_dp
    shift = n.bit_length() - 1
    W = sz.width
    lane_of = lax.broadcasted_iota(jnp.int32, (128, W), 1) + f * W
    spread = (jnp.bitwise_and(lane_of, n - 1) == lax.broadcasted_iota(jnp.int32, (128, W), 0)).astype(F32).astype(BF16)
    wide = dot(flat, spread)
    piece = jnp.right_shift(lax.broadcasted_iota(jnp.int32, (n_rows, W), 1) + f * W, shift) * sz.n_t + t
    owner = jnp.right_shift(lax.broadcasted_iota(jnp.int32, (n_rows, W), 0), 4)
    return dot(pick, jnp.where(piece == owner, wide, 0.0).astype(BF16))


def fused(sz, args):
    (
        inputs, segment_ids, ln_attn_gain, ln_attn_bias, ln_mlp_gain, ln_mlp_bias, qkv_weight, qkv_bias,
        out_weight, out_bias, up_weight, up_bias, down_weight, down_bias, cotangent,
    ) = args
    nz, r, D, W, S, R, T, nf, NCH = sz.nz, sz.shard, sz.d, sz.width, sz.seq, sz.rows, sz.n_t, sz.nf, sz.chunks

    def placed(v, first):
        return jnp.pad(v, ((first, 16 - first - v.shape[0]), (0, 128 - v.shape[1])))

    vectors = (ln_attn_gain, ln_attn_bias, ln_mlp_gain, ln_mlp_bias, out_bias, down_bias)
    small = placed(qkv_bias[:, 0], 6) + placed(up_bias, 9)
    for k, v in enumerate(vectors):
        small = small + placed(v[None], k)
    half_rot = ROT // 2
    place = np.arange(S, dtype=np.float32)
    inverse = (10000.0 ** (-(2.0 * np.arange(half_rot, dtype=np.float32)) / ROT)).astype(np.float32)
    theta = place[:, None] * inverse[None, :]
    cos, sin = np.cos(theta), np.sin(theta)
    cos_head = np.concatenate([cos, cos, np.ones((S, HEAD - ROT), np.float32)], axis=1)
    sin_head = np.concatenate([-sin, sin, np.zeros((S, HEAD - ROT), np.float32)], axis=1)
    cos_table = jnp.asarray(np.tile(cos_head, (1, 128 // HEAD)), F32)
    sin_table = jnp.asarray(np.tile(sin_head, (1, 128 // HEAD)), F32)

    hbm = pl.BlockSpec(memory_space=pl.ANY)
    vmem = pl.BlockSpec(memory_space=pltpu.VMEM)
    sw = sz.sums_width
    dma = pltpu.SemaphoreType.DMA
    n_small = T - 1 + nz - 1 + 2
    scratch = [
        pltpu.VMEM((S, D), BF16),
        pltpu.VMEM((S, D), BF16),
        pltpu.VMEM((S, D), BF16),
        pltpu.VMEM((S, D), BF16),
        pltpu.VMEM((2, S, 128), F32),
        pltpu.VMEM((NCH, 2, 2, 2, 2, r, W), BF16),
        pltpu.VMEM((nz, 2, 2, T, 16, 128), BF16),
        pltpu.VMEM((16, D), F32),
        pltpu.VMEM((16, W), F32),
        pltpu.VMEM((nf, 16, W), F32),
        pltpu.VMEM((max(4, nf), S, W), BF16),
        pltpu.VMEM((2, S, W), BF16),
        pltpu.VMEM((2, S, W), BF16),
        pltpu.VMEM((nf, S, W), BF16),
        pltpu.VMEM((S, D), F32),
        pltpu.VMEM((sz.block, S), F32),
        pltpu.VMEM((sz.p_slots, 2, 2, 2, 2, r, W), BF16),
        pltpu.VMEM((sz.r_slots, 2, 2, 2, r, W), BF16),
        pltpu.VMEM((NCH, 2, 2, r, W), BF16),
        pltpu.VMEM((NCH, 2, r, W), BF16),
        pltpu.VMEM((NCH, r, W), BF16),
        pltpu.VMEM((T - 1, R, D), BF16),
        pltpu.VMEM((T - 1, R, D), BF16),
        pltpu.VMEM((T - 1, R, D), BF16),
        pltpu.VMEM((T - 1, R, D), BF16),
        pltpu.VMEM((3 + T, 8, sw), F32),
        dma((5,)), dma((8 + 2 * nf,)),
        dma((n_small,)), dma((n_small,)),
        dma((2, T - 1)), dma((2, T - 1)),
        dma((NCH, 5)), dma((NCH, 5)),
        dma((NCH, 3)), dma((NCH, 3)),
        dma((NCH,)), dma((NCH,)),
        dma((NCH,)), dma((NCH,)),
        dma((NCH,)), dma((NCH,)),
        dma((NCH, nz - 1)), dma((NCH, nz - 1)),
        dma((2, T - 1)), dma((2, T - 1)),
        dma((3 + T,)), dma((3 + T,)),
        pltpu.SemaphoreType.REGULAR,
    ]
    units = sz.units
    output, input_grad, d_qkv, d_out, d_up, d_down, small_sums, _ = pl.pallas_call(
        functools.partial(fused_kernel, sz),
        out_shape=(
            jax.ShapeDtypeStruct((R, D), BF16),
            jax.ShapeDtypeStruct((R, D), F32),
            jax.ShapeDtypeStruct((3, r, W), F32),
            jax.ShapeDtypeStruct((r, W), F32),
            jax.ShapeDtypeStruct((r, units), F32),
            jax.ShapeDtypeStruct((r, units), F32),
            jax.ShapeDtypeStruct((16, 128), F32),
            jax.ShapeDtypeStruct((8, sw), F32),
        ),
        in_specs=[hbm, hbm, hbm, hbm, hbm, hbm, vmem, vmem, vmem, vmem],
        out_specs=(hbm, hbm, vmem, vmem, vmem, vmem, vmem, vmem),
        scratch_shapes=scratch,
        compiler_params=pltpu.CompilerParams(collective_id=0, has_side_effects=True, vmem_limit_bytes=VMEM_BYTES),
    )(
        inputs, cotangent, qkv_weight.transpose(1, 0, 2), out_weight.T, up_weight, down_weight.T, small,
        segment_ids.reshape(1, S), cos_table, sin_table,
    )

    n, nq, nu = D // (sz.n_dp * T), W // sz.n_dp, units // sz.n_dp
    return (
        output, input_grad, small_sums[0, :n], small_sums[1, :n], small_sums[2, :n], small_sums[3, :n],
        d_qkv.transpose(1, 0, 2), small_sums[5:8, :nq].reshape(3, 1, nq), d_out.T, small_sums[4, :n],
        d_up, small_sums[8:9, :nu], d_down.T, small_sums[4, :n],
    )


def rotated(values, cosine, sine, sign):
    half_rot = ROT // 2
    first_half = values[..., :half_rot]
    second_half = values[..., half_rot:ROT]
    new_first = first_half * cosine - sign * second_half * sine
    new_second = second_half * cosine + sign * first_half * sine
    return jnp.concatenate([new_first, new_second, values[..., ROT:]], axis=-1)


def angle_tables(length):
    position = jnp.arange(length).astype(jnp.float32)
    inverse = 10000.0 ** (-(2.0 * jnp.arange(ROT // 2).astype(jnp.float32)) / ROT)
    theta = position[:, None] * inverse[None, :]
    return (jnp.cos(theta)[:, None, :], jnp.sin(theta)[:, None, :])


def gelu_exact(value):
    return jax.nn.gelu(value, approximate=False)


def layer_norm(rows):
    centred = rows - jnp.mean(rows, axis=-1, keepdims=True)
    inv_std = lax.rsqrt(jnp.mean(centred * centred, axis=-1, keepdims=True) + EPSILON)
    return (centred * inv_std, inv_std)


def plain(
    inputs,
    segment_ids,
    ln_attn_gain,
    ln_attn_bias,
    ln_mlp_gain,
    ln_mlp_bias,
    qkv_weight,
    qkv_bias,
    out_weight,
    out_bias,
    up_weight,
    up_bias,
    down_weight,
    down_bias,
    cotangent,
):
    seq_len = segment_ids.shape[0]
    norm_terms = (
        lax.all_gather(ln_attn_gain, ("dp", "tensor"), axis=0, tiled=True),
        lax.all_gather(ln_attn_bias, ("dp", "tensor"), axis=0, tiled=True),
        lax.all_gather(ln_mlp_gain, ("dp", "tensor"), axis=0, tiled=True),
        lax.all_gather(ln_mlp_bias, ("dp", "tensor"), axis=0, tiled=True),
        lax.all_gather(out_bias, ("dp", "tensor"), axis=0, tiled=True),
        lax.all_gather(down_bias, ("dp", "tensor"), axis=0, tiled=True),
    )
    gain_attn = norm_terms[0].astype(jnp.float32)
    shift_attn = norm_terms[1].astype(jnp.float32)
    gain_mlp = norm_terms[2].astype(jnp.float32)
    shift_mlp = norm_terms[3].astype(jnp.float32)
    bias_sum = norm_terms[4].astype(jnp.float32) + norm_terms[5].astype(jnp.float32)
    w_qkv, b_qkv, w_out, w_up, b_up, w_down = (
        lax.all_gather(qkv_weight, "dp", axis=0, tiled=True),
        lax.all_gather(qkv_bias, "dp", axis=2, tiled=True),
        lax.all_gather(out_weight, "dp", axis=1, tiled=True),
        lax.all_gather(up_weight, "dp", axis=0, tiled=True),
        lax.all_gather(up_bias, "dp", axis=1, tiled=True),
        lax.all_gather(down_weight, "dp", axis=1, tiled=True),
    )
    local_width = w_qkv.shape[2]
    heads_here = local_width // HEAD
    score_scale = 1.0 / math.sqrt(HEAD)
    resid = inputs.astype(jnp.float32)
    normalized, inv_std = layer_norm(resid)
    whole_inputs = lax.all_gather(inputs, "tensor", axis=0, tiled=True)
    normal_all, unused_std = layer_norm(whole_inputs.astype(jnp.float32))
    attn_rows = (normal_all * gain_attn + shift_attn).astype(jnp.bfloat16)
    mlp_rows = (normal_all * gain_mlp + shift_mlp).astype(jnp.bfloat16)
    proj = jnp.einsum("sd,dje->sje", attn_rows, w_qkv, preferred_element_type=jnp.float32)
    proj = proj + b_qkv.astype(jnp.float32).reshape(1, 3, local_width)
    cosine, sine = angle_tables(seq_len)
    query = rotated(proj[:, 0].reshape(seq_len, heads_here, HEAD), cosine, sine, 1.0).astype(
        jnp.bfloat16
    )
    keys = rotated(proj[:, 1].reshape(seq_len, heads_here, HEAD), cosine, sine, 1.0).astype(
        jnp.bfloat16
    )
    values = proj[:, 2].reshape(seq_len, heads_here, HEAD).astype(jnp.bfloat16)
    block_rows = min(512, seq_len)
    block_count = seq_len // block_rows
    places = jnp.arange(seq_len)
    query_blocks = query.reshape(block_count, block_rows, heads_here, HEAD)
    segment_blocks = segment_ids.reshape(block_count, block_rows)
    place_blocks = places.reshape(block_count, block_rows)

    def masked_scores(query_part, segment_part, place_part):
        scores = (
            jnp.einsum("qhe,khe->hqk", query_part, keys, preferred_element_type=jnp.float32)
            * score_scale
        )
        allowed = (segment_part[:, None] == segment_ids[None, :]) & (
            place_part[:, None] >= places[None, :]
        )
        return jnp.where(allowed[None], scores, NEGATIVE)

    def forward_block(block_item):
        query_part, segment_part, place_part = block_item
        scores = masked_scores(query_part, segment_part, place_part)
        row_max = jnp.max(scores, axis=-1, keepdims=True)
        exponent = jnp.exp(scores - row_max)
        row_total = jnp.sum(exponent, axis=-1, keepdims=True)
        probability = (exponent / row_total).astype(jnp.bfloat16)
        context_part = jnp.einsum(
            "hqk,khe->qhe", probability, values, preferred_element_type=jnp.float32
        )
        return (context_part, (row_max + jnp.log(row_total))[..., 0])

    context_blocks, log_totals = lax.map(
        forward_block, (query_blocks, segment_blocks, place_blocks)
    )
    context = context_blocks.reshape(seq_len, local_width).astype(jnp.bfloat16)
    up_in = jnp.dot(mlp_rows, w_up, preferred_element_type=jnp.float32) + b_up.astype(jnp.float32)
    activated = gelu_exact(up_in).astype(jnp.bfloat16)
    context_part = context
    branch_sum = lax.psum_scatter(
        jnp.dot(context_part, w_out, preferred_element_type=jnp.float32)
        + jnp.dot(activated, w_down, preferred_element_type=jnp.float32),
        "tensor",
        scatter_dimension=0,
        tiled=True,
    )
    output = (resid + branch_sum + bias_sum).astype(jnp.bfloat16)
    grad_all = lax.all_gather(cotangent, "tensor", axis=0, tiled=True)
    d_active = jnp.einsum("sd,fd->sf", grad_all, w_down, preferred_element_type=jnp.float32)
    gelu_value, gelu_back = jax.vjp(gelu_exact, up_in)
    d_up = gelu_back(d_active)[0].astype(jnp.bfloat16)
    d_w_down = jnp.einsum("sf,sd->fd", activated, grad_all, preferred_element_type=jnp.float32)
    d_w_up = jnp.einsum("sd,sf->df", mlp_rows, d_up, preferred_element_type=jnp.float32)
    d_b_up = jnp.sum(d_up, axis=0, dtype=jnp.float32).reshape(1, -1)
    unit_sums = (d_w_up, d_b_up, d_w_down)
    d_context = jnp.einsum("sd,cd->sc", grad_all, w_out, preferred_element_type=jnp.float32).astype(
        jnp.bfloat16
    )
    d_w_out = jnp.einsum("sc,sd->cd", context, grad_all, preferred_element_type=jnp.float32)
    d_context_blocks = d_context.reshape(block_count, block_rows, heads_here, HEAD)

    def backward_block(carry, block_item):
        d_keys, d_values = carry
        query_part, d_context_part, segment_part, place_part, log_part = block_item
        scores = masked_scores(query_part, segment_part, place_part)
        probability = jnp.exp(scores - log_part[..., None])
        d_prob = jnp.einsum(
            "qhe,khe->hqk", d_context_part, values, preferred_element_type=jnp.float32
        )
        row_delta = jnp.sum(probability * d_prob, axis=-1, keepdims=True)
        d_scores = (probability * (d_prob - row_delta)).astype(jnp.bfloat16)
        d_query_part = (
            jnp.einsum("hqk,khe->qhe", d_scores, keys, preferred_element_type=jnp.float32)
            * score_scale
        )
        d_keys = (
            d_keys
            + jnp.einsum("hqk,qhe->khe", d_scores, query_part, preferred_element_type=jnp.float32)
            * score_scale
        )
        d_values = d_values + jnp.einsum(
            "hqk,qhe->khe",
            probability.astype(jnp.bfloat16),
            d_context_part,
            preferred_element_type=jnp.float32,
        )
        return ((d_keys, d_values), d_query_part)

    zero_rows = jnp.zeros((seq_len, heads_here, HEAD), jnp.float32)
    (d_keys, d_values), d_query_blocks = lax.scan(
        backward_block,
        (zero_rows, zero_rows),
        (query_blocks, d_context_blocks, segment_blocks, place_blocks, log_totals),
    )
    d_query = d_query_blocks.reshape(seq_len, heads_here, HEAD)
    d_proj = jnp.stack(
        [
            rotated(d_query, cosine, sine, -1.0).reshape(seq_len, local_width),
            rotated(d_keys, cosine, sine, -1.0).reshape(seq_len, local_width),
            d_values.reshape(seq_len, local_width),
        ],
        axis=1,
    ).astype(jnp.bfloat16)
    d_w_qkv = jnp.einsum("sd,sje->dje", attn_rows, d_proj, preferred_element_type=jnp.float32)
    d_b_qkv = jnp.sum(d_proj, axis=0, dtype=jnp.float32).reshape(3, 1, local_width)
    grad_rows = cotangent.astype(jnp.float32)
    attn_term = jnp.einsum("sje,dje->sd", d_proj, w_qkv, preferred_element_type=jnp.float32)
    mlp_term = jnp.einsum("sf,df->sd", d_up, w_up, preferred_element_type=jnp.float32)
    stacked = lax.psum_scatter(
        jnp.stack([attn_term, mlp_term], axis=1), "tensor", scatter_dimension=0, tiled=True
    )
    d_attn_norm = stacked[:, 0]
    d_mlp_norm = stacked[:, 1]
    d_hat = d_attn_norm * gain_attn + d_mlp_norm * gain_mlp
    norm_sums = (
        jnp.sum(d_attn_norm * normalized, axis=0),
        jnp.sum(d_attn_norm, axis=0),
        jnp.sum(d_mlp_norm * normalized, axis=0),
        jnp.sum(d_mlp_norm, axis=0),
    )
    input_grad = grad_rows + inv_std * (
        d_hat
        - jnp.mean(d_hat, axis=-1, keepdims=True)
        - normalized * jnp.mean(d_hat * normalized, axis=-1, keepdims=True)
    )
    small_sums = (
        lax.psum_scatter(norm_sums[0], ("dp", "tensor"), scatter_dimension=0, tiled=True),
        lax.psum_scatter(norm_sums[1], ("dp", "tensor"), scatter_dimension=0, tiled=True),
        lax.psum_scatter(norm_sums[2], ("dp", "tensor"), scatter_dimension=0, tiled=True),
        lax.psum_scatter(norm_sums[3], ("dp", "tensor"), scatter_dimension=0, tiled=True),
        lax.psum_scatter(
            jnp.sum(grad_rows, axis=0), ("dp", "tensor"), scatter_dimension=0, tiled=True
        ),
    )
    summed = (
        lax.psum_scatter(d_w_qkv, "dp", scatter_dimension=0, tiled=True),
        lax.psum_scatter(d_b_qkv, "dp", scatter_dimension=2, tiled=True),
        lax.psum_scatter(d_w_out, "dp", scatter_dimension=1, tiled=True),
        lax.psum_scatter(unit_sums[0], "dp", scatter_dimension=0, tiled=True),
        lax.psum_scatter(unit_sums[1], "dp", scatter_dimension=1, tiled=True),
        lax.psum_scatter(unit_sums[2], "dp", scatter_dimension=1, tiled=True),
    )
    return (
        output,
        input_grad,
        small_sums[0],
        small_sums[1],
        small_sums[2],
        small_sums[3],
        summed[0],
        summed[1],
        summed[2],
        small_sums[4],
        summed[3],
        summed[4],
        summed[5],
        small_sums[4],
    )


def fits(n_dp, n_t, seq, rows, d, width, units):
    if n_dp != 16 or n_t < 2 or width != 512 or units != 2048 or width % 128 or units % width or rows % 128 or seq != rows * n_t:
        return False
    small = (d // (n_dp * n_t), width // n_dp, units // n_dp)
    if any(n < 1 or n > 128 or n & (n - 1) for n in small) or (d // n_dp) % 16:
        return False
    rows_of = 2 * (4 * seq * d + seq * (max(4, units // width) * width + 4 * width + units)) + 4 * seq * d
    chunks = 4 + 2 * (units // width)
    weights_of = 2 * chunks * d * width
    reduction = 2 * d * width * (2 + 2) + weights_of * 7 // 16 + 4 * chunks * (d // n_dp) * width
    exchange = 8 * (n_t - 1) * rows * d
    return rows_of + weights_of + reduction + exchange <= 54 << 20


def local(n_dp, n_t, *args):
    rows, d = args[0].shape
    seq, width, units = args[1].shape[0], args[6].shape[2], args[10].shape[1]
    if fits(n_dp, n_t, seq, rows, d, width, units):
        return fused(Sizes(n_dp, n_t, seq, rows, d, width, units), args)
    return plain(*args)


def solution(mesh):
    return jax.shard_map(
        functools.partial(local, mesh.shape["dp"], mesh.shape["tensor"]),
        mesh=mesh,
        in_specs=(
            P(("dp", "tensor"), None),
            P("dp"),
            P(("dp", "tensor")),
            P(("dp", "tensor")),
            P(("dp", "tensor")),
            P(("dp", "tensor")),
            P("dp", None, "tensor"),
            P(None, "tensor", "dp"),
            P("tensor", "dp"),
            P(("dp", "tensor")),
            P("dp", "tensor"),
            P("tensor", "dp"),
            P("tensor", "dp"),
            P(("dp", "tensor")),
            P(("dp", "tensor"), None),
        ),
        out_specs=(
            P(("dp", "tensor"), None),
            P(("dp", "tensor"), None),
            P(("dp", "tensor")),
            P(("dp", "tensor")),
            P(("dp", "tensor")),
            P(("dp", "tensor")),
            P("dp", None, "tensor"),
            P(None, "tensor", "dp"),
            P("tensor", "dp"),
            P(("dp", "tensor")),
            P("dp", "tensor"),
            P("tensor", "dp"),
            P("tensor", "dp"),
            P(("dp", "tensor")),
        ),
        check_vma=False,
    )
```

```python
import functools
import math

import jax
import jax.numpy as jnp
import numpy as np
from jax import lax
from jax.experimental import pallas as pl
from jax.experimental.pallas import tpu as pltpu
from jax.sharding import PartitionSpec as P

HEAD = 64
ROT = 16

EPSILON = 1e-05
NEGATIVE = -1e30
MESH = pl.DeviceIdType.MESH
F32 = jnp.float32
BF16 = jnp.bfloat16
NN = (((1,), (0,)), ((), ()))
NT = (((1,), (1,)), ((), ()))
TN = (((0,), (0,)), ((), ()))
VMEM_BYTES = 63 << 20


def dot(a, b, dims=NN):
    return lax.dot_general(a, b, dims, preferred_element_type=F32)


class Sizes:
    def __init__(self, n_dp, n_t, seq, rows, d, width, units):
        self.n_dp, self.n_t, self.seq, self.rows, self.d = n_dp, n_t, seq, rows, d
        self.width, self.units = width, units
        self.nz = n_dp // 4
        self.shard = d // n_dp
        self.nf = units // width
        self.chunks = 4 + 2 * self.nf
        self.block = min(256, rows)
        self.n_blocks = seq // self.block
        self.own_blocks = rows // self.block
        self.pairs = width // 128
        self.sums_width = max(d, 3 * width, units)
        self.p_slots = 2
        self.r_slots = 7
        self.ahead_y, self.ahead_z = 5, 3
        self.gather_z_last = ()
        self.reduce_y_last = ()


def fused_kernel(sz, *refs):
    (
        x_hbm, g_hbm, qkv_hbm, outw_hbm, up_hbm, down_hbm, small_in, seg_ref, cos_ref, sin_ref,
        out_hbm, igrad_hbm, dqkv_ref, doutw_ref, dupw_ref, ddown_ref, small_out,
        xa, ga, ha, hm, stat, wts, sm, vec_d, vec_q, vec_u, pool, dqk, dvc, dup, acc, bias,
        part, red_c, red_y, red_z1, red_z2, b_send, b_recv, h_send, h_recv, sums_ref, sums_in,
        local_sem, w_sem, sm_s, sm_r, row_s, row_r, gz_s, gz_r, gy_s, gy_r, gc_s, gc_r,
        rc_s, rc_r, ry_s, ry_r, rz_s, rz_r, xt_s, xt_r, su_s, su_r, credit,
    ) = refs
    nz, r, D, W, S, R, T = sz.nz, sz.shard, sz.d, sz.width, sz.seq, sz.rows, sz.n_t
    nf, NCH = sz.nf, sz.chunks
    dp = lax.axis_index("dp")
    t = lax.axis_index("tensor")
    z, y, c = lax.div(dp, 4), lax.rem(lax.div(dp, 2), 2), lax.rem(dp, 2)

    def dev(z_, y_, c_, t_):
        return ((z_ * 2 + y_) * 2 + c_, t_)

    hi, lo = lax.div(z, 2), lax.rem(z, 2)
    far, near = dev((1 - hi) * 2 + lo, y, c, t), dev(hi * 2 + 1 - lo, y, c, t)
    z_peer = [dev(lax.rem(z + k, nz), y, c, t) for k in range(1, nz)]
    y_peer = dev(z, 1 - y, c, t)
    c_peer = dev(z, y, 1 - c, t)
    t_peer = [dev(z, y, c, lax.rem(t + k, T)) for k in range(1, T)]

    def remote(src, dst, s_sem, r_sem, to):
        return pltpu.make_async_remote_copy(
            src_ref=src, dst_ref=dst, send_sem=s_sem, recv_sem=r_sem, device_id=to, device_id_type=MESH
        )

    own = pl.ds(pl.multiple_of(t * R, R), R)

    Q = W // 2

    def shard_copies():
        copies = []

        def copy(src, ch, first, width):
            dst = wts.at[ch, hi, lo, y, c, :, pl.ds(first, width)]
            copies.append(pltpu.make_async_copy(src, dst, w_sem.at[len(copies)]))

        for g in range(2):
            mine_cols = pl.ds(g * Q, Q)
            copy(qkv_hbm.at[0, :, mine_cols], 2 * g, 0, Q)
            copy(qkv_hbm.at[1, :, mine_cols], 2 * g, Q, Q)
            copy(qkv_hbm.at[2, :, mine_cols], 2 * g + 1, 0, Q)
            copy(outw_hbm.at[:, mine_cols], 2 * g + 1, Q, Q)
        for f in range(nf):
            copy(up_hbm.at[:, pl.ds(f * W, W)], 4 + 2 * f, 0, W)
            copy(down_hbm.at[:, pl.ds(f * W, W)], 5 + 2 * f, 0, W)
        return copies

    cp_w = shard_copies()
    cp_x = pltpu.make_async_copy(x_hbm, xa.at[own], local_sem.at[1])
    cp_g = pltpu.make_async_copy(g_hbm, ga.at[own], local_sem.at[2])
    for cp in cp_w:
        cp.start()
    cp_x.start()
    cp_g.start()
    sm[z, y, c, t] = small_in[...]
    barrier = pltpu.get_barrier_semaphore()
    everyone = z_peer + [y_peer, c_peer] + t_peer
    for peer in everyone:
        pl.semaphore_signal(barrier, inc=1, device_id=peer, device_id_type=MESH)
    for cp in cp_w:
        cp.wait()
    cp_x.wait()
    cp_g.wait()
    pl.semaphore_wait(barrier, len(everyone))

    sm_t = [remote(sm.at[z, y, c, t], sm.at[z, y, c, t], sm_s.at[k], sm_r.at[k], t_peer[k]) for k in range(T - 1)]
    for cp in sm_t:
        cp.start()

    def one_of(ch, names):
        if isinstance(ch, int):
            return ch in names
        return functools.reduce(jnp.logical_or, [ch == n for n in names])

    def by_kind(ch, z_first, y_first):
        if not sz.gather_z_last:
            return z_first()
        kind = one_of(ch, sz.gather_z_last)
        if isinstance(ch, int):
            (y_first if kind else z_first)()
        else:
            pl.when(kind)(y_first)
            pl.when(jnp.logical_not(kind))(z_first)

    def g_far(ch, which=0):
        at = wts.at[ch, hi, lo, (1 - y) if which else y, c]
        return remote(at, at, gz_s.at[ch, which], gz_r.at[ch, which], far)

    def g_near(ch, which=0):
        at = wts.at[ch, hi, lo, (1 - y) if which else y, c]
        return remote(at, at, gz_s.at[ch, 2 + which], gz_r.at[ch, 2 + which], near)

    def g_pass(ch):
        at = wts.at[ch, 1 - hi, lo, y, c]
        return remote(at, at, gz_s.at[ch, 4], gz_r.at[ch, 4], near)

    def g_pass_both(ch):
        at = wts.at[ch, 1 - hi, lo, :, c]
        return remote(at, at, gz_s.at[ch, 4], gz_r.at[ch, 4], near)

    def gy(ch, which):
        at = (wts.at[ch, hi, lo, y, c], wts.at[ch, 1 - hi, lo, y, c], wts.at[ch, :, 1 - lo, y, c])[which]
        return remote(at, at, gy_s.at[ch, which], gy_r.at[ch, which], y_peer)

    def gc(ch):
        return remote(wts.at[ch, :, :, :, c], wts.at[ch, :, :, :, c], gc_s.at[ch], gc_r.at[ch], c_peer)

    def start_z(ch):
        g_far(ch).start()
        g_near(ch).start()

    start_z(0)
    for ch in range(sz.ahead_y):
        gy(ch, 0).start()
    row_x = [remote(xa.at[own], xa.at[own], row_s.at[0, k], row_r.at[0, k], t_peer[k]) for k in range(T - 1)]
    row_g = [remote(ga.at[own], ga.at[own], row_s.at[1, k], row_r.at[1, k], t_peer[k]) for k in range(T - 1)]
    for cp in row_x:
        cp.start()
    sm_z = [remote(sm.at[z, y, c], sm.at[z, y, c], sm_s.at[T - 1 + k], sm_r.at[T - 1 + k], z_peer[k]) for k in range(nz - 1)]
    sm_y = remote(sm.at[:, y, c], sm.at[:, y, c], sm_s.at[T + nz - 2], sm_r.at[T + nz - 2], y_peer)
    sm_c = remote(sm.at[:, :, c], sm.at[:, :, c], sm_s.at[T + nz - 1], sm_r.at[T + nz - 1], c_peer)
    tile = 128

    def stat_rows(first, count):
        def body(i, carry):
            rows = pl.ds(pl.multiple_of(first + i * tile, tile), tile)
            v = xa[rows, :].astype(F32)
            mean = jnp.mean(v, axis=-1, keepdims=True)
            cen = v - mean
            inv = lax.rsqrt(jnp.mean(cen * cen, axis=-1, keepdims=True) + EPSILON)
            stat[0, rows, :] = jnp.broadcast_to(mean, (tile, 128))
            stat[1, rows, :] = jnp.broadcast_to(inv, (tile, 128))
            return carry

        lax.fori_loop(0, count // tile, body, 0)

    stat_rows(t * R, R)
    for cp in sm_t:
        cp.wait_recv()
    for cp in sm_z:
        cp.start()

    def when(condition, act):
        if isinstance(condition, bool):
            if condition:
                act()
        else:
            pl.when(condition)(act)

    def on_z(e):
        def z_first():
            g_far(e).wait_recv()
            g_pass(e).start()
            gy(e, 1).start()

        def y_first():
            gy(e, 0).wait_recv()
            g_far(e, 1).start()
            g_near(e, 1).start()

        by_kind(e, z_first, y_first)

    def on_y(e):
        def z_first():
            g_near(e).wait_recv()
            g_pass(e).wait_recv()
            gy(e, 2).start()

        def y_first():
            g_far(e).wait_recv()
            g_far(e, 1).wait_recv()
            g_pass_both(e).start()

        by_kind(e, z_first, y_first)
        when(e + sz.ahead_z < NCH, lambda: start_z(e + sz.ahead_z))
        when(e + sz.ahead_y < NCH, lambda: gy(e + sz.ahead_y, 0).start())

    def on_c(e):
        def z_first():
            for which in range(3):
                gy(e, which).wait_recv()

        def y_first():
            g_near(e).wait_recv()
            g_near(e, 1).wait_recv()
            g_pass_both(e).wait_recv()

        by_kind(e, z_first, y_first)
        gc(e).start()

    def weights(ch):
        return wts[ch].reshape(D, W)

    def weight_half(ch, side):
        return wts[ch, :, :, :, :, :, side * Q : (side + 1) * Q].reshape(D, Q)

    def weight_rows_half(ch, i, side):
        return wts[ch, i, :, :, :, :, side * Q : (side + 1) * Q].reshape(D // 2, Q)

    def weight_rows(ch, i):
        return wts[ch, i].reshape(D // 2, W)

    on_z(0)
    for ch in range(1, sz.ahead_z):
        start_z(ch)
    for cp in sm_z:
        cp.wait_recv()
    sm_y.start()
    on_y(0)
    on_z(1)
    sm_y.wait_recv()
    sm_c.start()
    on_y(1)
    on_z(2)
    sm_c.wait_recv()

    flat = sm[...].reshape(sz.n_dp * T * 16, 128)
    n_rows = sz.n_dp * T * 16
    pick = (
        jnp.bitwise_and(lax.broadcasted_iota(jnp.int32, (16, n_rows), 1), 15)
        == lax.broadcasted_iota(jnp.int32, (16, n_rows), 0)
    ).astype(F32).astype(BF16)

    def lay_out(width, n, mine_only):
        shift = n.bit_length() - 1
        lane_of = lax.broadcasted_iota(jnp.int32, (128, width), 1)
        spread = (jnp.bitwise_and(lane_of, n - 1) == lax.broadcasted_iota(jnp.int32, (128, width), 0)).astype(F32).astype(BF16)
        wide = dot(flat, spread)
        piece = jnp.right_shift(lax.broadcasted_iota(jnp.int32, (n_rows, width), 1), shift)
        owner = jnp.right_shift(lax.broadcasted_iota(jnp.int32, (n_rows, width), 0), 4)
        if mine_only:
            piece = piece * T + t
        return dot(pick, jnp.where(piece == owner, wide, 0.0).astype(BF16))

    vec_d[...] = lay_out(D, D // (sz.n_dp * T), False)
    vec_q[...] = lay_out(W, W // sz.n_dp, True)
    def norm_rows(first, count):
        def body(i, carry):
            rows = pl.ds(pl.multiple_of(first + i * tile, tile), tile)
            norm = (xa[rows, :].astype(F32) - stat[0, rows, 0:1]) * stat[1, rows, 0:1]
            ha[rows, :] = (norm * vec_d[0:1, :] + vec_d[1:2, :]).astype(BF16)
            hm[rows, :] = (norm * vec_d[2:3, :] + vec_d[3:4, :]).astype(BF16)
            return carry

        lax.fori_loop(0, count // tile, body, 0)

    lane = lax.broadcasted_iota(jnp.int32, (1, 128), 1)
    low_half = lane < HEAD
    from_right = jnp.bitwise_and(lane, HEAD - 1) < ROT // 2
    big = min(512, R)
    scale = 1.0 / math.sqrt(HEAD)

    def turned(u, rows, sign):
        other = jnp.where(from_right, pltpu.roll(u, 128 - ROT // 2, 1), pltpu.roll(u, ROT // 2, 1))
        turn = other * sin_ref[rows, :]
        return u * cos_ref[rows, :] + (turn if sign > 0 else -turn)

    def project_qk(g, first):
        def body(i, carry):
            rows = pl.ds(pl.multiple_of(first + i * big, big), big)
            u = dot(ha[rows, :], weights(2 * g))
            for k in range(W // 128):
                side, at = divmod(k * 128, Q)
                part_u = u[:, k * 128 : (k + 1) * 128] + vec_q[6 + side : 7 + side, g * Q + at : g * Q + at + 128]
                part_u = turned(part_u, rows, 1)
                pool[2 * g, rows, k * 128 : (k + 1) * 128] = (part_u * scale if side == 0 else part_u).astype(BF16)
            return carry

        lax.fori_loop(0, R // big, body, 0)

    def project_v(g, first):
        def body(i, carry):
            rows = pl.ds(pl.multiple_of(first + i * big, big), big)
            u = dot(ha[rows, :], weight_half(2 * g + 1, 0)) + vec_q[8:9, g * Q : (g + 1) * Q]
            pool[2 * g + 1, rows, :Q] = u.astype(BF16)
            return carry

        lax.fori_loop(0, R // big, body, 0)

    def d_context(g, first):
        def body(i, carry):
            rows = pl.ds(pl.multiple_of(first + i * big, big), big)
            pool[2 * g + 1, rows, Q:] = dot(ga[rows, :], weight_half(2 * g + 1, 1)).astype(BF16)
            return carry

        lax.fori_loop(0, R // big, body, 0)

    norm_rows(t * R, R)
    for f in range(nf):
        vec_u[f] = lay_out_units(sz, flat, pick, n_rows, t, f)
    on_c(0)
    on_y(2)
    on_z(3)
    gc(0).wait_recv()
    project_qk(0, t * R)
    for k in range(1, T):
        row_x[k - 1].wait_recv()
        row_g[k - 1].start()
        first = lax.rem(t + T - k, T) * R
        stat_rows(first, R)
        norm_rows(first, R)
        project_qk(0, first)
    on_c(1)
    on_y(3)
    on_z(4)
    gc(1).wait_recv()
    for k in range(T):
        project_v(0, k * R)
    d_context(0, t * R)

    acc[...] = jnp.zeros_like(acc)

    def rc(i):
        return remote(
            part.at[lax.rem(i, sz.p_slots), :, :, :, 1 - c], red_c.at[lax.rem(i, sz.r_slots)], rc_s.at[i], rc_r.at[i], c_peer
        )

    def r1(i):
        at = red_c.at[lax.rem(i, sz.r_slots)]
        src, to = (at.at[:, 1 - lo], near) if i in sz.reduce_y_last else (at.at[:, :, 1 - y], y_peer)
        return remote(src, red_y.at[i], ry_s.at[i], ry_r.at[i], to)

    def r2(i):
        src, to = (red_y.at[i, 1 - hi], far) if i in sz.reduce_y_last else (red_y.at[i, :, 1 - lo], near)
        return remote(src, red_z1.at[i], rz_s.at[i, 0], rz_r.at[i, 0], to)

    def r3(i):
        src, to = (red_y.at[i, hi, 1 - y], y_peer) if i in sz.reduce_y_last else (red_y.at[i, 1 - hi, lo], far)
        return remote(src, red_z2.at[i], rz_s.at[i, 1], rz_r.at[i, 1], to)

    def emit(i, left, right):
        slot = lax.rem(i, sz.p_slots)

        def body(n, carry):
            cols = pl.ds(pl.multiple_of(n * (D // 2), D // 2), D // 2)
            made = dot(left[:, cols], right[...], TN)
            part[slot, n] = made.astype(BF16).reshape(2, 2, 2, r, W)
            return carry

        lax.fori_loop(0, 2, body, 0)
        send(i)

    def emit_heads(i, g):
        slot = lax.rem(i, sz.p_slots)

        def body(n, carry):
            cols = pl.ds(pl.multiple_of(n * (D // 2), D // 2), D // 2)
            for side, left in enumerate((ha, ga)):
                right = dvc[g, :, side * Q : (side + 1) * Q]
                made = dot(left[:, cols], right, TN).astype(BF16).reshape(2, 2, 2, r, Q)
                part[slot, n, :, :, :, :, side * Q : (side + 1) * Q] = made
            return carry

        lax.fori_loop(0, 2, body, 0)
        send(i)

    def send(i):
        if i >= sz.r_slots:
            pl.semaphore_wait(credit, 1)
        rc(i).start()

    def event_c(i):
        rc(i).wait()
        slot, rslot = lax.rem(i, sz.p_slots), lax.rem(i, sz.r_slots)
        red_c[rslot] = (part[slot, :, :, :, c].astype(F32) + red_c[rslot].astype(F32)).astype(BF16)
        r1(i).start()

    def event_y(i):
        r1(i).wait()
        rslot = lax.rem(i, sz.r_slots)
        kept = red_c[rslot, :, lo] if i in sz.reduce_y_last else red_c[rslot, :, :, y]
        red_y[i] = (kept.astype(F32) + red_y[i].astype(F32)).astype(BF16)
        if i < NCH - sz.r_slots:
            pl.semaphore_signal(credit, inc=1, device_id=c_peer, device_id_type=MESH)
        r2(i).start()

    def event_n(i):
        r2(i).wait()
        if i in sz.reduce_y_last:
            red_y[i, hi] = (red_y[i, hi].astype(F32) + red_z1[i].astype(F32)).astype(BF16)
        else:
            red_y[i, :, lo] = (red_y[i, :, lo].astype(F32) + red_z1[i].astype(F32)).astype(BF16)
        r3(i).start()

    def event_z(i, late=False):
        if (i in sz.reduce_y_last) != late:
            return
        r3(i).wait()
        kept = red_y[i, hi, y] if i in sz.reduce_y_last else red_y[i, hi, lo]
        total = kept.astype(F32) + red_z2[i].astype(F32)
        g = i // 2
        if i < 4 and i % 2 == 0:
            dqkv_ref[0, :, g * Q : (g + 1) * Q] = total[:, :Q]
            dqkv_ref[1, :, g * Q : (g + 1) * Q] = total[:, Q:]
        elif i < 4:
            dqkv_ref[2, :, g * Q : (g + 1) * Q] = total[:, :Q]
            doutw_ref[:, g * Q : (g + 1) * Q] = total[:, Q:]
        else:
            (dupw_ref, ddown_ref)[i % 2][:, (g - 2) * W : (g - 1) * W] = total

    sums_ref[...] = jnp.zeros_like(sums_ref)

    def row_sum(v):
        return jnp.sum(v.astype(F32), axis=0, keepdims=True)

    def mlp(first, count, f, act):
        def body(i, carry):
            rows = pl.ds(pl.multiple_of(first + i * big, big), big)
            u = dot(hm[rows, :], weights(4 + 2 * f)) + vec_u[f, 9:10, :]
            cdf = 0.5 + 0.5 * lax.erf(u * math.sqrt(0.5))
            act[rows, :] = (u * cdf).astype(BF16)
            slope = cdf + u * (jnp.exp(u * u * -0.5) * (1.0 / math.sqrt(2.0 * math.pi)))
            back = slope * dot(ga[rows, :], weights(5 + 2 * f))
            dup[f, rows, :] = back.astype(BF16)
            return carry

        lax.fori_loop(0, count // big, body, 0)

    def emit_units(i):
        f = (i - 4) // 2
        if i % 2:
            emit(i, ga, pool.at[f])
        else:
            emit(i, hm, dup.at[f])

    B = sz.block
    n_pairs = Q // 128
    steps = 2 * sz.n_blocks
    own_steps = 2 * sz.own_blocks

    def attend(qb, g, step):
        L = (qb + 1) * B
        rows = pl.ds(qb * B, B)
        for s in range(B // 128):
            here = pl.ds(s * 128, 128)
            start = jnp.broadcast_to(seg_ref[0:1, qb * B + s * 128 : qb * B + (s + 1) * 128].astype(F32), (128, 128)).T
            start = start[:, 0:1].astype(jnp.int32)
            key_at = lax.broadcasted_iota(jnp.int32, (128, L), 1)
            row_at = lax.broadcasted_iota(jnp.int32, (128, L), 0) + (qb * B + s * 128)
            bias[here, :L] = jnp.where((key_at >= start) & (key_at <= row_at), 0.0, NEGATIVE)

        def pair(p, carry):
            cols = pl.ds(pl.multiple_of(p * 128, 128), 128)
            cols_2 = pl.ds(pl.multiple_of(Q + p * 128, 128), 128)
            query, keys = pool[2 * g, rows, cols], pool[2 * g, :L, cols_2]
            values, d_ctx = pool[2 * g + 1, :L, cols], pool[2 * g + 1, rows, cols_2]
            made = []
            for h in range(2):
                mine = low_half if h == 0 else jnp.logical_not(low_half)
                q_h = jnp.where(mine, query, jnp.zeros_like(query))
                d_h = jnp.where(mine, d_ctx, jnp.zeros_like(d_ctx))
                scores = dot(q_h, keys, NT) + bias[:, :L]
                top = jnp.max(scores, axis=1, keepdims=True)
                e = jnp.exp(scores - top)
                prob = e * (1.0 / jnp.sum(e, axis=1, keepdims=True))
                d_prob = dot(d_h, values, NT)
                delta = jnp.sum(prob * d_prob, axis=1, keepdims=True)
                d_s = (prob * (d_prob - delta)).astype(BF16)
                p_b = prob.astype(BF16)
                made.append((dot(p_b, values), dot(d_s, keys), dot(d_s, q_h, TN), dot(p_b, d_h, TN)))
            dvc[g, rows, cols_2] = jnp.where(low_half, made[0][0], made[1][0]).astype(BF16)
            d_q = jnp.where(low_half, made[0][1], made[1][1]) * scale
            dqk[g, rows, cols] = turned(d_q, rows, -1).astype(BF16)
            cols_k = pl.ds(pl.multiple_of(g * Q + p * 128, 128), 128)
            cols_v = pl.ds(pl.multiple_of(W + g * Q + p * 128, 128), 128)
            acc[:L, cols_k] += made[0][2] + made[1][2]
            acc[:L, cols_v] += made[0][3] + made[1][3]
            at = step * n_pairs + p

            def poll():
                turn = lax.div(at, 2)
                e = 4 + turn + jnp.where(turn >= 2, 1, 0)
                on_z(e + 1)
                on_y(e)
                on_c(e - 2)

            pl.when((lax.rem(at, 2) == 0) & (at <= 10))(poll)
            pl.when(at == 12)(lambda: on_c(10))
            return carry

        lax.fori_loop(0, n_pairs, pair, 0)

    def finish_group(g):
        def body(i, carry):
            rows = pl.ds(pl.multiple_of(i * tile, tile), tile)
            for k in range(n_pairs):
                cols = pl.ds(g * Q + k * 128, 128)
                dqk[g, rows, pl.ds(Q + k * 128, 128)] = turned(acc[rows, cols], rows, -1).astype(BF16)
            dvc[g, rows, :Q] = acc[rows, pl.ds(W + g * Q, Q)].astype(BF16)
            return carry

        lax.fori_loop(0, S // tile, body, 0)
        emit(2 * g, ha, dqk.at[g])
        if g == 0:
            on_y(11)
            on_c(9)
        emit_heads(2 * g + 1, g)
        event_c(2 * g)
        sums_ref[5:6, g * Q : (g + 1) * Q] = row_sum(dqk[g, :, :Q])
        sums_ref[5:6, W + g * Q : W + (g + 1) * Q] = row_sum(dqk[g, :, Q:])
        sums_ref[5:6, 2 * W + g * Q : 2 * W + (g + 1) * Q] = row_sum(dvc[g, :, :Q])

    other_blocks = sz.n_blocks - sz.own_blocks

    def block_step(step, carry):
        def second_group():
            gc(2).wait_recv()
            gc(3).wait_recv()
            for k in range(T):
                project_qk(1, k * R)
            on_z(7)
            on_y(6)
            on_c(4)
            for k in range(T):
                project_v(1, k * R)
            d_context(1, t * R)

        def other_rows():
            for k in range(1, T):
                row_g[k - 1].wait_recv()
                for g in range(2):
                    d_context(g, lax.rem(t + T - k, T) * R)

        pl.when(step == sz.own_blocks)(second_group)
        pl.when(step == own_steps)(other_rows)
        pl.when(step == own_steps + other_blocks)(lambda: finish_group(0))
        later = step >= own_steps
        count = jnp.where(later, other_blocks, sz.own_blocks)
        at = jnp.where(later, step - own_steps, step)
        g = lax.div(at, count)
        j = lax.rem(at, count) + jnp.where(later, sz.own_blocks, 0)
        which = lax.rem(j + t * sz.own_blocks, sz.n_blocks)
        for qb in range(sz.n_blocks):
            pl.when(which == qb)(functools.partial(attend, qb, g, step))
        return carry

    lax.fori_loop(0, steps, block_step, 0)
    event_c(1)
    on_c(11)
    finish_group(1)

    half = D // 2

    def branch(first, i, n):
        rows = pl.ds(pl.multiple_of(first + i * big, big), big)
        total = dot(pool[0, rows, :], weight_rows(5, n), NT)
        for f in range(1, nf):
            total = total + dot(pool[f, rows, :], weight_rows(5 + 2 * f, n), NT)
        for g in range(2):
            total = total + dot(dvc[g, rows, Q:], weight_rows_half(2 * g + 1, n, 1), NT)
        return total

    def d_hidden(first, i, n):
        rows = pl.ds(pl.multiple_of(first + i * big, big), big)
        cols = pl.ds(pl.multiple_of(n * half, half), half)
        d_attn = dot(dqk[0, rows, :], weight_rows(0, n), NT) + dot(dqk[1, rows, :], weight_rows(2, n), NT)
        for g in range(2):
            d_attn = d_attn + dot(dvc[g, rows, :Q], weight_rows_half(2 * g + 1, n, 0), NT)
        d_mlp = dot(dup[0, rows, :], weight_rows(4, n), NT)
        for f in range(1, nf):
            d_mlp = d_mlp + dot(dup[f, rows, :], weight_rows(4 + 2 * f, n), NT)
        norm = (xa[rows, cols].astype(F32) - stat[0, rows, 0:1]) * stat[1, rows, 0:1]
        sums_ref[0:1, cols] += row_sum(d_attn * norm)
        sums_ref[1:2, cols] += row_sum(d_attn)
        sums_ref[2:3, cols] += row_sum(d_mlp * norm)
        sums_ref[3:4, cols] += row_sum(d_mlp)
        return d_attn * vec_d[0:1, cols] + d_mlp * vec_d[2:3, cols]

    def xt(which, k):
        src, dst = ((b_send, b_recv), (h_send, h_recv))[which]
        return remote(src.at[k], dst.at[k], xt_s.at[which, k], xt_r.at[which, k], t_peer[k])

    def events(i_y, i_n, i_z):
        if i_y is not None:
            event_y(i_y)
        if i_n is not None:
            event_n(i_n)
        if i_z is not None:
            event_z(i_z)

    for k in range(T - 1):
        first = lax.rem(t + k + 1, T) * R

        def other_units(f, carry, first=first, k=k):
            if k == 0:
                gc(4 + 2 * f).wait_recv()
                gc(5 + 2 * f).wait_recv()
            mlp(first, R, f, pool.at[f])
            return carry

        lax.fori_loop(0, nf, other_units, 0)
    event_c(3)
    event_y(0)
    for k in range(T - 1):
        first = lax.rem(t + k + 1, T) * R

        def both(q, carry, first=first, k=k):
            i, n = lax.div(q, 2), lax.rem(q, 2)
            cols = pl.ds(pl.multiple_of(n * half, half), half)
            rows = pl.ds(pl.multiple_of(i * big, big), big)
            b_send[k, rows, cols] = branch(first, i, n).astype(BF16)
            return carry

        lax.fori_loop(0, 2 * (R // big), both, 0)
        xt(0, k).start()
    event_y(1)
    mlp(t * R, R, 0, pool.at[0])
    emit_units(4)
    event_n(0)
    emit_units(5)
    event_c(4)
    event_y(2)
    for k in range(T - 1):
        first = lax.rem(t + k + 1, T) * R

        def both_back(q, carry, first=first, k=k):
            i, n = lax.div(q, 2), lax.rem(q, 2)
            cols = pl.ds(pl.multiple_of(n * half, half), half)
            rows = pl.ds(pl.multiple_of(i * big, big), big)
            h_send[k, rows, cols] = d_hidden(first, i, n).astype(BF16)
            return carry

        lax.fori_loop(0, 2 * (R // big), both_back, 0)
        xt(1, k).start()
    event_c(5)
    events(3, 1, None)
    mlp(t * R, R, 1, pool.at[1])
    emit_units(6)
    event_n(2)
    emit_units(7)
    event_c(6)
    event_y(4)
    mlp(t * R, R, 2, pool.at[2])
    event_c(7)
    mlp(t * R, R, 3, pool.at[3])
    events(5, 3, None)

    def own_back(q, carry):
        i, n = lax.div(q, 2), lax.rem(q, 2)
        cols = pl.ds(pl.multiple_of(n * half, half), half)
        acc[pl.ds(pl.multiple_of(R + i * big, big), big), cols] = d_hidden(t * R, i, n)
        return carry

    lax.fori_loop(0, 2 * (R // big), own_back, 0)
    sums_ref[4:5, :D] = row_sum(ga[own, :])
    for f in range(nf):
        sums_ref[6:7, f * W : (f + 1) * W] = row_sum(dup[f])

    su_c = remote(sums_ref, sums_in.at[0], su_s.at[0], su_r.at[0], c_peer)
    su_y = remote(sums_ref, sums_in.at[1], su_s.at[1], su_r.at[1], y_peer)
    su_n = remote(sums_ref, sums_in.at[2], su_s.at[2], su_r.at[2], near)
    su_f = remote(sums_ref, sums_in.at[3], su_s.at[3], su_r.at[3], far)
    su_t = [remote(sums_ref, sums_in.at[4 + k], su_s.at[4 + k], su_r.at[4 + k], t_peer[k]) for k in range(T - 1)]
    stages = (su_c, su_y, su_n, su_f)

    def sums_step(n):
        if n < 4:
            stages[n].wait()
            sums_ref[...] += sums_in[n]
        if n < 3:
            stages[n + 1].start()
        elif n == 3:
            for cp in su_t:
                cp.start()
        else:
            for cp in su_t:
                cp.wait()
            for k in range(T - 1):
                sums_ref[0:5, :] += sums_in[4 + k, 0:5, :]

    def mine(row, first, width, n, at):
        part_row = jnp.broadcast_to(sums_ref[row : row + 1, first : first + width], (8, width))
        return pltpu.roll(part_row, lax.rem(width - at, width), 1)[0:1, 0:128]

    def finish_out(i, carry):
        rows = pl.ds(pl.multiple_of(i * tile, tile), tile)
        here = pl.ds(pl.multiple_of(t * R + i * tile, tile), tile)
        total = xa[here, :].astype(F32) + acc[rows, :] + (vec_d[4:5, :] + vec_d[5:6, :])
        for k in range(T - 1):
            total = total + b_recv[k, rows, :].astype(F32)
        b_send[0, rows, :] = total.astype(BF16)
        return carry

    def finish_grad(i, carry):
        rows = pl.ds(pl.multiple_of(R + i * tile, tile), tile)
        there = pl.ds(pl.multiple_of(i * tile, tile), tile)
        here = pl.ds(pl.multiple_of(t * R + i * tile, tile), tile)
        inv = stat[1, here, 0:1]
        norm = (xa[here, :].astype(F32) - stat[0, here, 0:1]) * inv
        d_hat = acc[rows, :]
        for k in range(T - 1):
            d_hat = d_hat + h_recv[k, there, :].astype(F32)
        inner = jnp.mean(d_hat * norm, axis=-1, keepdims=True)
        acc[rows, :] = ga[here, :].astype(F32) + inv * (d_hat - jnp.mean(d_hat, axis=-1, keepdims=True) - norm * inner)
        return carry

    su_c.start()
    event_n(4)
    emit_units(8)
    sums_step(0)
    emit_units(9)
    event_c(8)
    event_y(6)
    emit_units(10)
    event_c(9)
    event_n(5)
    emit_units(11)
    event_c(10)
    event_y(7)
    event_c(11)

    def own_both(q, carry):
        i, n = lax.div(q, 2), lax.rem(q, 2)
        cols = pl.ds(pl.multiple_of(n * half, half), half)
        acc[pl.ds(pl.multiple_of(i * big, big), big), cols] = branch(t * R, i, n)
        return carry

    lax.fori_loop(0, 2 * (R // big), own_both, 0)
    events(8, 6, 0)
    sums_step(1)
    event_n(7)
    event_z(1)
    event_z(2)
    event_z(3)

    for k in range(T - 1):
        xt(0, k).wait()
    lax.fori_loop(0, R // tile, finish_out, 0)
    cp_out = pltpu.make_async_copy(b_send.at[0], out_hbm, local_sem.at[3])
    cp_out.start()
    event_y(9)
    event_n(8)
    sums_step(2)
    event_z(4)
    event_z(5)
    event_y(10)
    event_z(6)
    event_n(9)
    sums_step(3)
    event_z(7)
    event_y(11)
    event_z(8)
    for k in range(T - 1):
        xt(1, k).wait()
    lax.fori_loop(0, R // tile, finish_grad, 0)
    cp_grad = pltpu.make_async_copy(acc.at[pl.ds(R, R)], igrad_hbm, local_sem.at[4])
    cp_grad.start()
    event_n(10)
    sums_step(4)
    event_z(9)
    for i in sz.reduce_y_last:
        event_z(i, late=True)
    event_n(11)
    n_d, n_q, n_u = D // (sz.n_dp * T), W // sz.n_dp, sz.units // sz.n_dp
    small_out[...] = jnp.zeros_like(small_out)
    for k in range(5):
        small_out[k : k + 1, :] = mine(k, 0, D, n_d, (dp * T + t) * n_d)
    for j in range(3):
        small_out[5 + j : 6 + j, :] = mine(5, j * W, W, n_q, dp * n_q)
    small_out[8:9, :] = mine(6, 0, sz.units, n_u, dp * n_u)
    event_z(10)
    event_z(11)

    for cp in sm_t + sm_z + [sm_y, sm_c] + row_x + row_g:
        cp.wait_send()

    def sent(ch, carry):
        for copy in (g_far(ch), gy(ch, 0), g_near(ch), gc(ch)):
            copy.wait_send()

        def z_first():
            for copy in (g_pass(ch), gy(ch, 1), gy(ch, 2)):
                copy.wait_send()

        def y_first():
            for copy in (g_far(ch, 1), g_near(ch, 1), g_pass_both(ch)):
                copy.wait_send()

        by_kind(ch, z_first, y_first)
        return carry

    lax.fori_loop(0, NCH, sent, 0)
    cp_out.wait()
    cp_grad.wait()


def hand_out(n, nq, nu, *refs):
    large, small, out_large, out_small, held, sems = refs[:6], refs[6], refs[7:13], refs[13:21], refs[21:27], refs[27]
    into = [pltpu.make_async_copy(large[k], held[k], sems.at[0, k]) for k in range(6)]
    out = [pltpu.make_async_copy(held[k], out_large[k], sems.at[1, k]) for k in range(6)]
    for cp in into:
        cp.start()
    for k in range(5):
        out_small[k][...] = small[k : k + 1, :n]
    out_small[5][...] = small[4:5, :n]
    for j in range(3):
        out_small[6][j] = small[5 + j : 6 + j, :nq]
    out_small[7][...] = small[8:9, :nu]
    for k in range(6):
        into[k].wait()
        out[k].start()
    for cp in out:
        cp.wait()


def lay_out_units(sz, flat, pick, n_rows, t, f):
    n = sz.units // sz.n_dp
    shift = n.bit_length() - 1
    W = sz.width
    lane_of = lax.broadcasted_iota(jnp.int32, (128, W), 1) + f * W
    spread = (jnp.bitwise_and(lane_of, n - 1) == lax.broadcasted_iota(jnp.int32, (128, W), 0)).astype(F32).astype(BF16)
    wide = dot(flat, spread)
    piece = jnp.right_shift(lax.broadcasted_iota(jnp.int32, (n_rows, W), 1) + f * W, shift) * sz.n_t + t
    owner = jnp.right_shift(lax.broadcasted_iota(jnp.int32, (n_rows, W), 0), 4)
    return dot(pick, jnp.where(piece == owner, wide, 0.0).astype(BF16))


def fused(sz, args):
    (
        inputs, segment_ids, ln_attn_gain, ln_attn_bias, ln_mlp_gain, ln_mlp_bias, qkv_weight, qkv_bias,
        out_weight, out_bias, up_weight, up_bias, down_weight, down_bias, cotangent,
    ) = args
    nz, r, D, W, S, R, T, nf, NCH = sz.nz, sz.shard, sz.d, sz.width, sz.seq, sz.rows, sz.n_t, sz.nf, sz.chunks

    def placed(v, first):
        return jnp.pad(v, ((first, 16 - first - v.shape[0]), (0, 128 - v.shape[1])))

    vectors = (ln_attn_gain, ln_attn_bias, ln_mlp_gain, ln_mlp_bias, out_bias, down_bias)
    small = placed(qkv_bias[:, 0], 6) + placed(up_bias, 9)
    for k, v in enumerate(vectors):
        small = small + placed(v[None], k)
    half_rot = ROT // 2
    place = np.arange(S, dtype=np.float32)
    inverse = (10000.0 ** (-(2.0 * np.arange(half_rot, dtype=np.float32)) / ROT)).astype(np.float32)
    theta = place[:, None] * inverse[None, :]
    cos, sin = np.cos(theta), np.sin(theta)
    cos_head = np.concatenate([cos, cos, np.ones((S, HEAD - ROT), np.float32)], axis=1)
    sin_head = np.concatenate([-sin, sin, np.zeros((S, HEAD - ROT), np.float32)], axis=1)
    cos_table = jnp.asarray(np.tile(cos_head, (1, 128 // HEAD)), F32)
    sin_table = jnp.asarray(np.tile(sin_head, (1, 128 // HEAD)), F32)

    hbm = pl.BlockSpec(memory_space=pl.ANY)
    vmem = pl.BlockSpec(memory_space=pltpu.VMEM)
    sw = sz.sums_width
    dma = pltpu.SemaphoreType.DMA
    n_small = T - 1 + nz - 1 + 2
    scratch = [
        pltpu.VMEM((S, D), BF16),
        pltpu.VMEM((S, D), BF16),
        pltpu.VMEM((S, D), BF16),
        pltpu.VMEM((S, D), BF16),
        pltpu.VMEM((2, S, 128), F32),
        pltpu.VMEM((NCH, 2, 2, 2, 2, r, W), BF16),
        pltpu.VMEM((nz, 2, 2, T, 16, 128), BF16),
        pltpu.VMEM((16, D), F32),
        pltpu.VMEM((16, W), F32),
        pltpu.VMEM((nf, 16, W), F32),
        pltpu.VMEM((max(4, nf), S, W), BF16),
        pltpu.VMEM((2, S, W), BF16),
        pltpu.VMEM((2, S, W), BF16),
        pltpu.VMEM((nf, S, W), BF16),
        pltpu.VMEM((S, D), F32),
        pltpu.VMEM((sz.block, S), F32),
        pltpu.VMEM((sz.p_slots, 2, 2, 2, 2, r, W), BF16),
        pltpu.VMEM((sz.r_slots, 2, 2, 2, r, W), BF16),
        pltpu.VMEM((NCH, 2, 2, r, W), BF16),
        pltpu.VMEM((NCH, 2, r, W), BF16),
        pltpu.VMEM((NCH, r, W), BF16),
        pltpu.VMEM((T - 1, R, D), BF16),
        pltpu.VMEM((T - 1, R, D), BF16),
        pltpu.VMEM((T - 1, R, D), BF16),
        pltpu.VMEM((T - 1, R, D), BF16),
        pltpu.VMEM((8, sw), F32),
        pltpu.VMEM((3 + T, 8, sw), F32),
        dma((5,)), dma((8 + 2 * nf,)),
        dma((n_small,)), dma((n_small,)),
        dma((2, T - 1)), dma((2, T - 1)),
        dma((NCH, 5)), dma((NCH, 5)),
        dma((NCH, 3)), dma((NCH, 3)),
        dma((NCH,)), dma((NCH,)),
        dma((NCH,)), dma((NCH,)),
        dma((NCH,)), dma((NCH,)),
        dma((NCH, nz - 1)), dma((NCH, nz - 1)),
        dma((2, T - 1)), dma((2, T - 1)),
        dma((3 + T,)), dma((3 + T,)),
        pltpu.SemaphoreType.REGULAR,
    ]
    units = sz.units
    output, input_grad, d_qkv, d_out, d_up, d_down, small_sums = pl.pallas_call(
        functools.partial(fused_kernel, sz),
        out_shape=(
            jax.ShapeDtypeStruct((R, D), BF16),
            jax.ShapeDtypeStruct((R, D), F32),
            jax.ShapeDtypeStruct((3, r, W), F32),
            jax.ShapeDtypeStruct((r, W), F32),
            jax.ShapeDtypeStruct((r, units), F32),
            jax.ShapeDtypeStruct((r, units), F32),
            jax.ShapeDtypeStruct((16, 128), F32),
        ),
        in_specs=[hbm, hbm, hbm, hbm, hbm, hbm, vmem, vmem, vmem, vmem],
        out_specs=(hbm, hbm, vmem, vmem, vmem, vmem, vmem),
        scratch_shapes=scratch,
        compiler_params=pltpu.CompilerParams(collective_id=0, has_side_effects=True, vmem_limit_bytes=VMEM_BYTES),
    )(
        inputs, cotangent, qkv_weight.transpose(1, 0, 2), out_weight.T, up_weight, down_weight.T, small,
        segment_ids.reshape(1, S), cos_table, sin_table,
    )

    n, nq, nu = D // (sz.n_dp * T), W // sz.n_dp, units // sz.n_dp
    large = (output, input_grad, d_qkv, d_out, d_up, d_down)
    outs = pl.pallas_call(
        functools.partial(hand_out, n, nq, nu),
        out_shape=[jax.ShapeDtypeStruct(v.shape, v.dtype) for v in large]
        + [jax.ShapeDtypeStruct((1, n), F32)] * 6
        + [jax.ShapeDtypeStruct((3, 1, nq), F32), jax.ShapeDtypeStruct((1, nu), F32)],
        in_specs=[hbm] * 6 + [vmem],
        out_specs=[hbm] * 6 + [vmem] * 8,
        scratch_shapes=[pltpu.VMEM(v.shape, v.dtype) for v in large] + [dma((2, 6))],
    )(*large, small_sums)
    output, input_grad, d_qkv, d_out, d_up, d_down = outs[:6]
    vectors = [v.reshape(n) for v in outs[6:12]]
    return (
        output, input_grad, vectors[0], vectors[1], vectors[2], vectors[3],
        d_qkv.transpose(1, 0, 2), outs[12], d_out.T, vectors[4], d_up, outs[13], d_down.T, vectors[5],
    )


def rotated(values, cosine, sine, sign):
    half_rot = ROT // 2
    first_half = values[..., :half_rot]
    second_half = values[..., half_rot:ROT]
    new_first = first_half * cosine - sign * second_half * sine
    new_second = second_half * cosine + sign * first_half * sine
    return jnp.concatenate([new_first, new_second, values[..., ROT:]], axis=-1)


def angle_tables(length):
    position = jnp.arange(length).astype(jnp.float32)
    inverse = 10000.0 ** (-(2.0 * jnp.arange(ROT // 2).astype(jnp.float32)) / ROT)
    theta = position[:, None] * inverse[None, :]
    return (jnp.cos(theta)[:, None, :], jnp.sin(theta)[:, None, :])


def gelu_exact(value):
    return jax.nn.gelu(value, approximate=False)


def layer_norm(rows):
    centred = rows - jnp.mean(rows, axis=-1, keepdims=True)
    inv_std = lax.rsqrt(jnp.mean(centred * centred, axis=-1, keepdims=True) + EPSILON)
    return (centred * inv_std, inv_std)


def plain(
    inputs,
    segment_ids,
    ln_attn_gain,
    ln_attn_bias,
    ln_mlp_gain,
    ln_mlp_bias,
    qkv_weight,
    qkv_bias,
    out_weight,
    out_bias,
    up_weight,
    up_bias,
    down_weight,
    down_bias,
    cotangent,
):
    seq_len = segment_ids.shape[0]
    norm_terms = (
        lax.all_gather(ln_attn_gain, ("dp", "tensor"), axis=0, tiled=True),
        lax.all_gather(ln_attn_bias, ("dp", "tensor"), axis=0, tiled=True),
        lax.all_gather(ln_mlp_gain, ("dp", "tensor"), axis=0, tiled=True),
        lax.all_gather(ln_mlp_bias, ("dp", "tensor"), axis=0, tiled=True),
        lax.all_gather(out_bias, ("dp", "tensor"), axis=0, tiled=True),
        lax.all_gather(down_bias, ("dp", "tensor"), axis=0, tiled=True),
    )
    gain_attn = norm_terms[0].astype(jnp.float32)
    shift_attn = norm_terms[1].astype(jnp.float32)
    gain_mlp = norm_terms[2].astype(jnp.float32)
    shift_mlp = norm_terms[3].astype(jnp.float32)
    bias_sum = norm_terms[4].astype(jnp.float32) + norm_terms[5].astype(jnp.float32)
    w_qkv, b_qkv, w_out, w_up, b_up, w_down = (
        lax.all_gather(qkv_weight, "dp", axis=0, tiled=True),
        lax.all_gather(qkv_bias, "dp", axis=2, tiled=True),
        lax.all_gather(out_weight, "dp", axis=1, tiled=True),
        lax.all_gather(up_weight, "dp", axis=0, tiled=True),
        lax.all_gather(up_bias, "dp", axis=1, tiled=True),
        lax.all_gather(down_weight, "dp", axis=1, tiled=True),
    )
    local_width = w_qkv.shape[2]
    heads_here = local_width // HEAD
    score_scale = 1.0 / math.sqrt(HEAD)
    resid = inputs.astype(jnp.float32)
    normalized, inv_std = layer_norm(resid)
    whole_inputs = lax.all_gather(inputs, "tensor", axis=0, tiled=True)
    normal_all, unused_std = layer_norm(whole_inputs.astype(jnp.float32))
    attn_rows = (normal_all * gain_attn + shift_attn).astype(jnp.bfloat16)
    mlp_rows = (normal_all * gain_mlp + shift_mlp).astype(jnp.bfloat16)
    proj = jnp.einsum("sd,dje->sje", attn_rows, w_qkv, preferred_element_type=jnp.float32)
    proj = proj + b_qkv.astype(jnp.float32).reshape(1, 3, local_width)
    cosine, sine = angle_tables(seq_len)
    query = rotated(proj[:, 0].reshape(seq_len, heads_here, HEAD), cosine, sine, 1.0).astype(
        jnp.bfloat16
    )
    keys = rotated(proj[:, 1].reshape(seq_len, heads_here, HEAD), cosine, sine, 1.0).astype(
        jnp.bfloat16
    )
    values = proj[:, 2].reshape(seq_len, heads_here, HEAD).astype(jnp.bfloat16)
    block_rows = min(512, seq_len)
    block_count = seq_len // block_rows
    places = jnp.arange(seq_len)
    query_blocks = query.reshape(block_count, block_rows, heads_here, HEAD)
    segment_blocks = segment_ids.reshape(block_count, block_rows)
    place_blocks = places.reshape(block_count, block_rows)

    def masked_scores(query_part, segment_part, place_part):
        scores = (
            jnp.einsum("qhe,khe->hqk", query_part, keys, preferred_element_type=jnp.float32)
            * score_scale
        )
        allowed = (segment_part[:, None] == segment_ids[None, :]) & (
            place_part[:, None] >= places[None, :]
        )
        return jnp.where(allowed[None], scores, NEGATIVE)

    def forward_block(block_item):
        query_part, segment_part, place_part = block_item
        scores = masked_scores(query_part, segment_part, place_part)
        row_max = jnp.max(scores, axis=-1, keepdims=True)
        exponent = jnp.exp(scores - row_max)
        row_total = jnp.sum(exponent, axis=-1, keepdims=True)
        probability = (exponent / row_total).astype(jnp.bfloat16)
        context_part = jnp.einsum(
            "hqk,khe->qhe", probability, values, preferred_element_type=jnp.float32
        )
        return (context_part, (row_max + jnp.log(row_total))[..., 0])

    context_blocks, log_totals = lax.map(
        forward_block, (query_blocks, segment_blocks, place_blocks)
    )
    context = context_blocks.reshape(seq_len, local_width).astype(jnp.bfloat16)
    up_in = jnp.dot(mlp_rows, w_up, preferred_element_type=jnp.float32) + b_up.astype(jnp.float32)
    activated = gelu_exact(up_in).astype(jnp.bfloat16)
    context_part = context
    branch_sum = lax.psum_scatter(
        jnp.dot(context_part, w_out, preferred_element_type=jnp.float32)
        + jnp.dot(activated, w_down, preferred_element_type=jnp.float32),
        "tensor",
        scatter_dimension=0,
        tiled=True,
    )
    output = (resid + branch_sum + bias_sum).astype(jnp.bfloat16)
    grad_all = lax.all_gather(cotangent, "tensor", axis=0, tiled=True)
    d_active = jnp.einsum("sd,fd->sf", grad_all, w_down, preferred_element_type=jnp.float32)
    gelu_value, gelu_back = jax.vjp(gelu_exact, up_in)
    d_up = gelu_back(d_active)[0].astype(jnp.bfloat16)
    d_w_down = jnp.einsum("sf,sd->fd", activated, grad_all, preferred_element_type=jnp.float32)
    d_w_up = jnp.einsum("sd,sf->df", mlp_rows, d_up, preferred_element_type=jnp.float32)
    d_b_up = jnp.sum(d_up, axis=0, dtype=jnp.float32).reshape(1, -1)
    unit_sums = (d_w_up, d_b_up, d_w_down)
    d_context = jnp.einsum("sd,cd->sc", grad_all, w_out, preferred_element_type=jnp.float32).astype(
        jnp.bfloat16
    )
    d_w_out = jnp.einsum("sc,sd->cd", context, grad_all, preferred_element_type=jnp.float32)
    d_context_blocks = d_context.reshape(block_count, block_rows, heads_here, HEAD)

    def backward_block(carry, block_item):
        d_keys, d_values = carry
        query_part, d_context_part, segment_part, place_part, log_part = block_item
        scores = masked_scores(query_part, segment_part, place_part)
        probability = jnp.exp(scores - log_part[..., None])
        d_prob = jnp.einsum(
            "qhe,khe->hqk", d_context_part, values, preferred_element_type=jnp.float32
        )
        row_delta = jnp.sum(probability * d_prob, axis=-1, keepdims=True)
        d_scores = (probability * (d_prob - row_delta)).astype(jnp.bfloat16)
        d_query_part = (
            jnp.einsum("hqk,khe->qhe", d_scores, keys, preferred_element_type=jnp.float32)
            * score_scale
        )
        d_keys = (
            d_keys
            + jnp.einsum("hqk,qhe->khe", d_scores, query_part, preferred_element_type=jnp.float32)
            * score_scale
        )
        d_values = d_values + jnp.einsum(
            "hqk,qhe->khe",
            probability.astype(jnp.bfloat16),
            d_context_part,
            preferred_element_type=jnp.float32,
        )
        return ((d_keys, d_values), d_query_part)

    zero_rows = jnp.zeros((seq_len, heads_here, HEAD), jnp.float32)
    (d_keys, d_values), d_query_blocks = lax.scan(
        backward_block,
        (zero_rows, zero_rows),
        (query_blocks, d_context_blocks, segment_blocks, place_blocks, log_totals),
    )
    d_query = d_query_blocks.reshape(seq_len, heads_here, HEAD)
    d_proj = jnp.stack(
        [
            rotated(d_query, cosine, sine, -1.0).reshape(seq_len, local_width),
            rotated(d_keys, cosine, sine, -1.0).reshape(seq_len, local_width),
            d_values.reshape(seq_len, local_width),
        ],
        axis=1,
    ).astype(jnp.bfloat16)
    d_w_qkv = jnp.einsum("sd,sje->dje", attn_rows, d_proj, preferred_element_type=jnp.float32)
    d_b_qkv = jnp.sum(d_proj, axis=0, dtype=jnp.float32).reshape(3, 1, local_width)
    grad_rows = cotangent.astype(jnp.float32)
    attn_term = jnp.einsum("sje,dje->sd", d_proj, w_qkv, preferred_element_type=jnp.float32)
    mlp_term = jnp.einsum("sf,df->sd", d_up, w_up, preferred_element_type=jnp.float32)
    stacked = lax.psum_scatter(
        jnp.stack([attn_term, mlp_term], axis=1), "tensor", scatter_dimension=0, tiled=True
    )
    d_attn_norm = stacked[:, 0]
    d_mlp_norm = stacked[:, 1]
    d_hat = d_attn_norm * gain_attn + d_mlp_norm * gain_mlp
    norm_sums = (
        jnp.sum(d_attn_norm * normalized, axis=0),
        jnp.sum(d_attn_norm, axis=0),
        jnp.sum(d_mlp_norm * normalized, axis=0),
        jnp.sum(d_mlp_norm, axis=0),
    )
    input_grad = grad_rows + inv_std * (
        d_hat
        - jnp.mean(d_hat, axis=-1, keepdims=True)
        - normalized * jnp.mean(d_hat * normalized, axis=-1, keepdims=True)
    )
    small_sums = (
        lax.psum_scatter(norm_sums[0], ("dp", "tensor"), scatter_dimension=0, tiled=True),
        lax.psum_scatter(norm_sums[1], ("dp", "tensor"), scatter_dimension=0, tiled=True),
        lax.psum_scatter(norm_sums[2], ("dp", "tensor"), scatter_dimension=0, tiled=True),
        lax.psum_scatter(norm_sums[3], ("dp", "tensor"), scatter_dimension=0, tiled=True),
        lax.psum_scatter(
            jnp.sum(grad_rows, axis=0), ("dp", "tensor"), scatter_dimension=0, tiled=True
        ),
    )
    summed = (
        lax.psum_scatter(d_w_qkv, "dp", scatter_dimension=0, tiled=True),
        lax.psum_scatter(d_b_qkv, "dp", scatter_dimension=2, tiled=True),
        lax.psum_scatter(d_w_out, "dp", scatter_dimension=1, tiled=True),
        lax.psum_scatter(unit_sums[0], "dp", scatter_dimension=0, tiled=True),
        lax.psum_scatter(unit_sums[1], "dp", scatter_dimension=1, tiled=True),
        lax.psum_scatter(unit_sums[2], "dp", scatter_dimension=1, tiled=True),
    )
    return (
        output,
        input_grad,
        small_sums[0],
        small_sums[1],
        small_sums[2],
        small_sums[3],
        summed[0],
        summed[1],
        summed[2],
        small_sums[4],
        summed[3],
        summed[4],
        summed[5],
        small_sums[4],
    )


def fits(n_dp, n_t, seq, rows, d, width, units):
    if n_dp != 16 or n_t < 2 or width != 512 or units != 2048 or width % 128 or units % width or rows % 128 or seq != rows * n_t:
        return False
    small = (d // (n_dp * n_t), width // n_dp, units // n_dp)
    if any(n < 1 or n > 128 or n & (n - 1) for n in small) or (d // n_dp) % 16:
        return False
    rows_of = 2 * (4 * seq * d + seq * (max(4, units // width) * width + 4 * width + units)) + 4 * seq * d
    chunks = 4 + 2 * (units // width)
    weights_of = 2 * chunks * d * width
    reduction = 2 * d * width * (2 + 2) + weights_of * 7 // 16 + 4 * chunks * (d // n_dp) * width
    exchange = 8 * (n_t - 1) * rows * d
    return rows_of + weights_of + reduction + exchange <= 54 << 20


def local(n_dp, n_t, *args):
    rows, d = args[0].shape
    seq, width, units = args[1].shape[0], args[6].shape[2], args[10].shape[1]
    if fits(n_dp, n_t, seq, rows, d, width, units):
        return fused(Sizes(n_dp, n_t, seq, rows, d, width, units), args)
    return plain(*args)


def solution(mesh):
    return jax.shard_map(
        functools.partial(local, mesh.shape["dp"], mesh.shape["tensor"]),
        mesh=mesh,
        in_specs=(
            P(("dp", "tensor"), None),
            P("dp"),
            P(("dp", "tensor")),
            P(("dp", "tensor")),
            P(("dp", "tensor")),
            P(("dp", "tensor")),
            P("dp", None, "tensor"),
            P(None, "tensor", "dp"),
            P("tensor", "dp"),
            P(("dp", "tensor")),
            P("dp", "tensor"),
            P("tensor", "dp"),
            P("tensor", "dp"),
            P(("dp", "tensor")),
            P(("dp", "tensor"), None),
        ),
        out_specs=(
            P(("dp", "tensor"), None),
            P(("dp", "tensor"), None),
            P(("dp", "tensor")),
            P(("dp", "tensor")),
            P(("dp", "tensor")),
            P(("dp", "tensor")),
            P("dp", None, "tensor"),
            P(None, "tensor", "dp"),
            P("tensor", "dp"),
            P(("dp", "tensor")),
            P("dp", "tensor"),
            P("tensor", "dp"),
            P("tensor", "dp"),
            P(("dp", "tensor")),
        ),
        check_vma=False,
    )
```

```python
import functools
import math

import jax
import jax.numpy as jnp
import numpy as np
from jax import lax
from jax.experimental import pallas as pl
from jax.experimental.pallas import tpu as pltpu
from jax.sharding import PartitionSpec as P

HEAD = 64
ROT = 16

EPSILON = 1e-05
NEGATIVE = -1e30
MESH = pl.DeviceIdType.MESH
F32 = jnp.float32
BF16 = jnp.bfloat16
NN = (((1,), (0,)), ((), ()))
NT = (((1,), (1,)), ((), ()))
TN = (((0,), (0,)), ((), ()))
VMEM_BYTES = 63 << 20


def dot(a, b, dims=NN):
    return lax.dot_general(a, b, dims, preferred_element_type=F32)


class Sizes:
    def __init__(self, n_dp, n_t, seq, rows, d, width, units):
        self.n_dp, self.n_t, self.seq, self.rows, self.d = n_dp, n_t, seq, rows, d
        self.width, self.units = width, units
        self.nz = n_dp // 4
        self.shard = d // n_dp
        self.nf = units // width
        self.chunks = 4 + 2 * self.nf
        self.block = min(256, rows)
        self.n_blocks = seq // self.block
        self.own_blocks = rows // self.block
        self.pairs = width // 128
        self.sums_width = max(d, 3 * width, units)
        self.p_slots = 2
        self.r_slots = 7
        self.ahead_y, self.ahead_z = 5, 3
        self.gather_z_last = ()
        self.reduce_y_last = ()
        self.halved = (10, 11)


def fused_kernel(sz, *refs):
    (
        x_hbm, g_hbm, qkv_hbm, outw_hbm, up_hbm, down_hbm, small_in, seg_ref, cos_ref, sin_ref,
        out_hbm, igrad_hbm, dqkv_ref, doutw_ref, dupw_ref, ddown_ref, small_out,
        xa, ga, ha, hm, stat, wts, sm, vec_d, vec_q, vec_u, pool, dqk, dvc, dup, acc, bias,
        part, red_c, red_y, red_z1, red_z2, b_send, b_recv, h_send, h_recv, sums_ref, sums_in,
        local_sem, w_sem, sm_s, sm_r, row_s, row_r, gz_s, gz_r, gy_s, gy_r, gc_s, gc_r,
        rc_s, rc_r, ry_s, ry_r, rz_s, rz_r, rh_s, rh_r, xt_s, xt_r, su_s, su_r, credit,
    ) = refs
    nz, r, D, W, S, R, T = sz.nz, sz.shard, sz.d, sz.width, sz.seq, sz.rows, sz.n_t
    nf, NCH = sz.nf, sz.chunks
    dp = lax.axis_index("dp")
    t = lax.axis_index("tensor")
    z, y, c = lax.div(dp, 4), lax.rem(lax.div(dp, 2), 2), lax.rem(dp, 2)

    def dev(z_, y_, c_, t_):
        return ((z_ * 2 + y_) * 2 + c_, t_)

    hi, lo = lax.div(z, 2), lax.rem(z, 2)
    far, near = dev((1 - hi) * 2 + lo, y, c, t), dev(hi * 2 + 1 - lo, y, c, t)
    z_peer = [dev(lax.rem(z + k, nz), y, c, t) for k in range(1, nz)]
    y_peer = dev(z, 1 - y, c, t)
    c_peer = dev(z, y, 1 - c, t)
    t_peer = [dev(z, y, c, lax.rem(t + k, T)) for k in range(1, T)]

    def remote(src, dst, s_sem, r_sem, to):
        return pltpu.make_async_remote_copy(
            src_ref=src, dst_ref=dst, send_sem=s_sem, recv_sem=r_sem, device_id=to, device_id_type=MESH
        )

    own = pl.ds(pl.multiple_of(t * R, R), R)

    Q = W // 2

    def shard_copies():
        copies = []

        def copy(src, ch, first, width):
            dst = wts.at[ch, hi, lo, y, c, :, pl.ds(first, width)]
            copies.append(pltpu.make_async_copy(src, dst, w_sem.at[len(copies)]))

        for g in range(2):
            mine_cols = pl.ds(g * Q, Q)
            copy(qkv_hbm.at[0, :, mine_cols], 2 * g, 0, Q)
            copy(qkv_hbm.at[1, :, mine_cols], 2 * g, Q, Q)
            copy(qkv_hbm.at[2, :, mine_cols], 2 * g + 1, 0, Q)
            copy(outw_hbm.at[:, mine_cols], 2 * g + 1, Q, Q)
        for f in range(nf):
            copy(up_hbm.at[:, pl.ds(f * W, W)], 4 + 2 * f, 0, W)
            copy(down_hbm.at[:, pl.ds(f * W, W)], 5 + 2 * f, 0, W)
        return copies

    cp_w = shard_copies()
    cp_x = pltpu.make_async_copy(x_hbm, xa.at[own], local_sem.at[1])
    cp_g = pltpu.make_async_copy(g_hbm, ga.at[own], local_sem.at[2])
    for cp in cp_w:
        cp.start()
    cp_x.start()
    cp_g.start()
    sm[z, y, c, t] = small_in[...]
    barrier = pltpu.get_barrier_semaphore()
    everyone = z_peer + [y_peer, c_peer] + t_peer
    for peer in everyone:
        pl.semaphore_signal(barrier, inc=1, device_id=peer, device_id_type=MESH)
    for cp in cp_w:
        cp.wait()
    cp_x.wait()
    cp_g.wait()
    pl.semaphore_wait(barrier, len(everyone))

    sm_t = [remote(sm.at[z, y, c, t], sm.at[z, y, c, t], sm_s.at[k], sm_r.at[k], t_peer[k]) for k in range(T - 1)]
    for cp in sm_t:
        cp.start()

    def one_of(ch, names):
        if isinstance(ch, int):
            return ch in names
        return functools.reduce(jnp.logical_or, [ch == n for n in names])

    def by_kind(ch, z_first, y_first):
        if not sz.gather_z_last:
            return z_first()
        kind = one_of(ch, sz.gather_z_last)
        if isinstance(ch, int):
            (y_first if kind else z_first)()
        else:
            pl.when(kind)(y_first)
            pl.when(jnp.logical_not(kind))(z_first)

    def g_far(ch, which=0):
        at = wts.at[ch, hi, lo, (1 - y) if which else y, c]
        return remote(at, at, gz_s.at[ch, which], gz_r.at[ch, which], far)

    def g_near(ch, which=0):
        at = wts.at[ch, hi, lo, (1 - y) if which else y, c]
        return remote(at, at, gz_s.at[ch, 2 + which], gz_r.at[ch, 2 + which], near)

    def g_pass(ch):
        at = wts.at[ch, 1 - hi, lo, y, c]
        return remote(at, at, gz_s.at[ch, 4], gz_r.at[ch, 4], near)

    def g_pass_both(ch):
        at = wts.at[ch, 1 - hi, lo, :, c]
        return remote(at, at, gz_s.at[ch, 4], gz_r.at[ch, 4], near)

    def gy(ch, which):
        at = (wts.at[ch, hi, lo, y, c], wts.at[ch, 1 - hi, lo, y, c], wts.at[ch, :, 1 - lo, y, c])[which]
        return remote(at, at, gy_s.at[ch, which], gy_r.at[ch, which], y_peer)

    def gc(ch):
        return remote(wts.at[ch, :, :, :, c], wts.at[ch, :, :, :, c], gc_s.at[ch], gc_r.at[ch], c_peer)

    def start_z(ch):
        g_far(ch).start()
        g_near(ch).start()

    start_z(0)
    for ch in range(sz.ahead_y):
        gy(ch, 0).start()
    row_x = [remote(xa.at[own], xa.at[own], row_s.at[0, k], row_r.at[0, k], t_peer[k]) for k in range(T - 1)]
    row_g = [remote(ga.at[own], ga.at[own], row_s.at[1, k], row_r.at[1, k], t_peer[k]) for k in range(T - 1)]
    for cp in row_x:
        cp.start()
    sm_z = [remote(sm.at[z, y, c], sm.at[z, y, c], sm_s.at[T - 1 + k], sm_r.at[T - 1 + k], z_peer[k]) for k in range(nz - 1)]
    sm_y = remote(sm.at[:, y, c], sm.at[:, y, c], sm_s.at[T + nz - 2], sm_r.at[T + nz - 2], y_peer)
    sm_c = remote(sm.at[:, :, c], sm.at[:, :, c], sm_s.at[T + nz - 1], sm_r.at[T + nz - 1], c_peer)
    tile = 128

    def stat_rows(first, count):
        def body(i, carry):
            rows = pl.ds(pl.multiple_of(first + i * tile, tile), tile)
            v = xa[rows, :].astype(F32)
            mean = jnp.mean(v, axis=-1, keepdims=True)
            cen = v - mean
            inv = lax.rsqrt(jnp.mean(cen * cen, axis=-1, keepdims=True) + EPSILON)
            stat[0, rows, :] = jnp.broadcast_to(mean, (tile, 128))
            stat[1, rows, :] = jnp.broadcast_to(inv, (tile, 128))
            return carry

        lax.fori_loop(0, count // tile, body, 0)

    stat_rows(t * R, R)
    for cp in sm_t:
        cp.wait_recv()
    for cp in sm_z:
        cp.start()

    def when(condition, act):
        if isinstance(condition, bool):
            if condition:
                act()
        else:
            pl.when(condition)(act)

    def on_z(e):
        def z_first():
            g_far(e).wait_recv()
            g_pass(e).start()
            gy(e, 1).start()

        def y_first():
            gy(e, 0).wait_recv()
            g_far(e, 1).start()
            g_near(e, 1).start()

        by_kind(e, z_first, y_first)

    def on_y(e):
        def z_first():
            g_near(e).wait_recv()
            g_pass(e).wait_recv()
            gy(e, 2).start()

        def y_first():
            g_far(e).wait_recv()
            g_far(e, 1).wait_recv()
            g_pass_both(e).start()

        by_kind(e, z_first, y_first)
        when(e + sz.ahead_z < NCH, lambda: start_z(e + sz.ahead_z))
        when(e + sz.ahead_y < NCH, lambda: gy(e + sz.ahead_y, 0).start())

    def on_c(e):
        def z_first():
            for which in range(3):
                gy(e, which).wait_recv()

        def y_first():
            g_near(e).wait_recv()
            g_near(e, 1).wait_recv()
            g_pass_both(e).wait_recv()

        by_kind(e, z_first, y_first)
        gc(e).start()

    def weights(ch):
        return wts[ch].reshape(D, W)

    def weight_half(ch, side):
        return wts[ch, :, :, :, :, :, side * Q : (side + 1) * Q].reshape(D, Q)

    def weight_rows_half(ch, i, side):
        return wts[ch, i, :, :, :, :, side * Q : (side + 1) * Q].reshape(D // 2, Q)

    def weight_rows(ch, i):
        return wts[ch, i].reshape(D // 2, W)

    on_z(0)
    for ch in range(1, sz.ahead_z):
        start_z(ch)
    for cp in sm_z:
        cp.wait_recv()
    sm_y.start()
    on_y(0)
    on_z(1)
    sm_y.wait_recv()
    sm_c.start()
    on_y(1)
    on_z(2)
    sm_c.wait_recv()

    flat = sm[...].reshape(sz.n_dp * T * 16, 128)
    n_rows = sz.n_dp * T * 16
    pick = (
        jnp.bitwise_and(lax.broadcasted_iota(jnp.int32, (16, n_rows), 1), 15)
        == lax.broadcasted_iota(jnp.int32, (16, n_rows), 0)
    ).astype(F32).astype(BF16)

    def lay_out(width, n, mine_only):
        shift = n.bit_length() - 1
        lane_of = lax.broadcasted_iota(jnp.int32, (128, width), 1)
        spread = (jnp.bitwise_and(lane_of, n - 1) == lax.broadcasted_iota(jnp.int32, (128, width), 0)).astype(F32).astype(BF16)
        wide = dot(flat, spread)
        piece = jnp.right_shift(lax.broadcasted_iota(jnp.int32, (n_rows, width), 1), shift)
        owner = jnp.right_shift(lax.broadcasted_iota(jnp.int32, (n_rows, width), 0), 4)
        if mine_only:
            piece = piece * T + t
        return dot(pick, jnp.where(piece == owner, wide, 0.0).astype(BF16))

    vec_d[...] = lay_out(D, D // (sz.n_dp * T), False)
    vec_q[...] = lay_out(W, W // sz.n_dp, True)
    def norm_rows(first, count):
        def body(i, carry):
            rows = pl.ds(pl.multiple_of(first + i * tile, tile), tile)
            norm = (xa[rows, :].astype(F32) - stat[0, rows, 0:1]) * stat[1, rows, 0:1]
            ha[rows, :] = (norm * vec_d[0:1, :] + vec_d[1:2, :]).astype(BF16)
            hm[rows, :] = (norm * vec_d[2:3, :] + vec_d[3:4, :]).astype(BF16)
            return carry

        lax.fori_loop(0, count // tile, body, 0)

    lane = lax.broadcasted_iota(jnp.int32, (1, 128), 1)
    low_half = lane < HEAD
    from_right = jnp.bitwise_and(lane, HEAD - 1) < ROT // 2
    big = min(512, R)
    scale = 1.0 / math.sqrt(HEAD)

    def turned(u, rows, sign):
        other = jnp.where(from_right, pltpu.roll(u, 128 - ROT // 2, 1), pltpu.roll(u, ROT // 2, 1))
        turn = other * sin_ref[rows, :]
        return u * cos_ref[rows, :] + (turn if sign > 0 else -turn)

    def project_qk(g, first):
        def body(i, carry):
            rows = pl.ds(pl.multiple_of(first + i * big, big), big)
            u = dot(ha[rows, :], weights(2 * g))
            for k in range(W // 128):
                side, at = divmod(k * 128, Q)
                part_u = u[:, k * 128 : (k + 1) * 128] + vec_q[6 + side : 7 + side, g * Q + at : g * Q + at + 128]
                part_u = turned(part_u, rows, 1)
                pool[2 * g, rows, k * 128 : (k + 1) * 128] = (part_u * scale if side == 0 else part_u).astype(BF16)
            return carry

        lax.fori_loop(0, R // big, body, 0)

    def project_v(g, first):
        def body(i, carry):
            rows = pl.ds(pl.multiple_of(first + i * big, big), big)
            u = dot(ha[rows, :], weight_half(2 * g + 1, 0)) + vec_q[8:9, g * Q : (g + 1) * Q]
            pool[2 * g + 1, rows, :Q] = u.astype(BF16)
            return carry

        lax.fori_loop(0, R // big, body, 0)

    def d_context(g, first):
        def body(i, carry):
            rows = pl.ds(pl.multiple_of(first + i * big, big), big)
            pool[2 * g + 1, rows, Q:] = dot(ga[rows, :], weight_half(2 * g + 1, 1)).astype(BF16)
            return carry

        lax.fori_loop(0, R // big, body, 0)

    norm_rows(t * R, R)
    for f in range(nf):
        vec_u[f] = lay_out_units(sz, flat, pick, n_rows, t, f)
    on_c(0)
    on_y(2)
    on_z(3)
    gc(0).wait_recv()
    project_qk(0, t * R)
    for k in range(1, T):
        row_x[k - 1].wait_recv()
        row_g[k - 1].start()
        first = lax.rem(t + T - k, T) * R
        stat_rows(first, R)
        norm_rows(first, R)
        project_qk(0, first)
    on_c(1)
    on_y(3)
    on_z(4)
    gc(1).wait_recv()
    for k in range(T):
        project_v(0, k * R)
    d_context(0, t * R)

    acc[...] = jnp.zeros_like(acc)

    def rc(i):
        return remote(
            part.at[lax.rem(i, sz.p_slots), :, :, :, 1 - c], red_c.at[lax.rem(i, sz.r_slots)], rc_s.at[i], rc_r.at[i], c_peer
        )

    def r1(i):
        at = red_c.at[lax.rem(i, sz.r_slots)]
        src, to = (at.at[:, 1 - lo], near) if i in sz.reduce_y_last else (at.at[:, :, 1 - y], y_peer)
        return remote(src, red_y.at[i], ry_s.at[i], ry_r.at[i], to)

    def r2(i):
        src, to = (red_y.at[i, 1 - hi], far) if i in sz.reduce_y_last else (red_y.at[i, :, 1 - lo], near)
        return remote(src, red_z1.at[i], rz_s.at[i, 0], rz_r.at[i, 0], to)

    def part_of(half):
        return hi if half else 1 - hi

    def r1_half(i, half):
        at = part_of(half)
        src = red_c.at[lax.rem(i, sz.r_slots), at, :, 1 - y]
        return remote(src, red_y.at[i, at], rh_s.at[i, half], rh_r.at[i, half], y_peer)

    def r2_half(i, half):
        at = part_of(half)
        return remote(red_y.at[i, at, 1 - lo], red_z1.at[i, at], rh_s.at[i, 2 + half], rh_r.at[i, 2 + half], near)

    def event_y_half(i, half):
        r1_half(i, half).wait()
        at = part_of(half)
        kept = red_c[lax.rem(i, sz.r_slots), at, :, y]
        red_y[i, at] = (kept.astype(F32) + red_y[i, at].astype(F32)).astype(BF16)
        r2_half(i, half).start()

    def event_n_half(i, half):
        r2_half(i, half).wait()
        at = part_of(half)
        red_y[i, at, lo] = (red_y[i, at, lo].astype(F32) + red_z1[i, at].astype(F32)).astype(BF16)
        if half == 0:
            r3(i).start()

    def r3(i):
        src, to = (red_y.at[i, hi, 1 - y], y_peer) if i in sz.reduce_y_last else (red_y.at[i, 1 - hi, lo], far)
        return remote(src, red_z2.at[i], rz_s.at[i, 1], rz_r.at[i, 1], to)

    def emit(i, left, right):
        slot = lax.rem(i, sz.p_slots)

        def body(n, carry):
            cols = pl.ds(pl.multiple_of(n * (D // 2), D // 2), D // 2)
            made = dot(left[:, cols], right[...], TN)
            part[slot, n] = made.astype(BF16).reshape(2, 2, 2, r, W)
            return carry

        lax.fori_loop(0, 2, body, 0)
        send(i)

    def emit_heads(i, g):
        slot = lax.rem(i, sz.p_slots)

        def body(n, carry):
            cols = pl.ds(pl.multiple_of(n * (D // 2), D // 2), D // 2)
            for side, left in enumerate((ha, ga)):
                right = dvc[g, :, side * Q : (side + 1) * Q]
                made = dot(left[:, cols], right, TN).astype(BF16).reshape(2, 2, 2, r, Q)
                part[slot, n, :, :, :, :, side * Q : (side + 1) * Q] = made
            return carry

        lax.fori_loop(0, 2, body, 0)
        send(i)

    def send(i):
        if i >= sz.r_slots:
            pl.semaphore_wait(credit, 1)
        rc(i).start()

    def event_c(i):
        rc(i).wait()
        slot, rslot = lax.rem(i, sz.p_slots), lax.rem(i, sz.r_slots)
        red_c[rslot] = (part[slot, :, :, :, c].astype(F32) + red_c[rslot].astype(F32)).astype(BF16)
        if i in sz.halved:
            r1_half(i, 0).start()
            r1_half(i, 1).start()
        else:
            r1(i).start()

    def event_y(i):
        r1(i).wait()
        rslot = lax.rem(i, sz.r_slots)
        kept = red_c[rslot, :, lo] if i in sz.reduce_y_last else red_c[rslot, :, :, y]
        red_y[i] = (kept.astype(F32) + red_y[i].astype(F32)).astype(BF16)
        if i < NCH - sz.r_slots:
            pl.semaphore_signal(credit, inc=1, device_id=c_peer, device_id_type=MESH)
        r2(i).start()

    def event_n(i):
        r2(i).wait()
        if i in sz.reduce_y_last:
            red_y[i, hi] = (red_y[i, hi].astype(F32) + red_z1[i].astype(F32)).astype(BF16)
        else:
            red_y[i, :, lo] = (red_y[i, :, lo].astype(F32) + red_z1[i].astype(F32)).astype(BF16)
        r3(i).start()

    def event_z(i, late=False):
        if (i in sz.reduce_y_last) != late:
            return
        r3(i).wait()
        kept = red_y[i, hi, y] if i in sz.reduce_y_last else red_y[i, hi, lo]
        total = kept.astype(F32) + red_z2[i].astype(F32)
        g = i // 2
        if i < 4 and i % 2 == 0:
            dqkv_ref[0, :, g * Q : (g + 1) * Q] = total[:, :Q]
            dqkv_ref[1, :, g * Q : (g + 1) * Q] = total[:, Q:]
        elif i < 4:
            dqkv_ref[2, :, g * Q : (g + 1) * Q] = total[:, :Q]
            doutw_ref[:, g * Q : (g + 1) * Q] = total[:, Q:]
        else:
            (dupw_ref, ddown_ref)[i % 2][:, (g - 2) * W : (g - 1) * W] = total

    sums_ref[...] = jnp.zeros_like(sums_ref)

    def row_sum(v):
        return jnp.sum(v.astype(F32), axis=0, keepdims=True)

    def mlp(first, count, f, act):
        def body(i, carry):
            rows = pl.ds(pl.multiple_of(first + i * big, big), big)
            u = dot(hm[rows, :], weights(4 + 2 * f)) + vec_u[f, 9:10, :]
            cdf = 0.5 + 0.5 * lax.erf(u * math.sqrt(0.5))
            act[rows, :] = (u * cdf).astype(BF16)
            slope = cdf + u * (jnp.exp(u * u * -0.5) * (1.0 / math.sqrt(2.0 * math.pi)))
            back = slope * dot(ga[rows, :], weights(5 + 2 * f))
            dup[f, rows, :] = back.astype(BF16)
            return carry

        lax.fori_loop(0, count // big, body, 0)

    def emit_units(i):
        f = (i - 4) // 2
        if i % 2:
            emit(i, ga, pool.at[f])
        else:
            emit(i, hm, dup.at[f])

    B = sz.block
    n_pairs = Q // 128
    steps = 2 * sz.n_blocks
    own_steps = 2 * sz.own_blocks

    def attend(qb, g, step):
        L = (qb + 1) * B
        rows = pl.ds(qb * B, B)
        for s in range(B // 128):
            here = pl.ds(s * 128, 128)
            start = jnp.broadcast_to(seg_ref[0:1, qb * B + s * 128 : qb * B + (s + 1) * 128].astype(F32), (128, 128)).T
            start = start[:, 0:1].astype(jnp.int32)
            key_at = lax.broadcasted_iota(jnp.int32, (128, L), 1)
            row_at = lax.broadcasted_iota(jnp.int32, (128, L), 0) + (qb * B + s * 128)
            bias[here, :L] = jnp.where((key_at >= start) & (key_at <= row_at), 0.0, NEGATIVE)

        def pair(p, carry):
            cols = pl.ds(pl.multiple_of(p * 128, 128), 128)
            cols_2 = pl.ds(pl.multiple_of(Q + p * 128, 128), 128)
            query, keys = pool[2 * g, rows, cols], pool[2 * g, :L, cols_2]
            values, d_ctx = pool[2 * g + 1, :L, cols], pool[2 * g + 1, rows, cols_2]
            made = []
            for h in range(2):
                mine = low_half if h == 0 else jnp.logical_not(low_half)
                q_h = jnp.where(mine, query, jnp.zeros_like(query))
                d_h = jnp.where(mine, d_ctx, jnp.zeros_like(d_ctx))
                scores = dot(q_h, keys, NT) + bias[:, :L]
                top = jnp.max(scores, axis=1, keepdims=True)
                e = jnp.exp(scores - top)
                prob = e * (1.0 / jnp.sum(e, axis=1, keepdims=True))
                d_prob = dot(d_h, values, NT)
                delta = jnp.sum(prob * d_prob, axis=1, keepdims=True)
                d_s = (prob * (d_prob - delta)).astype(BF16)
                p_b = prob.astype(BF16)
                made.append((dot(p_b, values), dot(d_s, keys), dot(d_s, q_h, TN), dot(p_b, d_h, TN)))
            dvc[g, rows, cols_2] = jnp.where(low_half, made[0][0], made[1][0]).astype(BF16)
            d_q = jnp.where(low_half, made[0][1], made[1][1]) * scale
            dqk[g, rows, cols] = turned(d_q, rows, -1).astype(BF16)
            cols_k = pl.ds(pl.multiple_of(g * Q + p * 128, 128), 128)
            cols_v = pl.ds(pl.multiple_of(W + g * Q + p * 128, 128), 128)
            acc[:L, cols_k] += made[0][2] + made[1][2]
            acc[:L, cols_v] += made[0][3] + made[1][3]
            at = step * n_pairs + p

            def poll():
                turn = lax.div(at, 2)
                e = 4 + turn + jnp.where(turn >= 2, 1, 0)
                on_z(e + 1)
                on_y(e)
                on_c(e - 2)

            pl.when((lax.rem(at, 2) == 0) & (at <= 10))(poll)
            pl.when(at == 12)(lambda: on_c(10))
            return carry

        lax.fori_loop(0, n_pairs, pair, 0)

    def finish_group(g):
        def body(i, carry):
            rows = pl.ds(pl.multiple_of(i * tile, tile), tile)
            for k in range(n_pairs):
                cols = pl.ds(g * Q + k * 128, 128)
                dqk[g, rows, pl.ds(Q + k * 128, 128)] = turned(acc[rows, cols], rows, -1).astype(BF16)
            dvc[g, rows, :Q] = acc[rows, pl.ds(W + g * Q, Q)].astype(BF16)
            return carry

        lax.fori_loop(0, S // tile, body, 0)
        emit(2 * g, ha, dqk.at[g])
        if g == 0:
            on_y(11)
            on_c(9)
        emit_heads(2 * g + 1, g)
        event_c(2 * g)
        sums_ref[5:6, g * Q : (g + 1) * Q] = row_sum(dqk[g, :, :Q])
        sums_ref[5:6, W + g * Q : W + (g + 1) * Q] = row_sum(dqk[g, :, Q:])
        sums_ref[5:6, 2 * W + g * Q : 2 * W + (g + 1) * Q] = row_sum(dvc[g, :, :Q])

    other_blocks = sz.n_blocks - sz.own_blocks

    def block_step(step, carry):
        def second_group():
            gc(2).wait_recv()
            gc(3).wait_recv()
            for k in range(T):
                project_qk(1, k * R)
            on_z(7)
            on_y(6)
            on_c(4)
            for k in range(T):
                project_v(1, k * R)
            d_context(1, t * R)

        def other_rows():
            for k in range(1, T):
                row_g[k - 1].wait_recv()
                for g in range(2):
                    d_context(g, lax.rem(t + T - k, T) * R)

        pl.when(step == sz.own_blocks)(second_group)
        pl.when(step == own_steps)(other_rows)
        pl.when(step == own_steps + other_blocks)(lambda: finish_group(0))
        later = step >= own_steps
        count = jnp.where(later, other_blocks, sz.own_blocks)
        at = jnp.where(later, step - own_steps, step)
        g = lax.div(at, count)
        j = lax.rem(at, count) + jnp.where(later, sz.own_blocks, 0)
        which = lax.rem(j + t * sz.own_blocks, sz.n_blocks)
        for qb in range(sz.n_blocks):
            pl.when(which == qb)(functools.partial(attend, qb, g, step))
        return carry

    lax.fori_loop(0, steps, block_step, 0)
    event_c(1)
    on_c(11)
    finish_group(1)

    half = D // 2

    def branch(first, i, n):
        rows = pl.ds(pl.multiple_of(first + i * big, big), big)
        total = dot(pool[0, rows, :], weight_rows(5, n), NT)
        for f in range(1, nf):
            total = total + dot(pool[f, rows, :], weight_rows(5 + 2 * f, n), NT)
        for g in range(2):
            total = total + dot(dvc[g, rows, Q:], weight_rows_half(2 * g + 1, n, 1), NT)
        return total

    def d_hidden(first, i, n):
        rows = pl.ds(pl.multiple_of(first + i * big, big), big)
        cols = pl.ds(pl.multiple_of(n * half, half), half)
        d_attn = dot(dqk[0, rows, :], weight_rows(0, n), NT) + dot(dqk[1, rows, :], weight_rows(2, n), NT)
        for g in range(2):
            d_attn = d_attn + dot(dvc[g, rows, :Q], weight_rows_half(2 * g + 1, n, 0), NT)
        d_mlp = dot(dup[0, rows, :], weight_rows(4, n), NT)
        for f in range(1, nf):
            d_mlp = d_mlp + dot(dup[f, rows, :], weight_rows(4 + 2 * f, n), NT)
        norm = (xa[rows, cols].astype(F32) - stat[0, rows, 0:1]) * stat[1, rows, 0:1]
        sums_ref[0:1, cols] += row_sum(d_attn * norm)
        sums_ref[1:2, cols] += row_sum(d_attn)
        sums_ref[2:3, cols] += row_sum(d_mlp * norm)
        sums_ref[3:4, cols] += row_sum(d_mlp)
        return d_attn * vec_d[0:1, cols] + d_mlp * vec_d[2:3, cols]

    def xt(which, k):
        src, dst = ((b_send, b_recv), (h_send, h_recv))[which]
        return remote(src.at[k], dst.at[k], xt_s.at[which, k], xt_r.at[which, k], t_peer[k])

    def events(i_y, i_n, i_z):
        if i_y is not None:
            event_y(i_y)
        if i_n is not None:
            event_n(i_n)
        if i_z is not None:
            event_z(i_z)

    for k in range(T - 1):
        first = lax.rem(t + k + 1, T) * R

        def other_units(f, carry, first=first, k=k):
            if k == 0:
                gc(4 + 2 * f).wait_recv()
                gc(5 + 2 * f).wait_recv()
            mlp(first, R, f, pool.at[f])
            return carry

        lax.fori_loop(0, nf, other_units, 0)
    event_c(3)
    event_y(0)
    for k in range(T - 1):
        first = lax.rem(t + k + 1, T) * R

        def both(q, carry, first=first, k=k):
            i, n = lax.div(q, 2), lax.rem(q, 2)
            cols = pl.ds(pl.multiple_of(n * half, half), half)
            rows = pl.ds(pl.multiple_of(i * big, big), big)
            b_send[k, rows, cols] = branch(first, i, n).astype(BF16)
            return carry

        lax.fori_loop(0, 2 * (R // big), both, 0)
        xt(0, k).start()
    event_y(1)
    mlp(t * R, R, 0, pool.at[0])
    emit_units(4)
    event_n(0)
    emit_units(5)
    event_c(4)
    event_y(2)
    for k in range(T - 1):
        first = lax.rem(t + k + 1, T) * R

        def both_back(q, carry, first=first, k=k):
            i, n = lax.div(q, 2), lax.rem(q, 2)
            cols = pl.ds(pl.multiple_of(n * half, half), half)
            rows = pl.ds(pl.multiple_of(i * big, big), big)
            h_send[k, rows, cols] = d_hidden(first, i, n).astype(BF16)
            return carry

        lax.fori_loop(0, 2 * (R // big), both_back, 0)
        xt(1, k).start()
    event_c(5)
    events(3, 1, None)
    mlp(t * R, R, 1, pool.at[1])
    emit_units(6)
    event_n(2)
    emit_units(7)
    event_c(6)
    event_y(4)
    mlp(t * R, R, 2, pool.at[2])
    event_c(7)
    mlp(t * R, R, 3, pool.at[3])
    events(5, 3, None)

    def own_back(q, carry):
        i, n = lax.div(q, 2), lax.rem(q, 2)
        cols = pl.ds(pl.multiple_of(n * half, half), half)
        acc[pl.ds(pl.multiple_of(R + i * big, big), big), cols] = d_hidden(t * R, i, n)
        return carry

    lax.fori_loop(0, 2 * (R // big), own_back, 0)
    sums_ref[4:5, :D] = row_sum(ga[own, :])
    for f in range(nf):
        sums_ref[6:7, f * W : (f + 1) * W] = row_sum(dup[f])

    su_c = remote(sums_ref, sums_in.at[0], su_s.at[0], su_r.at[0], c_peer)
    su_y = remote(sums_ref, sums_in.at[3], su_s.at[3], su_r.at[3], y_peer)
    su_n = remote(sums_ref, sums_in.at[1], su_s.at[1], su_r.at[1], near)
    su_f = remote(sums_ref, sums_in.at[2], su_s.at[2], su_r.at[2], far)
    su_t = [remote(sums_ref, sums_in.at[4 + k], su_s.at[4 + k], su_r.at[4 + k], t_peer[k]) for k in range(T - 1)]
    stages = (su_c, su_n, su_f, su_y)

    def sums_step(n):
        if n < 4:
            stages[n].wait()
            sums_ref[...] += sums_in[n]
        if n < 3:
            stages[n + 1].start()
        elif n == 3:
            for cp in su_t:
                cp.start()
        else:
            for cp in su_t:
                cp.wait()
            for k in range(T - 1):
                sums_ref[0:5, :] += sums_in[4 + k, 0:5, :]

    def mine(row, first, width, n, at):
        part_row = jnp.broadcast_to(sums_ref[row : row + 1, first : first + width], (8, width))
        return pltpu.roll(part_row, lax.rem(width - at, width), 1)[0:1, 0:128]

    def finish_out(i, carry):
        rows = pl.ds(pl.multiple_of(i * tile, tile), tile)
        here = pl.ds(pl.multiple_of(t * R + i * tile, tile), tile)
        total = xa[here, :].astype(F32) + acc[rows, :] + (vec_d[4:5, :] + vec_d[5:6, :])
        for k in range(T - 1):
            total = total + b_recv[k, rows, :].astype(F32)
        b_send[0, rows, :] = total.astype(BF16)
        return carry

    def finish_grad(i, carry):
        rows = pl.ds(pl.multiple_of(R + i * tile, tile), tile)
        there = pl.ds(pl.multiple_of(i * tile, tile), tile)
        here = pl.ds(pl.multiple_of(t * R + i * tile, tile), tile)
        inv = stat[1, here, 0:1]
        norm = (xa[here, :].astype(F32) - stat[0, here, 0:1]) * inv
        d_hat = acc[rows, :]
        for k in range(T - 1):
            d_hat = d_hat + h_recv[k, there, :].astype(F32)
        inner = jnp.mean(d_hat * norm, axis=-1, keepdims=True)
        acc[rows, :] = ga[here, :].astype(F32) + inv * (d_hat - jnp.mean(d_hat, axis=-1, keepdims=True) - norm * inner)
        return carry

    su_c.start()
    event_n(4)
    emit_units(8)
    sums_step(0)
    emit_units(9)
    event_c(8)
    event_y(6)
    emit_units(10)
    event_c(9)
    event_n(5)
    emit_units(11)
    event_c(10)
    event_y(7)
    sums_step(1)
    event_c(11)

    def own_both(q, carry):
        i, n = lax.div(q, 2), lax.rem(q, 2)
        cols = pl.ds(pl.multiple_of(n * half, half), half)
        acc[pl.ds(pl.multiple_of(i * big, big), big), cols] = branch(t * R, i, n)
        return carry

    lax.fori_loop(0, 2 * (R // big), own_both, 0)
    events(8, 6, 0)
    sums_step(2)
    event_n(7)
    event_z(1)
    event_z(2)
    event_z(3)

    for k in range(T - 1):
        xt(0, k).wait()
    lax.fori_loop(0, R // tile, finish_out, 0)
    cp_out = pltpu.make_async_copy(b_send.at[0], out_hbm, local_sem.at[3])
    cp_out.start()
    event_y(9)
    event_n(8)
    event_z(4)
    event_z(5)
    event_y_half(10, 0)
    event_z(6)
    event_y_half(10, 1)
    event_n(9)
    event_z(7)
    event_n_half(10, 0)
    event_y_half(11, 0)
    event_z(8)
    event_n_half(10, 1)
    event_y_half(11, 1)
    sums_step(3)
    event_n_half(11, 0)
    for k in range(T - 1):
        xt(1, k).wait()
    lax.fori_loop(0, R // tile, finish_grad, 0)
    cp_grad = pltpu.make_async_copy(acc.at[pl.ds(R, R)], igrad_hbm, local_sem.at[4])
    cp_grad.start()
    event_z(9)
    event_n_half(11, 1)
    sums_step(4)
    n_d, n_q, n_u = D // (sz.n_dp * T), W // sz.n_dp, sz.units // sz.n_dp
    small_out[...] = jnp.zeros_like(small_out)
    for k in range(5):
        small_out[k : k + 1, :] = mine(k, 0, D, n_d, (dp * T + t) * n_d)
    for j in range(3):
        small_out[5 + j : 6 + j, :] = mine(5, j * W, W, n_q, dp * n_q)
    small_out[8:9, :] = mine(6, 0, sz.units, n_u, dp * n_u)
    event_z(10)
    event_z(11)

    for cp in sm_t + sm_z + [sm_y, sm_c] + row_x + row_g:
        cp.wait_send()

    def sent(ch, carry):
        for copy in (g_far(ch), gy(ch, 0), g_near(ch), gc(ch)):
            copy.wait_send()

        def z_first():
            for copy in (g_pass(ch), gy(ch, 1), gy(ch, 2)):
                copy.wait_send()

        def y_first():
            for copy in (g_far(ch, 1), g_near(ch, 1), g_pass_both(ch)):
                copy.wait_send()

        by_kind(ch, z_first, y_first)
        return carry

    lax.fori_loop(0, NCH, sent, 0)
    cp_out.wait()
    cp_grad.wait()


def hand_out(n, nq, nu, *refs):
    large, small, out_large, out_small, held, sems = refs[:6], refs[6], refs[7:13], refs[13:21], refs[21:27], refs[27]
    into = [pltpu.make_async_copy(large[k], held[k], sems.at[0, k]) for k in range(6)]
    out = [pltpu.make_async_copy(held[k], out_large[k], sems.at[1, k]) for k in range(6)]
    for cp in into:
        cp.start()
    for k in range(5):
        out_small[k][...] = small[k : k + 1, :n]
    out_small[5][...] = small[4:5, :n]
    for j in range(3):
        out_small[6][j] = small[5 + j : 6 + j, :nq]
    out_small[7][...] = small[8:9, :nu]
    for k in range(6):
        into[k].wait()
        out[k].start()
    for cp in out:
        cp.wait()


def lay_out_units(sz, flat, pick, n_rows, t, f):
    n = sz.units // sz.n_dp
    shift = n.bit_length() - 1
    W = sz.width
    lane_of = lax.broadcasted_iota(jnp.int32, (128, W), 1) + f * W
    spread = (jnp.bitwise_and(lane_of, n - 1) == lax.broadcasted_iota(jnp.int32, (128, W), 0)).astype(F32).astype(BF16)
    wide = dot(flat, spread)
    piece = jnp.right_shift(lax.broadcasted_iota(jnp.int32, (n_rows, W), 1) + f * W, shift) * sz.n_t + t
    owner = jnp.right_shift(lax.broadcasted_iota(jnp.int32, (n_rows, W), 0), 4)
    return dot(pick, jnp.where(piece == owner, wide, 0.0).astype(BF16))


def fused(sz, args):
    (
        inputs, segment_ids, ln_attn_gain, ln_attn_bias, ln_mlp_gain, ln_mlp_bias, qkv_weight, qkv_bias,
        out_weight, out_bias, up_weight, up_bias, down_weight, down_bias, cotangent,
    ) = args
    nz, r, D, W, S, R, T, nf, NCH = sz.nz, sz.shard, sz.d, sz.width, sz.seq, sz.rows, sz.n_t, sz.nf, sz.chunks

    def placed(v, first):
        return jnp.pad(v, ((first, 16 - first - v.shape[0]), (0, 128 - v.shape[1])))

    vectors = (ln_attn_gain, ln_attn_bias, ln_mlp_gain, ln_mlp_bias, out_bias, down_bias)
    small = placed(qkv_bias[:, 0], 6) + placed(up_bias, 9)
    for k, v in enumerate(vectors):
        small = small + placed(v[None], k)
    half_rot = ROT // 2
    place = np.arange(S, dtype=np.float32)
    inverse = (10000.0 ** (-(2.0 * np.arange(half_rot, dtype=np.float32)) / ROT)).astype(np.float32)
    theta = place[:, None] * inverse[None, :]
    cos, sin = np.cos(theta), np.sin(theta)
    cos_head = np.concatenate([cos, cos, np.ones((S, HEAD - ROT), np.float32)], axis=1)
    sin_head = np.concatenate([-sin, sin, np.zeros((S, HEAD - ROT), np.float32)], axis=1)
    cos_table = jnp.asarray(np.tile(cos_head, (1, 128 // HEAD)), F32)
    sin_table = jnp.asarray(np.tile(sin_head, (1, 128 // HEAD)), F32)

    hbm = pl.BlockSpec(memory_space=pl.ANY)
    vmem = pl.BlockSpec(memory_space=pltpu.VMEM)
    sw = sz.sums_width
    dma = pltpu.SemaphoreType.DMA
    n_small = T - 1 + nz - 1 + 2
    scratch = [
        pltpu.VMEM((S, D), BF16),
        pltpu.VMEM((S, D), BF16),
        pltpu.VMEM((S, D), BF16),
        pltpu.VMEM((S, D), BF16),
        pltpu.VMEM((2, S, 128), F32),
        pltpu.VMEM((NCH, 2, 2, 2, 2, r, W), BF16),
        pltpu.VMEM((nz, 2, 2, T, 16, 128), BF16),
        pltpu.VMEM((16, D), F32),
        pltpu.VMEM((16, W), F32),
        pltpu.VMEM((nf, 16, W), F32),
        pltpu.VMEM((max(4, nf), S, W), BF16),
        pltpu.VMEM((2, S, W), BF16),
        pltpu.VMEM((2, S, W), BF16),
        pltpu.VMEM((nf, S, W), BF16),
        pltpu.VMEM((S, D), F32),
        pltpu.VMEM((sz.block, S), F32),
        pltpu.VMEM((sz.p_slots, 2, 2, 2, 2, r, W), BF16),
        pltpu.VMEM((sz.r_slots, 2, 2, 2, r, W), BF16),
        pltpu.VMEM((NCH, 2, 2, r, W), BF16),
        pltpu.VMEM((NCH, 2, r, W), BF16),
        pltpu.VMEM((NCH, r, W), BF16),
        pltpu.VMEM((T - 1, R, D), BF16),
        pltpu.VMEM((T - 1, R, D), BF16),
        pltpu.VMEM((T - 1, R, D), BF16),
        pltpu.VMEM((T - 1, R, D), BF16),
        pltpu.VMEM((8, sw), F32),
        pltpu.VMEM((3 + T, 8, sw), F32),
        dma((5,)), dma((8 + 2 * nf,)),
        dma((n_small,)), dma((n_small,)),
        dma((2, T - 1)), dma((2, T - 1)),
        dma((NCH, 5)), dma((NCH, 5)),
        dma((NCH, 3)), dma((NCH, 3)),
        dma((NCH,)), dma((NCH,)),
        dma((NCH,)), dma((NCH,)),
        dma((NCH,)), dma((NCH,)),
        dma((NCH, nz - 1)), dma((NCH, nz - 1)),
        dma((NCH, 4)), dma((NCH, 4)),
        dma((2, T - 1)), dma((2, T - 1)),
        dma((3 + T,)), dma((3 + T,)),
        pltpu.SemaphoreType.REGULAR,
    ]
    units = sz.units
    output, input_grad, d_qkv, d_out, d_up, d_down, small_sums = pl.pallas_call(
        functools.partial(fused_kernel, sz),
        out_shape=(
            jax.ShapeDtypeStruct((R, D), BF16),
            jax.ShapeDtypeStruct((R, D), F32),
            jax.ShapeDtypeStruct((3, r, W), F32),
            jax.ShapeDtypeStruct((r, W), F32),
            jax.ShapeDtypeStruct((r, units), F32),
            jax.ShapeDtypeStruct((r, units), F32),
            jax.ShapeDtypeStruct((16, 128), F32),
        ),
        in_specs=[hbm, hbm, hbm, hbm, hbm, hbm, vmem, vmem, vmem, vmem],
        out_specs=(hbm, hbm, vmem, vmem, vmem, vmem, vmem),
        scratch_shapes=scratch,
        compiler_params=pltpu.CompilerParams(collective_id=0, has_side_effects=True, vmem_limit_bytes=VMEM_BYTES),
    )(
        inputs, cotangent, qkv_weight.transpose(1, 0, 2), out_weight.T, up_weight, down_weight.T, small,
        segment_ids.reshape(1, S), cos_table, sin_table,
    )

    n, nq, nu = D // (sz.n_dp * T), W // sz.n_dp, units // sz.n_dp
    large = (output, input_grad, d_qkv, d_out, d_up, d_down)
    outs = pl.pallas_call(
        functools.partial(hand_out, n, nq, nu),
        out_shape=[jax.ShapeDtypeStruct(v.shape, v.dtype) for v in large]
        + [jax.ShapeDtypeStruct((1, n), F32)] * 6
        + [jax.ShapeDtypeStruct((3, 1, nq), F32), jax.ShapeDtypeStruct((1, nu), F32)],
        in_specs=[hbm] * 6 + [vmem],
        out_specs=[hbm] * 6 + [vmem] * 8,
        scratch_shapes=[pltpu.VMEM(v.shape, v.dtype) for v in large] + [dma((2, 6))],
    )(*large, small_sums)
    output, input_grad, d_qkv, d_out, d_up, d_down = outs[:6]
    vectors = [v.reshape(n) for v in outs[6:12]]
    return (
        output, input_grad, vectors[0], vectors[1], vectors[2], vectors[3],
        d_qkv.transpose(1, 0, 2), outs[12], d_out.T, vectors[4], d_up, outs[13], d_down.T, vectors[5],
    )


def rotated(values, cosine, sine, sign):
    half_rot = ROT // 2
    first_half = values[..., :half_rot]
    second_half = values[..., half_rot:ROT]
    new_first = first_half * cosine - sign * second_half * sine
    new_second = second_half * cosine + sign * first_half * sine
    return jnp.concatenate([new_first, new_second, values[..., ROT:]], axis=-1)


def angle_tables(length):
    position = jnp.arange(length).astype(jnp.float32)
    inverse = 10000.0 ** (-(2.0 * jnp.arange(ROT // 2).astype(jnp.float32)) / ROT)
    theta = position[:, None] * inverse[None, :]
    return (jnp.cos(theta)[:, None, :], jnp.sin(theta)[:, None, :])


def gelu_exact(value):
    return jax.nn.gelu(value, approximate=False)


def layer_norm(rows):
    centred = rows - jnp.mean(rows, axis=-1, keepdims=True)
    inv_std = lax.rsqrt(jnp.mean(centred * centred, axis=-1, keepdims=True) + EPSILON)
    return (centred * inv_std, inv_std)


def plain(
    inputs,
    segment_ids,
    ln_attn_gain,
    ln_attn_bias,
    ln_mlp_gain,
    ln_mlp_bias,
    qkv_weight,
    qkv_bias,
    out_weight,
    out_bias,
    up_weight,
    up_bias,
    down_weight,
    down_bias,
    cotangent,
):
    seq_len = segment_ids.shape[0]
    norm_terms = (
        lax.all_gather(ln_attn_gain, ("dp", "tensor"), axis=0, tiled=True),
        lax.all_gather(ln_attn_bias, ("dp", "tensor"), axis=0, tiled=True),
        lax.all_gather(ln_mlp_gain, ("dp", "tensor"), axis=0, tiled=True),
        lax.all_gather(ln_mlp_bias, ("dp", "tensor"), axis=0, tiled=True),
        lax.all_gather(out_bias, ("dp", "tensor"), axis=0, tiled=True),
        lax.all_gather(down_bias, ("dp", "tensor"), axis=0, tiled=True),
    )
    gain_attn = norm_terms[0].astype(jnp.float32)
    shift_attn = norm_terms[1].astype(jnp.float32)
    gain_mlp = norm_terms[2].astype(jnp.float32)
    shift_mlp = norm_terms[3].astype(jnp.float32)
    bias_sum = norm_terms[4].astype(jnp.float32) + norm_terms[5].astype(jnp.float32)
    w_qkv, b_qkv, w_out, w_up, b_up, w_down = (
        lax.all_gather(qkv_weight, "dp", axis=0, tiled=True),
        lax.all_gather(qkv_bias, "dp", axis=2, tiled=True),
        lax.all_gather(out_weight, "dp", axis=1, tiled=True),
        lax.all_gather(up_weight, "dp", axis=0, tiled=True),
        lax.all_gather(up_bias, "dp", axis=1, tiled=True),
        lax.all_gather(down_weight, "dp", axis=1, tiled=True),
    )
    local_width = w_qkv.shape[2]
    heads_here = local_width // HEAD
    score_scale = 1.0 / math.sqrt(HEAD)
    resid = inputs.astype(jnp.float32)
    normalized, inv_std = layer_norm(resid)
    whole_inputs = lax.all_gather(inputs, "tensor", axis=0, tiled=True)
    normal_all, unused_std = layer_norm(whole_inputs.astype(jnp.float32))
    attn_rows = (normal_all * gain_attn + shift_attn).astype(jnp.bfloat16)
    mlp_rows = (normal_all * gain_mlp + shift_mlp).astype(jnp.bfloat16)
    proj = jnp.einsum("sd,dje->sje", attn_rows, w_qkv, preferred_element_type=jnp.float32)
    proj = proj + b_qkv.astype(jnp.float32).reshape(1, 3, local_width)
    cosine, sine = angle_tables(seq_len)
    query = rotated(proj[:, 0].reshape(seq_len, heads_here, HEAD), cosine, sine, 1.0).astype(
        jnp.bfloat16
    )
    keys = rotated(proj[:, 1].reshape(seq_len, heads_here, HEAD), cosine, sine, 1.0).astype(
        jnp.bfloat16
    )
    values = proj[:, 2].reshape(seq_len, heads_here, HEAD).astype(jnp.bfloat16)
    block_rows = min(512, seq_len)
    block_count = seq_len // block_rows
    places = jnp.arange(seq_len)
    query_blocks = query.reshape(block_count, block_rows, heads_here, HEAD)
    segment_blocks = segment_ids.reshape(block_count, block_rows)
    place_blocks = places.reshape(block_count, block_rows)

    def masked_scores(query_part, segment_part, place_part):
        scores = (
            jnp.einsum("qhe,khe->hqk", query_part, keys, preferred_element_type=jnp.float32)
            * score_scale
        )
        allowed = (segment_part[:, None] == segment_ids[None, :]) & (
            place_part[:, None] >= places[None, :]
        )
        return jnp.where(allowed[None], scores, NEGATIVE)

    def forward_block(block_item):
        query_part, segment_part, place_part = block_item
        scores = masked_scores(query_part, segment_part, place_part)
        row_max = jnp.max(scores, axis=-1, keepdims=True)
        exponent = jnp.exp(scores - row_max)
        row_total = jnp.sum(exponent, axis=-1, keepdims=True)
        probability = (exponent / row_total).astype(jnp.bfloat16)
        context_part = jnp.einsum(
            "hqk,khe->qhe", probability, values, preferred_element_type=jnp.float32
        )
        return (context_part, (row_max + jnp.log(row_total))[..., 0])

    context_blocks, log_totals = lax.map(
        forward_block, (query_blocks, segment_blocks, place_blocks)
    )
    context = context_blocks.reshape(seq_len, local_width).astype(jnp.bfloat16)
    up_in = jnp.dot(mlp_rows, w_up, preferred_element_type=jnp.float32) + b_up.astype(jnp.float32)
    activated = gelu_exact(up_in).astype(jnp.bfloat16)
    context_part = context
    branch_sum = lax.psum_scatter(
        jnp.dot(context_part, w_out, preferred_element_type=jnp.float32)
        + jnp.dot(activated, w_down, preferred_element_type=jnp.float32),
        "tensor",
        scatter_dimension=0,
        tiled=True,
    )
    output = (resid + branch_sum + bias_sum).astype(jnp.bfloat16)
    grad_all = lax.all_gather(cotangent, "tensor", axis=0, tiled=True)
    d_active = jnp.einsum("sd,fd->sf", grad_all, w_down, preferred_element_type=jnp.float32)
    gelu_value, gelu_back = jax.vjp(gelu_exact, up_in)
    d_up = gelu_back(d_active)[0].astype(jnp.bfloat16)
    d_w_down = jnp.einsum("sf,sd->fd", activated, grad_all, preferred_element_type=jnp.float32)
    d_w_up = jnp.einsum("sd,sf->df", mlp_rows, d_up, preferred_element_type=jnp.float32)
    d_b_up = jnp.sum(d_up, axis=0, dtype=jnp.float32).reshape(1, -1)
    unit_sums = (d_w_up, d_b_up, d_w_down)
    d_context = jnp.einsum("sd,cd->sc", grad_all, w_out, preferred_element_type=jnp.float32).astype(
        jnp.bfloat16
    )
    d_w_out = jnp.einsum("sc,sd->cd", context, grad_all, preferred_element_type=jnp.float32)
    d_context_blocks = d_context.reshape(block_count, block_rows, heads_here, HEAD)

    def backward_block(carry, block_item):
        d_keys, d_values = carry
        query_part, d_context_part, segment_part, place_part, log_part = block_item
        scores = masked_scores(query_part, segment_part, place_part)
        probability = jnp.exp(scores - log_part[..., None])
        d_prob = jnp.einsum(
            "qhe,khe->hqk", d_context_part, values, preferred_element_type=jnp.float32
        )
        row_delta = jnp.sum(probability * d_prob, axis=-1, keepdims=True)
        d_scores = (probability * (d_prob - row_delta)).astype(jnp.bfloat16)
        d_query_part = (
            jnp.einsum("hqk,khe->qhe", d_scores, keys, preferred_element_type=jnp.float32)
            * score_scale
        )
        d_keys = (
            d_keys
            + jnp.einsum("hqk,qhe->khe", d_scores, query_part, preferred_element_type=jnp.float32)
            * score_scale
        )
        d_values = d_values + jnp.einsum(
            "hqk,qhe->khe",
            probability.astype(jnp.bfloat16),
            d_context_part,
            preferred_element_type=jnp.float32,
        )
        return ((d_keys, d_values), d_query_part)

    zero_rows = jnp.zeros((seq_len, heads_here, HEAD), jnp.float32)
    (d_keys, d_values), d_query_blocks = lax.scan(
        backward_block,
        (zero_rows, zero_rows),
        (query_blocks, d_context_blocks, segment_blocks, place_blocks, log_totals),
    )
    d_query = d_query_blocks.reshape(seq_len, heads_here, HEAD)
    d_proj = jnp.stack(
        [
            rotated(d_query, cosine, sine, -1.0).reshape(seq_len, local_width),
            rotated(d_keys, cosine, sine, -1.0).reshape(seq_len, local_width),
            d_values.reshape(seq_len, local_width),
        ],
        axis=1,
    ).astype(jnp.bfloat16)
    d_w_qkv = jnp.einsum("sd,sje->dje", attn_rows, d_proj, preferred_element_type=jnp.float32)
    d_b_qkv = jnp.sum(d_proj, axis=0, dtype=jnp.float32).reshape(3, 1, local_width)
    grad_rows = cotangent.astype(jnp.float32)
    attn_term = jnp.einsum("sje,dje->sd", d_proj, w_qkv, preferred_element_type=jnp.float32)
    mlp_term = jnp.einsum("sf,df->sd", d_up, w_up, preferred_element_type=jnp.float32)
    stacked = lax.psum_scatter(
        jnp.stack([attn_term, mlp_term], axis=1), "tensor", scatter_dimension=0, tiled=True
    )
    d_attn_norm = stacked[:, 0]
    d_mlp_norm = stacked[:, 1]
    d_hat = d_attn_norm * gain_attn + d_mlp_norm * gain_mlp
    norm_sums = (
        jnp.sum(d_attn_norm * normalized, axis=0),
        jnp.sum(d_attn_norm, axis=0),
        jnp.sum(d_mlp_norm * normalized, axis=0),
        jnp.sum(d_mlp_norm, axis=0),
    )
    input_grad = grad_rows + inv_std * (
        d_hat
        - jnp.mean(d_hat, axis=-1, keepdims=True)
        - normalized * jnp.mean(d_hat * normalized, axis=-1, keepdims=True)
    )
    small_sums = (
        lax.psum_scatter(norm_sums[0], ("dp", "tensor"), scatter_dimension=0, tiled=True),
        lax.psum_scatter(norm_sums[1], ("dp", "tensor"), scatter_dimension=0, tiled=True),
        lax.psum_scatter(norm_sums[2], ("dp", "tensor"), scatter_dimension=0, tiled=True),
        lax.psum_scatter(norm_sums[3], ("dp", "tensor"), scatter_dimension=0, tiled=True),
        lax.psum_scatter(
            jnp.sum(grad_rows, axis=0), ("dp", "tensor"), scatter_dimension=0, tiled=True
        ),
    )
    summed = (
        lax.psum_scatter(d_w_qkv, "dp", scatter_dimension=0, tiled=True),
        lax.psum_scatter(d_b_qkv, "dp", scatter_dimension=2, tiled=True),
        lax.psum_scatter(d_w_out, "dp", scatter_dimension=1, tiled=True),
        lax.psum_scatter(unit_sums[0], "dp", scatter_dimension=0, tiled=True),
        lax.psum_scatter(unit_sums[1], "dp", scatter_dimension=1, tiled=True),
        lax.psum_scatter(unit_sums[2], "dp", scatter_dimension=1, tiled=True),
    )
    return (
        output,
        input_grad,
        small_sums[0],
        small_sums[1],
        small_sums[2],
        small_sums[3],
        summed[0],
        summed[1],
        summed[2],
        small_sums[4],
        summed[3],
        summed[4],
        summed[5],
        small_sums[4],
    )


def fits(n_dp, n_t, seq, rows, d, width, units):
    if n_dp != 16 or n_t < 2 or width != 512 or units != 2048 or width % 128 or units % width or rows % 128 or seq != rows * n_t:
        return False
    small = (d // (n_dp * n_t), width // n_dp, units // n_dp)
    if any(n < 1 or n > 128 or n & (n - 1) for n in small) or (d // n_dp) % 16:
        return False
    rows_of = 2 * (4 * seq * d + seq * (max(4, units // width) * width + 4 * width + units)) + 4 * seq * d
    chunks = 4 + 2 * (units // width)
    weights_of = 2 * chunks * d * width
    reduction = 2 * d * width * (2 + 2) + weights_of * 7 // 16 + 4 * chunks * (d // n_dp) * width
    exchange = 8 * (n_t - 1) * rows * d
    return rows_of + weights_of + reduction + exchange <= 54 << 20


def local(n_dp, n_t, *args):
    rows, d = args[0].shape
    seq, width, units = args[1].shape[0], args[6].shape[2], args[10].shape[1]
    if fits(n_dp, n_t, seq, rows, d, width, units):
        return fused(Sizes(n_dp, n_t, seq, rows, d, width, units), args)
    return plain(*args)


def solution(mesh):
    return jax.shard_map(
        functools.partial(local, mesh.shape["dp"], mesh.shape["tensor"]),
        mesh=mesh,
        in_specs=(
            P(("dp", "tensor"), None),
            P("dp"),
            P(("dp", "tensor")),
            P(("dp", "tensor")),
            P(("dp", "tensor")),
            P(("dp", "tensor")),
            P("dp", None, "tensor"),
            P(None, "tensor", "dp"),
            P("tensor", "dp"),
            P(("dp", "tensor")),
            P("dp", "tensor"),
            P("tensor", "dp"),
            P("tensor", "dp"),
            P(("dp", "tensor")),
            P(("dp", "tensor"), None),
        ),
        out_specs=(
            P(("dp", "tensor"), None),
            P(("dp", "tensor"), None),
            P(("dp", "tensor")),
            P(("dp", "tensor")),
            P(("dp", "tensor")),
            P(("dp", "tensor")),
            P("dp", None, "tensor"),
            P(None, "tensor", "dp"),
            P("tensor", "dp"),
            P(("dp", "tensor")),
            P("dp", "tensor"),
            P("tensor", "dp"),
            P("tensor", "dp"),
            P(("dp", "tensor")),
        ),
        check_vma=False,
    )
```
